256 devices in a mesh: gz: 32 (over x, y, core), gy: 8 (over z).
Axes of the slice: x: 4, y: 4, z: 8, core: 2. Of those that a mesh axis runs over, the one named last changes fastest.
Arguments:
- volume: bfloat16 [4, 128, 128, 256], P(None, 'gz', 'gy'), may hold values from -6 to 6
- first_weight: bfloat16 [3, 3, 3, 4, 32], replicated, may hold values from -0.625 to 0.625
- first_bias: float32 [32], replicated, may hold values from -0.5 to 0.5
- second_weight: bfloat16 [3, 3, 3, 32, 64], replicated, may hold values from -0.21875 to 0.21875
- second_bias: float32 [64], replicated, may hold values from -0.5 to 0.5
- upstream: bfloat16 [64, 32, 2048], P('gz', None, 'gy'), may hold values from -0.079589844 to 0.079589844
Outputs:
- pooled: bfloat16 [64, 32, 2048], P('gz', None, 'gy')
- first_grad: float32 [3, 3, 3, 4, 32], replicated
- second_grad: float32 [3, 3, 3, 32, 64], replicated
The draws below stay inside these ranges and needn't reach their ends.
All inputs are finite; a program needn't handle non-finite values.
Results may differ from the reference program's by a relative error of at most 0.0085.
The reference program's roundings to bfloat16 on the way count: a program that leaves them out, or rounds other values in their place, can miss the bound.
Values may be sent and summed in bfloat16 or wider, within the bound.
A program may use at most 128 MiB of HBM per device.

```python
import math
import jax
import jax.numpy as jnp
from jax import lax

CIN = 4
C1 = 32
C2 = 64
NX = 256
NZ = 128
NY = 128


def shard_levels(rng, shape, pieces, low, top_value):
    factor_of, own = 1.0, jax.random.fold_in(rng, 6)
    for dim, blocks in pieces:
        steps = jnp.exp(jax.random.uniform(jax.random.fold_in(own, dim), (blocks,), jnp.float32, low / len(pieces), top_value / len(pieces)))
        factor_of = factor_of * jnp.repeat(steps, shape[dim] // blocks).reshape([-1 if axis == dim else 1 for axis in range(len(shape))])
    return factor_of


def scatter_about(key, dims, scale, bound, shards=(), held_as=jnp.bfloat16):
    array = jax.random.normal(key, dims, jnp.float32) * scale
    if len(shards) > 0:
        array = shard_levels(key, dims, shards, -0.22, 0.18) * array
    return jnp.clip(array, min=-bound, max=bound).astype(held_as)


def setup_inputs(seed: int = 0) -> dict:
    streams_of = jax.random.split(jax.random.key(seed), 7)
    volume = scatter_about(streams_of[0], (CIN, NZ, NY, NX), 1.0, 6.0, ((1, 32), (2, 8)))
    first_weight = scatter_about(streams_of[1], (3, 3, 3, CIN, C1), (27 * CIN) ** -0.5, 0.625)
    first_bias = jnp.clip(jax.random.uniform(streams_of[2], (C1,), jnp.float32, -0.5, 0.5), -0.5, 0.5)
    second_weight = scatter_about(streams_of[3], (3, 3, 3, C1, C2), (27 * C1) ** -0.5, 0.21875)
    second_bias = jnp.clip(jax.random.uniform(streams_of[4], (C2,), jnp.float32, -0.5, 0.5), -0.5, 0.5)
    upstream = scatter_about(streams_of[5], (C2, NZ // 4, (NY // 4) * (NX // 4)), 0.01, 0.079589844, ((0, 32), (2, 8)))
    return dict(volume=volume, first_weight=first_weight, first_bias=first_bias, second_weight=second_weight, second_bias=second_bias, upstream=upstream)


leak = 0.3

def leaky(value):
    return jnp.where(value > 0, value, leak * value)

def slope(value):
    return jnp.where(value > 0, 1.0, leak)

def pool(field):
    chans, depth, rows, width = field.shape
    return field.reshape(chans, depth // 2, 2, rows // 2, 2, width // 2, 2).mean(axis=(2, 4, 6))

def unpool(field):
    chans, depth, rows, width = field.shape
    spread = jnp.broadcast_to(field[:, :, None, :, None, :, None], (chans, depth, 2, rows, 2, width, 2))
    return spread.reshape(chans, depth * 2, rows * 2, width * 2) * 0.125

def convolve(field, kernel):
    return lax.conv_general_dilated(field[None], kernel, (1, 1, 1), 'VALID', dimension_numbers=('NCDHW', 'DHWIO', 'NCDHW'), precision=lax.Precision.HIGHEST)[0]

def reference(volume, first_weight, first_bias, second_weight, second_bias, upstream):
    w_one = first_weight.astype(jnp.float32)
    w_two = second_weight.astype(jnp.float32)
    padded = jnp.pad(volume.astype(jnp.float32), ((0, 0), (1, 1), (1, 1), (1, 1)))
    block = math.gcd(NZ, 16)
    count = NZ // block

    def slab_of(index):
        return lax.dynamic_slice_in_dim(padded, (index * block).astype(jnp.int32), block + 2, 1)

    def layer_one(slab):
        return convolve(slab, w_one) + first_bias[:, None, None, None]

    def forward_block(index):
        return pool(leaky(layer_one(slab_of(index)))).astype(jnp.bfloat16)
    blocks = lax.map(forward_block, jnp.arange(count, dtype=jnp.int32))
    act_one = jnp.transpose(blocks, (1, 0, 2, 3, 4)).reshape(C1, NZ // 2, NY // 2, NX // 2)
    act_one = lax.optimization_barrier(act_one)

    def layer_two(act, kernel):
        return convolve(jnp.pad(act, ((0, 0), (1, 1), (1, 1), (1, 1))), kernel)
    pre_two, pullback = jax.vjp(layer_two, act_one.astype(jnp.float32), w_two)
    pre_two = pre_two + second_bias[:, None, None, None]
    act_two = pool(leaky(pre_two)).astype(jnp.bfloat16)
    pooled = act_two.reshape(C2, NZ // 4, NY // 4 * (NX // 4))
    back = upstream.astype(jnp.float32).reshape(C2, NZ // 4, NY // 4, NX // 4)
    grad_two = lax.optimization_barrier((unpool(back) * slope(pre_two)).astype(jnp.bfloat16))
    grad_act, second_grad = pullback(grad_two.astype(jnp.float32))

    def backward_block(total, index):
        slab = slab_of(index)
        pre = layer_one(slab)
        part = lax.dynamic_slice_in_dim(grad_act, (index * (block // 2)).astype(jnp.int32), block // 2, 1)
        grad_pre = lax.optimization_barrier((unpool(part) * slope(pre)).astype(jnp.bfloat16))
        _, pull = jax.vjp(lambda kernel: convolve(slab, kernel), w_one)
        return (total + pull(grad_pre.astype(jnp.float32))[0], None)
    first_grad, _ = lax.scan(backward_block, jnp.zeros(first_weight.shape, jnp.float32), jnp.arange(count, dtype=jnp.int32))
    return (pooled, first_grad, second_grad)
```

```python
import functools

import jax
import jax.numpy as jnp
import numpy as np
from jax import lax
from jax.experimental import pallas as pl
from jax.experimental.pallas import tpu as pltpu
from jax.sharding import PartitionSpec as P

LEAK = 0.3
F32 = jnp.float32
BF16 = jnp.bfloat16
MESH = pl.DeviceIdType.MESH
VMEM = pl.BlockSpec(memory_space=pltpu.VMEM)
GZ, GY = 32, 8
LIMIT = 56 * 2**20


def lanes_of(shape):
    return lax.broadcasted_iota(jnp.int32, shape, len(shape) - 1)


def before(x):
    lane = lanes_of(x.shape)
    return jnp.where(lane >= 64, pltpu.roll(x, 64, 1), jnp.where(lane == 0, 0.0, pltpu.roll(x, 65, 1)))


def after(x):
    lane = lanes_of(x.shape)
    return jnp.where(lane < 64, pltpu.roll(x, 64, 1), jnp.where(lane == 127, 0.0, pltpu.roll(x, 63, 1)))


def mm(a, b):
    return jnp.dot(a, b, preferred_element_type=F32)


def mm_nt(a, b):
    return lax.dot_general(a, b, (((1,), (1,)), ((), ())), preferred_element_type=F32)


def place():
    return lax.axis_index("gz"), lax.axis_index("gy")


def spread_matrix():
    out = np.zeros((256, 4, 128), np.float32)
    for lane in range(128):
        cell = 2 * (lane % 64) + lane // 64
        for dw in range(4):
            w = 2 * cell + dw - 1
            if 0 <= w < 256:
                out[w, dw, lane] = 1
    return out.reshape(256, 512).astype(jnp.bfloat16)


def channel_matrix():
    out = np.zeros((64, 64), np.float32)
    for q in range(64):
        out[q, (q % 2) * 32 + q // 2] = 1
    return out.astype(jnp.bfloat16)


def gather_matrix():
    out = np.zeros((2, 2, 2, 4, 4, 4, 4, 128), np.float32)
    for pd in range(2):
        for pr in range(2):
            for pw in range(2):
                for r in range(3):
                    for s in range(3):
                        for t in range(3):
                            for c in range(4):
                                out[pd, pr, pw, pd + r, pw + t, pr + s, c, ((r * 3 + s) * 3 + t) * 4 + c] = 1
    return out.reshape(2048, 128).astype(jnp.bfloat16)


def partners(gz, gy, dz, dy):
    return lax.rem(gz + dz + GZ, GZ), lax.rem(gy + dy + GY, GY)


def exchange_in(vol_ref, up_ref, ext_ref, back_ref, land, stage, got, send, recv, a_send, a_recv):
    gz, gy = place()
    for half in range(2):
        for chan in range(2):
            stage[pl.ds(chan * 2 + half, GZ, stride=8), :] = up_ref[chan, :, half * 128 : half * 128 + 128].astype(F32)
    copies = []
    number = 0
    for dz in (-1, 0, 1):
        src_d, dst_d = {-1: (slice(0, 3), slice(7, 10)), 0: (slice(0, 4), slice(3, 7)), 1: (slice(1, 4), slice(0, 3))}[dz]
        for dy in (-1, 0, 1):
            if dz == 0 and dy == 0:
                continue
            src_r, dst_r = {
                -1: (slice(0, 16), slice(80, 96)),
                0: (slice(0, 64), slice(16, 80)),
                1: (slice(48, 64), slice(0, 16)),
            }[dy]
            copy = pltpu.make_async_remote_copy(
                src_ref=vol_ref.at[src_d, src_r],
                dst_ref=land.at[dst_d, dst_r],
                send_sem=send.at[number],
                recv_sem=recv.at[number],
                device_id=partners(gz, gy, dz, dy),
                device_id_type=MESH,
            )
            copy.start()
            copies.append(copy)
            number += 1

    def scatter(k, _):
        to = lax.rem(gz + k, GZ)
        pltpu.make_async_remote_copy(
            src_ref=stage.at[pl.ds(pl.multiple_of(to * 8, 8), 8)],
            dst_ref=got.at[pl.ds(pl.multiple_of(gz * 8, 8), 8)],
            send_sem=a_send,
            recv_sem=a_recv,
            device_id=(to, gy),
            device_id_type=MESH,
        ).start()
        return 0

    lax.fori_loop(1, GZ, scatter, 0)
    land[3:7, 16:80] = vol_ref[...]
    mine = pl.ds(pl.multiple_of(gz * 8, 8), 8)
    for copy in copies:
        copy.wait()
    whole = pltpu.make_async_remote_copy(
        src_ref=stage.at[pl.ds(0, 8 * GZ - 8)],
        dst_ref=got.at[pl.ds(0, 8 * GZ - 8)],
        send_sem=a_send,
        recv_sem=a_recv,
        device_id=(lax.rem(gz + 1, GZ), gy),
        device_id_type=MESH,
    )
    whole.wait()
    got[mine, :] = stage[mine, :]
    row = lax.broadcasted_iota(jnp.int32, (10, 96, 256), 1)
    dep = lax.broadcasted_iota(jnp.int32, (10, 96, 256), 0)
    low_d = jnp.where(gz == 0, 3, 0)
    high_d = jnp.where(gz == GZ - 1, 7, 10)
    low_r = jnp.where(gy == 0, 16, 0)
    high_r = jnp.where(gy == GY - 1, 80, 96)
    inside = (dep >= low_d) & (dep < high_d) & (row >= low_r) & (row < high_r)
    ext_ref[...] = jnp.where(inside, land[...].astype(F32), 0.0).astype(BF16)
    for half in range(2):
        for chan in range(2):
            back_ref[chan * 32 : chan * 32 + 32, half * 128 : half * 128 + 128] = got[
                pl.ds(chan * 2 + half, GZ, stride=8), :
            ].astype(BF16)


def forward(
    ext_ref, back_ref, w1_ref, b1_ref, w2_ref, b2_ref, spread_ref, chan_ref,
    patch_ref, pre_ref, grad_ref, pool_ref, sg_ref, rows, act, full,
):
    gz, gy = place()
    for d in range(10):
        wide = mm(ext_ref[d], spread_ref[...])
        for dw in range(4):
            rows[d, dw] = wide[:, dw * 128 : dw * 128 + 128]

    def window(d, _):
        for dd in range(4):
            for dw in range(4):
                for r in range(10):
                    patch_ref[d, dd * 64 + dw * 16 : dd * 64 + dw * 16 + 16, r * 128 : r * 128 + 128] = rows[
                        2 * d + dd, dw, 8 * r + 4 : 8 * r + 20, :
                    ].astype(BF16)
        return 0

    lax.fori_loop(0, 4, window, 0)

    def layer_one(d, _):
        d_in = jnp.where(d == 0, gz > 0, jnp.where(d == 3, gz < GZ - 1, True))
        for j in range(5):
            pre = mm(w1_ref[...], patch_ref[d, :, j * 256 : j * 256 + 256]) + b1_ref[...]
            pre_ref[d, :, j * 256 : j * 256 + 256] = pre.astype(BF16)
            out = jnp.maximum(pre, LEAK * pre)
            cell = out[0:32]
            for g in range(1, 8):
                cell = cell + out[g * 32 : g * 32 + 32]
            cell = (cell * 0.125).astype(BF16).astype(F32)
            for k in range(2):
                r = 2 * j + k
                ok = d_in
                if r == 0:
                    ok = ok & (gy > 0)
                if r == 9:
                    ok = ok & (gy < GY - 1)
                one = jnp.where(ok, cell[:, k * 128 : k * 128 + 128], 0.0)
                act[d, 0, r * 32 : r * 32 + 32, :] = before(one).astype(BF16)
                act[d, 1, r * 32 : r * 32 + 32, :] = one.astype(BF16)
                act[d, 2, r * 32 : r * 32 + 32, :] = after(one).astype(BF16)
        return 0

    lax.fori_loop(0, 4, layer_one, 0)
    back = mm(chan_ref[...], back_ref[...])
    lane = lanes_of((64, 128))
    for h in range(2):
        sides = []
        for k in range(2):
            r = 4 * h + 2 * k
            sides.append(
                jnp.concatenate([act[dd, dw, r * 32 : r * 32 + 128, :] for dd in range(4) for dw in range(3)], axis=0)
            )
        patches = jnp.concatenate(sides, axis=1)
        pre = mm(w2_ref[...], patches) + b2_ref[...]
        out = jnp.maximum(pre, LEAK * pre)
        cell = out[0:64] + out[64:128] + out[128:192] + out[192:256]
        left, right = cell[:, :128], cell[:, 128:]
        left = left + pltpu.roll(left, 64, 1)
        right = right + pltpu.roll(right, 64, 1)
        pooled = (jnp.where(lane < 64, left, right) * 0.125).astype(BF16)
        pool_ref[:, h * 128 : h * 128 + 128] = pooled
        up = back[:, h * 128 : h * 128 + 128] * 0.125
        other = pltpu.roll(up, 64, 1)
        both = jnp.concatenate([jnp.where(lane < 64, up, other), jnp.where(lane < 64, other, up)], axis=1)
        weak = both * LEAK
        parts = []
        for g in range(4):
            part = jnp.where(pre[g * 64 : g * 64 + 64] > 0, both, weak).astype(BF16)
            parts.append(part)
            for k in range(2):
                grad_ref[g // 2, 4 * h + 2 * k + g % 2] = part[:, k * 128 : k * 128 + 128]
        term = mm_nt(patches, jnp.concatenate(parts, axis=0))
        if h == 0:
            full[...] = term
        else:
            full[...] += term
    lane = lanes_of((16, 128))
    for r in range(3):
        for t in range(3):
            near = []
            for dr in range(4):
                a = ((r * 3 + t) * 4 + dr) * 32
                b = (((r + 1) * 3 + t) * 4 + dr) * 32
                near.append(full[a : a + 32, 0:128] + full[b : b + 32, 128:256])
            for s in range(3):
                low = near[s][:16] + pltpu.roll(near[s + 1][:16], 64, 1)
                high = pltpu.roll(near[s][16:], 64, 1) + near[s + 1][16:]
                at = ((r * 3 + s) * 3 + t) * 16
                sg_ref[at : at + 16, :] = jnp.where(lane < 64, low, high)
    sg_ref[432:512, :] = jnp.zeros((80, 128), F32)


def spread16(kind, gz, gy, k):
    if kind == 0:
        return lax.rem(gz + 2 * k, GZ), gy
    own = gy * 2 + lax.rem(gz, 2)
    other = lax.rem(own + k, 16)
    return gz - lax.rem(gz, 2) + lax.rem(other, 2), other // 2


def rank16(kind, gz, gy):
    return gz // 2 if kind == 0 else gy * 2 + lax.rem(gz, 2)


def share(kind, src_of, landing, own_slot, send, recv, one):
    gz, gy = place()

    def go(k, _):
        to = spread16(kind, gz, gy, k)
        pltpu.make_async_remote_copy(
            src_ref=src_of(rank16(kind, *to)),
            dst_ref=landing.at[own_slot],
            send_sem=send,
            recv_sem=recv,
            device_id=to,
            device_id_type=MESH,
        ).start()
        return 0

    lax.fori_loop(1, 16, go, 0)

    def wait():
        pltpu.make_async_remote_copy(
            src_ref=landing.at[pl.ds(0, 15)],
            dst_ref=landing.at[pl.ds(0, 15)],
            send_sem=send,
            recv_sem=recv,
            device_id=spread16(kind, gz, gy, 1),
            device_id_type=MESH,
        ).wait()

    return wait


def total16(landing):
    value = landing[0]
    for k in range(1, 16):
        value = value + landing[k]
    return value


def exchange_out(
    grad_ref, pool_ref, chan_ref, sg_ref, ext_ref, out_ref, total_ref,
    land, stage, got, one, two, part, done, send, recv, a_send, a_recv, s_send, s_recv,
):
    gz, gy = place()
    copies = []
    number = 0
    for dz in (-1, 0, 1):
        src_d, dst_d = {-1: (slice(0, 1), slice(3, 4)), 0: (slice(0, 2), slice(1, 3)), 1: (slice(1, 2), slice(0, 1))}[dz]
        for dy in (-1, 0, 1):
            if dz == 0 and dy == 0:
                continue
            src_r, dst_r = {-1: (slice(0, 1), slice(9, 10)), 0: (slice(0, 8), slice(1, 9)), 1: (slice(7, 8), slice(0, 1))}[dy]
            copy = pltpu.make_async_remote_copy(
                src_ref=grad_ref.at[src_d, src_r],
                dst_ref=land.at[dst_d, dst_r],
                send_sem=send.at[number],
                recv_sem=recv.at[number],
                device_id=partners(gz, gy, dz, dy),
                device_id_type=MESH,
            )
            copy.start()
            copies.append(copy)
            number += 1
    chip = rank16(0, gz, gy)
    line = rank16(1, gz, gy)
    wait_one = share(0, lambda j: sg_ref.at[pl.ds(pl.multiple_of(j * 32, 32), 32)], one, chip, s_send.at[0], s_recv.at[0], None)
    one_own = sg_ref[pl.ds(pl.multiple_of(chip * 32, 32), 32), :]
    pooled = lax.dot_general(chan_ref[...], pool_ref[...], (((0,), (0,)), ((), ())), preferred_element_type=F32)
    for half in range(2):
        for chan in range(2):
            stage[pl.ds(chan * 2 + half, GZ, stride=8), :] = pooled[chan * 32 : chan * 32 + 32, half * 128 : half * 128 + 128]

    def scatter(k, _):
        to = lax.rem(gz + k, GZ)
        pltpu.make_async_remote_copy(
            src_ref=stage.at[pl.ds(pl.multiple_of(to * 8, 8), 8)],
            dst_ref=got.at[pl.ds(pl.multiple_of(gz * 8, 8), 8)],
            send_sem=a_send,
            recv_sem=a_recv,
            device_id=(to, gy),
            device_id_type=MESH,
        ).start()
        return 0

    lax.fori_loop(1, GZ, scatter, 0)
    wait_one()
    one[chip] = one_own
    part[...] = total16(one)
    wait_two = share(1, lambda j: part, two, line, s_send.at[1], s_recv.at[1], None)
    for copy in copies:
        copy.wait()
    land[1:3, 1:9] = grad_ref[...]

    @pl.when(gz == 0)
    def _():
        land[0] = jnp.zeros((10, 64, 128), BF16)

    @pl.when(gz == GZ - 1)
    def _():
        land[3] = jnp.zeros((10, 64, 128), BF16)

    @pl.when(gy == 0)
    def _():
        land[:, 0] = jnp.zeros((4, 64, 128), BF16)

    @pl.when(gy == GY - 1)
    def _():
        land[:, 9] = jnp.zeros((4, 64, 128), BF16)

    ext_ref[...] = land[...]
    wait_two()
    two[line] = part[...]
    done[chip] = total16(two)
    wait_three = share(0, lambda j: done.at[chip], done, chip, s_send.at[2], s_recv.at[2], None)
    mine = pl.ds(pl.multiple_of(gz * 8, 8), 8)
    whole = pltpu.make_async_remote_copy(
        src_ref=stage.at[pl.ds(0, 8 * GZ - 8)],
        dst_ref=got.at[pl.ds(0, 8 * GZ - 8)],
        send_sem=a_send,
        recv_sem=a_recv,
        device_id=(lax.rem(gz + 1, GZ), gy),
        device_id_type=MESH,
    )
    whole.wait()
    got[mine, :] = stage[mine, :]
    for half in range(2):
        for chan in range(2):
            out_ref[chan, :, half * 128 : half * 128 + 128] = got[pl.ds(chan * 2 + half, GZ, stride=8), :].astype(BF16)
    wait_three()
    for j in range(27):
        block = done[j // 2, (j % 2) * 16 : (j % 2) * 16 + 16, :]
        total_ref[j * 32 : j * 32 + 16, :] = block[:, :64]
        total_ref[j * 32 + 16 : j * 32 + 32, :] = block[:, 64:]


def backward(ext_ref, patch_ref, pre_ref, w3_ref, gather_ref, out_ref, first):
    for h in range(2):
        sides = []
        for k in range(2):
            r = 4 * h + 2 * k
            sides.append(
                jnp.concatenate([ext_ref[dd, r : r + 4].reshape(256, 128) for dd in range(4)], axis=0)
            )
        spread = mm(w3_ref[...], jnp.concatenate(sides, axis=1))
        for k in range(2):
            lanes = slice(k * 128, k * 128 + 128)
            grad = after(spread[0:128, lanes]) + spread[128:256, lanes] + before(spread[256:384, lanes])
            grad = grad * 0.125
            for g in range(4):
                pd, r = g // 2, 4 * h + 2 * k + g % 2
                strong = grad[g * 32 : g * 32 + 32]
                weak = strong * LEAK
                for m in range(8):
                    pre = pre_ref[1 + pd, m * 32 : m * 32 + 32, (1 + r) * 128 : (2 + r) * 128].astype(F32)
                    first[m * 32 : m * 32 + 32, (pd * 8 + r) * 128 : (pd * 8 + r + 1) * 128] = jnp.where(
                        pre > 0, strong, weak
                    ).astype(BF16)
    full = mm_nt(first[:, :1024], patch_ref[1, :, 128:1152]) + mm_nt(first[:, 1024:], patch_ref[2, :, 128:1152])
    flat = jnp.concatenate([full[g * 32 : g * 32 + 32] for g in range(8)], axis=1)
    total = jnp.zeros((32, 128), F32)
    for _ in range(3):
        piece = flat.astype(BF16)
        total = total + mm(piece, gather_ref[...])
        flat = flat - piece.astype(F32)
    out_ref[...] = total


def sum_first(term_ref, out_ref, one, two, part, send, recv):
    gz, gy = place()
    chip, line = rank16(0, gz, gy), rank16(1, gz, gy)
    wait_one = share(0, lambda j: term_ref, one, chip, send.at[0], recv.at[0], None)
    wait_one()
    one[chip] = term_ref[...]
    part[...] = total16(one)
    wait_two = share(1, lambda j: part, two, line, send.at[1], recv.at[1], None)
    wait_two()
    two[line] = part[...]
    out_ref[...] = total16(two)


def kernel_call(body, outs, scratch, remote, *operands):
    return pl.pallas_call(
        body,
        out_shape=[jax.ShapeDtypeStruct(shape, dtype) for shape, dtype in outs],
        in_specs=[VMEM] * len(operands),
        out_specs=[VMEM] * len(outs),
        scratch_shapes=scratch,
        compiler_params=pltpu.CompilerParams(vmem_limit_bytes=LIMIT, has_side_effects=remote),
    )(*operands)


def prepare(first_weight, second_weight):
    turned = jnp.transpose(first_weight, (4, 0, 2, 1, 3))
    first = [
        jnp.pad(turned, ((0, 0), (pd, 1 - pd), (pw, 1 - pw), (pr, 1 - pr), (0, 0)))
        for pd in range(2)
        for pr in range(2)
        for pw in range(2)
    ]
    first = jnp.stack(first).reshape(256, 256)
    turned = jnp.transpose(second_weight, (4, 0, 2, 1, 3))
    second = [
        jnp.pad(turned, ((0, 0), (pd, 1 - pd), (0, 0), (pr, 1 - pr), (0, 0))) for pd in range(2) for pr in range(2)
    ]
    second = jnp.stack(second).reshape(256, 1536)
    turned = jnp.transpose(second_weight[::-1, ::-1], (2, 3, 0, 1, 4))
    third = [
        jnp.pad(turned, ((0, 0), (0, 0), (pd, 1 - pd), (pr, 1 - pr), (0, 0))) for pd in range(2) for pr in range(2)
    ]
    third = jnp.stack(third, axis=1).reshape(384, 1024)
    return first, second, third


def on_device(volume, first_weight, first_bias, second_weight, second_bias, upstream):
    dma, sem = pltpu.SemaphoreType.DMA, pltpu.VMEM
    w1, w2, w3 = prepare(first_weight, second_weight)
    b1 = jnp.tile(first_bias, 8)[:, None]
    b2 = jnp.tile(second_bias, 4)[:, None]
    spread = jnp.asarray(spread_matrix())
    chan = jnp.asarray(channel_matrix())
    gather = jnp.asarray(gather_matrix())
    own = jnp.transpose(volume, (1, 2, 0, 3)).reshape(4, 64, 256)
    ext, back = kernel_call(
        exchange_in,
        [((10, 96, 256), BF16), ((64, 256), BF16)],
        [sem((10, 96, 256), BF16), sem((256, 128), F32), sem((256, 128), F32), dma((8,)), dma((8,)), dma, dma],
        True, own, upstream,
    )
    patch, pre, grad, pool, sg = kernel_call(
        forward,
        [((4, 256, 1280), BF16), ((4, 256, 1280), BF16), ((2, 8, 64, 128), BF16), ((64, 256), BF16), ((512, 128), F32)],
        [sem((10, 4, 96, 128), F32), sem((4, 3, 320, 128), BF16), sem((1536, 256), F32)],
        False, ext, back, w1, b1, w2, b2, spread, chan,
    )
    grads, pooled, second = kernel_call(
        exchange_out,
        [((4, 10, 64, 128), BF16), ((2, 32, 256), BF16), ((864, 64), F32)],
        [
            sem((4, 10, 64, 128), BF16), sem((256, 128), F32), sem((256, 128), F32), sem((16, 32, 128), F32),
            sem((16, 32, 128), F32), sem((32, 128), F32), sem((16, 32, 128), F32),
            dma((8,)), dma((8,)), dma, dma, dma((3,)), dma((3,)),
        ],
        True, grad, pool, chan, sg,
    )
    (term,) = kernel_call(backward, [((32, 128), F32)], [sem((256, 2048), BF16)], False, grads, patch, pre, w3, gather)
    (first,) = kernel_call(
        sum_first,
        [((32, 128), F32)],
        [sem((16, 32, 128), F32), sem((16, 32, 128), F32), sem((32, 128), F32), dma((2,)), dma((2,))],
        True, term,
    )
    first = jnp.transpose(first[:, :108]).reshape(3, 3, 3, 4, 32)
    return pooled, first, second.reshape(3, 3, 3, 32, 64)


def solution(mesh):
    placed = (P(None, "gz", "gy", None), P(), P(), P(), P(), P("gz", None, "gy"))
    return jax.shard_map(
        on_device,
        mesh=mesh,
        in_specs=placed,
        out_specs=(P("gz", None, "gy"), P(), P()),
        check_vma=False,
    )
```

```python
import jax
import jax.numpy as jnp
import numpy as np
from jax import lax
from jax.experimental import pallas as pl
from jax.experimental.pallas import tpu as pltpu
from jax.sharding import PartitionSpec as P

LEAK = 0.3
F32 = jnp.float32
BF16 = jnp.bfloat16
MESH = pl.DeviceIdType.MESH
VMEM = pl.BlockSpec(memory_space=pltpu.VMEM)
GZ, GY = 32, 8
LIMIT = 56 * 2**20


def lanes_of(shape):
    return lax.broadcasted_iota(jnp.int32, shape, len(shape) - 1)


def before(x):
    lane = lanes_of(x.shape)
    return jnp.where(lane >= 64, pltpu.roll(x, 64, 1), jnp.where(lane == 0, 0.0, pltpu.roll(x, 65, 1)))


def after(x):
    lane = lanes_of(x.shape)
    return jnp.where(lane < 64, pltpu.roll(x, 64, 1), jnp.where(lane == 127, 0.0, pltpu.roll(x, 63, 1)))


def mm(a, b):
    return jnp.dot(a, b, preferred_element_type=F32)


def mm_nt(a, b):
    return lax.dot_general(a, b, (((1,), (1,)), ((), ())), preferred_element_type=F32)


def eye(n):
    return lax.broadcasted_iota(jnp.int32, (n, n), 0) == lax.broadcasted_iota(jnp.int32, (n, n), 1)


def one_hot(n):
    return jnp.where(eye(n), 1.0, 0.0).astype(BF16)


def column(row, times):
    n = row.shape[0]
    wide = jnp.broadcast_to(row[None, :], (n, n))
    once = jnp.sum(jnp.where(eye(n), wide, 0.0), axis=1, keepdims=True)
    return jnp.concatenate([once] * times, axis=0)


def place():
    return lax.axis_index("gz"), lax.axis_index("gy")


def spread_matrix():
    out = np.zeros((256, 4, 128), np.float32)
    for lane in range(128):
        cell = 2 * (lane % 64) + lane // 64
        for dw in range(4):
            w = 2 * cell + dw - 1
            if 0 <= w < 256:
                out[w, dw, lane] = 1
    return out.reshape(256, 512).astype(jnp.bfloat16)


def channel_matrix():
    out = np.zeros((64, 64), np.float32)
    for q in range(64):
        out[q, (q % 2) * 32 + q // 2] = 1
    return out.astype(jnp.bfloat16)


def turn_matrix():
    out = np.zeros((64, 64), np.float32)
    for r in range(16):
        for c in range(4):
            out[r * 4 + c, c * 16 + r] = 1
    return out.astype(jnp.bfloat16)


def gather_matrix():
    out = np.zeros((2, 2, 2, 4, 4, 4, 4, 128), np.float32)
    for pd in range(2):
        for pr in range(2):
            for pw in range(2):
                for r in range(3):
                    for s in range(3):
                        for t in range(3):
                            for c in range(4):
                                out[pd, pr, pw, pd + r, pw + t, pr + s, c, ((r * 3 + s) * 3 + t) * 4 + c] = 1
    return out.reshape(2048, 128).astype(jnp.bfloat16)


def around(dz, dy):
    gz, gy = place()
    return lax.rem(gz + dz + GZ, GZ), lax.rem(gy + dy + GY, GY)


def partner(kind, k):
    gz, gy = place()
    if kind == 0:
        return lax.rem(gz + 2 * k, GZ), gy
    if kind == 2:
        return lax.rem(gz + k, GZ), gy
    other = lax.rem(gy * 2 + lax.rem(gz, 2) + k, 16)
    return gz - lax.rem(gz, 2) + lax.rem(other, 2), other // 2


def rank(kind, gz, gy):
    return (gz // 2, gy * 2 + lax.rem(gz, 2), gz)[kind]


COUNT = (16, 16, 32)


def share(kind, source, landing, send, recv):
    gz, gy = place()
    slot = rank(kind, gz, gy)

    def go(k, _):
        to = partner(kind, k)
        pltpu.make_async_remote_copy(
            src_ref=source(rank(kind, *to)),
            dst_ref=landing.at[slot],
            send_sem=send,
            recv_sem=recv,
            device_id=to,
            device_id_type=MESH,
        ).start()
        return 0

    lax.fori_loop(1, COUNT[kind], go, 0)

    def wait():
        pltpu.make_async_remote_copy(
            src_ref=landing.at[pl.ds(0, COUNT[kind] - 1)],
            dst_ref=landing.at[pl.ds(0, COUNT[kind] - 1)],
            send_sem=send,
            recv_sem=recv,
            device_id=partner(kind, 1),
            device_id_type=MESH,
        ).wait()

    return wait


def greet():
    gz, gy = place()
    barrier = pltpu.get_barrier_semaphore()

    def tell(to):
        pl.semaphore_signal(barrier, inc=1, device_id=to, device_id_type=MESH)

    def along(k, _):
        tell((lax.rem(gz + k, GZ), gy))
        return 0

    def across(k, _):
        row = lax.rem(gy + k, GY)
        tell((gz, row))
        tell((gz + 1 - 2 * lax.rem(gz, 2), row))
        return 0

    far = lax.rem(gz + 2 * lax.rem(gz, 2) - 1 + GZ, GZ)
    tell((far, lax.rem(gy + 1, GY)))
    tell((far, lax.rem(gy + GY - 1, GY)))
    lax.fori_loop(1, GY, across, 0)
    lax.fori_loop(1, GZ, along, 0)

    def wait():
        pl.semaphore_wait(barrier, 47)

    return wait


def total16(landing):
    value = landing[0].astype(F32)
    for k in range(1, 16):
        value = value + landing[k].astype(F32)
    return value


def body(
    vol_ref, w1_ref, b1_ref, w2_ref, b2_ref, up_ref, spread_ref, chan_ref, turn_ref, gather_ref,
    pool_out, first_out, second_out,
    own, ext, up_stage, up_got, pool_stage, pool_got,
    w1_rows, w1, w2, w2_turned, rows, patch, pre, act, full, gact, ffull,
    sg, sg_one, sg_part, sg_two, sg_done, term, t_one, t_part, t_two,
    send, recv, a_send, a_recv, s_send, s_recv,
):
    gz, gy = place()
    greeted = greet()

    for d in range(4):
        flat = jnp.concatenate([vol_ref[c, d] for c in range(4)], axis=0)
        own[d] = mm(turn_ref[...], flat).astype(BF16)
    for half in range(2):
        for chan in range(2):
            up_stage[:, chan * 2 + half, :] = up_ref[chan, :, half * 128 : half * 128 + 128].astype(F32)
    w1_rows[...] = jnp.zeros((128, 32), F32)
    for i in range(27):
        w1_rows[4 * i : 4 * i + 4, :] = w1_ref[i // 9, i // 3 % 3, i % 3].astype(F32)
    flat = mm_nt(one_hot(32), w1_rows[...].astype(BF16)).astype(BF16)
    for g in range(8):
        w1[g * 32 : g * 32 + 32, :] = mm_nt(flat, gather_ref[g * 256 : g * 256 + 256, :]).astype(BF16)
    b1 = column(b1_ref[...], 8)
    b2 = column(b2_ref[...], 4)
    greeted()

    copies = []
    for dz in (-1, 1, 0):
        src_d, dst_d = {-1: (slice(0, 3), slice(7, 10)), 0: (slice(0, 4), slice(3, 7)), 1: (slice(1, 4), slice(0, 3))}[dz]
        for dy in (-1, 1, 0):
            if dz == 0 and dy == 0:
                continue
            src_r, dst_r = {
                -1: (slice(0, 16), slice(80, 96)),
                0: (slice(0, 64), slice(16, 80)),
                1: (slice(48, 64), slice(0, 16)),
            }[dy]
            copy = pltpu.make_async_remote_copy(
                src_ref=own.at[src_d, src_r],
                dst_ref=ext.at[dst_d, dst_r],
                send_sem=send.at[len(copies)],
                recv_sem=recv.at[len(copies)],
                device_id=around(dz, dy),
                device_id_type=MESH,
            )
            copy.start()
            copies.append(copy)
    up_wait = share(2, lambda j: up_stage.at[j], up_got, a_send.at[0], a_recv.at[0])

    lane = lanes_of((32, 128))
    zero = jnp.zeros((32, 128), F32)
    for t in range(3):
        for r in range(4):
            for s in range(4):
                at = ((r * 3 + t) * 4 + s) * 32
                for pd in range(2):
                    near = w2_ref[r - pd, s, t].astype(F32) if 0 <= r - pd < 3 and s < 3 else None
                    next_ = w2_ref[r - pd, s - 1, t].astype(F32) if 0 <= r - pd < 3 and s > 0 else None
                    left = zero[:, :64] if near is None else near
                    right = zero[:, :64] if next_ is None else next_
                    w2[at : at + 32, pd * 128 : pd * 128 + 128] = jnp.concatenate([left, right], axis=1).astype(BF16)
    w2_turned[...] = mm_nt(one_hot(256), w2[...]).astype(BF16)

    ext[3:7, 16:80] = own[...]
    for copy in copies:
        copy.wait()

    @pl.when(gz == 0)
    def _():
        ext[0:3] = jnp.zeros((3, 96, 256), BF16)

    @pl.when(gz == GZ - 1)
    def _():
        ext[7:10] = jnp.zeros((3, 96, 256), BF16)

    @pl.when(gy == 0)
    def _():
        ext[:, 0:16] = jnp.zeros((10, 16, 256), BF16)

    @pl.when(gy == GY - 1)
    def _():
        ext[:, 80:96] = jnp.zeros((10, 16, 256), BF16)

    def widen(d, _):
        wide = mm(ext[d], spread_ref[...])
        for dw in range(4):
            rows[d, dw] = wide[:, dw * 128 : dw * 128 + 128]
        return 0

    lax.fori_loop(0, 10, widen, 0)

    def inside(d, r):
        ok = jnp.where(d == 0, gz > 0, jnp.where(d == 3, gz < GZ - 1, True))
        if r == 0:
            ok = ok & (gy > 0)
        if r == 9:
            ok = ok & (gy < GY - 1)
        return ok

    def layer_one(d, _):
        for dd in range(4):
            for dw in range(4):
                for r in range(10):
                    patch[d, dd * 64 + dw * 16 : dd * 64 + dw * 16 + 16, r * 128 : r * 128 + 128] = rows[
                        2 * d + dd, dw, 8 * r + 4 : 8 * r + 20, :
                    ].astype(BF16)
        for j in range(5):
            value = mm(w1[...], patch[d, :, j * 256 : j * 256 + 256]) + b1
            pre[d, :, j * 256 : j * 256 + 256] = value.astype(BF16)
            out = jnp.maximum(value, LEAK * value)
            cell = out[0:32]
            for g in range(1, 8):
                cell = cell + out[g * 32 : g * 32 + 32]
            cell = (cell * 0.125).astype(BF16).astype(F32)
            for k in range(2):
                r = 2 * j + k
                one = jnp.where(inside(d, r), cell[:, k * 128 : k * 128 + 128], 0.0)
                act[d, 0, r * 32 : r * 32 + 32, :] = before(one).astype(BF16)
                act[d, 1, r * 32 : r * 32 + 32, :] = one.astype(BF16)
                act[d, 2, r * 32 : r * 32 + 32, :] = after(one).astype(BF16)
        return 0

    lax.fori_loop(0, 4, layer_one, 0)

    up_wait()
    up_got[gz] = up_stage[gz]
    lane = lanes_of((64, 128))
    wide = []
    for half in range(2):
        wide.append(jnp.concatenate([up_got[:, chan * 2 + half, :] for chan in range(2)], axis=0))
    back = mm(chan_ref[...], jnp.concatenate(wide, axis=1).astype(BF16))
    pooled = []
    grads = []
    for h in range(2):
        sides = []
        for k in range(2):
            r = 4 * h + 2 * k
            sides.append(
                jnp.concatenate([act[dd, dw, r * 32 : r * 32 + 128, :] for dd in range(4) for dw in range(3)], axis=0)
            )
        patches = jnp.concatenate(sides, axis=1)
        value = mm(w2_turned[...], patches) + b2
        out = jnp.maximum(value, LEAK * value)
        cell = out[0:64] + out[64:128] + out[128:192] + out[192:256]
        left, right = cell[:, :128], cell[:, 128:]
        left = left + pltpu.roll(left, 64, 1)
        right = right + pltpu.roll(right, 64, 1)
        pooled.append((jnp.where(lane < 64, left, right) * 0.125).astype(BF16))
        up = back[:, h * 128 : h * 128 + 128] * 0.125
        other = pltpu.roll(up, 64, 1)
        both = jnp.concatenate([jnp.where(lane < 64, up, other), jnp.where(lane < 64, other, up)], axis=1)
        weak = both * LEAK
        grad = jnp.concatenate(
            [jnp.where(value[g * 64 : g * 64 + 64] > 0, both, weak).astype(BF16) for g in range(4)], axis=0
        )
        grads.append(grad)
        if h == 0:
            full[...] = mm_nt(patches, grad)
        else:
            full[...] += mm_nt(patches, grad)

    lane = lanes_of((16, 128))
    for r in range(3):
        for t in range(3):
            near = []
            for s in range(4):
                a = ((r * 3 + t) * 4 + s) * 32
                b = (((r + 1) * 3 + t) * 4 + s) * 32
                near.append(full[a : a + 32, 0:128] + full[b : b + 32, 128:256])
            for s in range(3):
                low = near[s][:16] + pltpu.roll(near[s + 1][:16], 64, 1)
                high = pltpu.roll(near[s][16:], 64, 1) + near[s + 1][16:]
                at = (r * 3 + s) * 3 + t
                sg[at // 2, (at % 2) * 16 : (at % 2) * 16 + 16, :] = jnp.where(lane < 64, low, high).astype(SENT)
    sg[13, 16:32, :] = jnp.zeros((16, 128), SENT)
    sg[14:16] = jnp.zeros((2, 32, 128), SENT)
    chip, line = rank(0, gz, gy), rank(1, gz, gy)
    one_wait = share(0, lambda j: sg.at[j], sg_one, s_send.at[0], s_recv.at[0])
    sg_one[chip] = sg[chip]

    turned = lax.dot_general(
        chan_ref[...], jnp.concatenate(pooled, axis=1), (((0,), (0,)), ((), ())), preferred_element_type=F32
    )
    for half in range(2):
        for chan in range(2):
            pool_stage[:, chan * 2 + half, :] = turned[chan * 32 : chan * 32 + 32, half * 128 : half * 128 + 128]
    pool_wait = share(2, lambda j: pool_stage.at[j], pool_got, a_send.at[1], a_recv.at[1])
    pool_got[gz] = pool_stage[gz]

    for h in range(2):
        pulled = mm(w2[...], grads[h])
        for dd in range(4):
            for t in range(3):
                at = (dd * 3 + t) * 128
                for k in range(2):
                    gact[dd, t, 2 * h + k] = pulled[at : at + 128, k * 128 : k * 128 + 128]

    def layer_back(d, _):
        for j in range(5):
            sides = []
            for k in range(2):
                parts = []
                for t in range(3):
                    value = None
                    for r, at in ((j, k * 32), (j - 1, 64 + k * 32)):
                        if 0 <= r < 4:
                            piece = gact[d, t, r, at : at + 32, :]
                            value = piece if value is None else value + piece
                    parts.append(value)
                value = (after(parts[0]) + parts[1] + before(parts[2])) * 0.125
                sides.append(jnp.where(inside(d, 2 * j + k), value, 0.0))
            strong = jnp.concatenate(sides, axis=1)
            weak = strong * LEAK
            seen = pre[d, :, j * 256 : j * 256 + 256].astype(F32)
            grad = jnp.concatenate(
                [jnp.where(seen[g * 32 : g * 32 + 32] > 0, strong, weak).astype(BF16) for g in range(8)], axis=0
            )
            ffull[...] += mm_nt(grad, patch[d, :, j * 256 : j * 256 + 256])
        return 0

    ffull[...] = jnp.zeros((256, 256), F32)
    lax.fori_loop(0, 4, layer_back, 0)
    flat = jnp.concatenate([ffull[g * 32 : g * 32 + 32, :] for g in range(8)], axis=1)
    total = jnp.zeros((32, 128), F32)
    for _ in range(3):
        piece = flat.astype(BF16)
        total = total + mm(piece, gather_ref[...])
        flat = flat - piece.astype(F32)
    term[...] = total.astype(SENT)

    t_wait = share(0, lambda j: term, t_one, s_send.at[3], s_recv.at[3])
    t_one[chip] = term[...]
    one_wait()
    sg_part[...] = total16(sg_one).astype(SENT)
    two_wait = share(1, lambda j: sg_part, sg_two, s_send.at[1], s_recv.at[1])
    sg_two[line] = sg_part[...]
    t_wait()
    t_part[...] = total16(t_one).astype(SENT)
    t_wait = share(1, lambda j: t_part, t_two, s_send.at[4], s_recv.at[4])
    t_two[line] = t_part[...]
    two_wait()
    sg_done[chip] = total16(sg_two).astype(SENT)
    done_wait = share(0, lambda j: sg_done.at[chip], sg_done, s_send.at[2], s_recv.at[2])
    pool_wait()
    for half in range(2):
        for chan in range(2):
            pool_out[chan, :, half * 128 : half * 128 + 128] = pool_got[:, chan * 2 + half, :].astype(BF16)
    t_wait()
    turned = jnp.transpose(total16(t_two))
    for i in range(27):
        first_out[i // 9, i // 3 % 3, i % 3] = turned[4 * i : 4 * i + 4, :]
    done_wait()
    for i in range(27):
        block = sg_done[i // 2, (i % 2) * 16 : (i % 2) * 16 + 16, :].astype(F32)
        second_out[i // 9, i // 3 % 3, i % 3, 0:16, :] = block[:, :64]
        second_out[i // 9, i // 3 % 3, i % 3, 16:32, :] = block[:, 64:]


SENT = F32


def on_device(volume, first_weight, first_bias, second_weight, second_bias, upstream):
    dma, mem = pltpu.SemaphoreType.DMA, pltpu.VMEM
    constants = [jnp.asarray(m()) for m in (spread_matrix, channel_matrix, turn_matrix, gather_matrix)]
    operands = [volume, first_weight, first_bias, second_weight, second_bias, upstream, *constants]
    return pl.pallas_call(
        body,
        out_shape=[
            jax.ShapeDtypeStruct((2, 32, 256), BF16),
            jax.ShapeDtypeStruct((3, 3, 3, 4, 32), F32),
            jax.ShapeDtypeStruct((3, 3, 3, 32, 64), F32),
        ],
        in_specs=[VMEM] * len(operands),
        out_specs=[VMEM] * 3,
        scratch_shapes=[
            mem((4, 64, 256), BF16), mem((10, 96, 256), BF16), mem((32, 8, 128), F32), mem((32, 8, 128), F32),
            mem((32, 8, 128), F32), mem((32, 8, 128), F32),
            mem((128, 32), F32), mem((256, 256), BF16), mem((1536, 256), BF16), mem((256, 1536), BF16),
            mem((10, 4, 96, 128), F32), mem((4, 256, 1280), BF16), mem((4, 256, 1280), BF16), mem((4, 3, 320, 128), BF16),
            mem((1536, 256), F32), mem((4, 3, 4, 128, 128), F32), mem((256, 256), F32),
            mem((16, 32, 128), SENT), mem((16, 32, 128), SENT), mem((32, 128), SENT), mem((16, 32, 128), SENT),
            mem((16, 32, 128), SENT), mem((32, 128), SENT), mem((16, 32, 128), SENT), mem((32, 128), SENT),
            mem((16, 32, 128), SENT),
            dma((8,)), dma((8,)), dma((2,)), dma((2,)), dma((5,)), dma((5,)),
        ],
        compiler_params=pltpu.CompilerParams(vmem_limit_bytes=LIMIT, has_side_effects=True, collective_id=1),
    )(*operands)


def solution(mesh):
    placed = (P(None, "gz", "gy", None), P(), P(), P(), P(), P("gz", None, "gy"))
    return jax.shard_map(
        on_device,
        mesh=mesh,
        in_specs=placed,
        out_specs=(P("gz", None, "gy"), P(), P()),
        check_vma=False,
    )
```

```python
import jax
import jax.numpy as jnp
import numpy as np
from jax import lax
from jax.experimental import pallas as pl
from jax.experimental.pallas import tpu as pltpu
from jax.sharding import PartitionSpec as P

LEAK = 0.3
F32 = jnp.float32
BF16 = jnp.bfloat16
MESH = pl.DeviceIdType.MESH
VMEM = pl.BlockSpec(memory_space=pltpu.VMEM)
GZ, GY = 32, 8
LIMIT = 56 * 2**20


def lanes_of(shape):
    return lax.broadcasted_iota(jnp.int32, shape, len(shape) - 1)


def before(x):
    lane = lanes_of(x.shape)
    return jnp.where(lane >= 64, pltpu.roll(x, 64, 1), jnp.where(lane == 0, 0.0, pltpu.roll(x, 65, 1)))


def after(x):
    lane = lanes_of(x.shape)
    return jnp.where(lane < 64, pltpu.roll(x, 64, 1), jnp.where(lane == 127, 0.0, pltpu.roll(x, 63, 1)))


def mm(a, b):
    return jnp.dot(a, b, preferred_element_type=F32)


def mm_nt(a, b):
    return lax.dot_general(a, b, (((1,), (1,)), ((), ())), preferred_element_type=F32)


def eye(n):
    return lax.broadcasted_iota(jnp.int32, (n, n), 0) == lax.broadcasted_iota(jnp.int32, (n, n), 1)


def one_hot(n):
    return jnp.where(eye(n), 1.0, 0.0).astype(BF16)


def column(row, times):
    n = row.shape[0]
    wide = jnp.broadcast_to(row[None, :], (n, n))
    once = jnp.sum(jnp.where(eye(n), wide, 0.0), axis=1, keepdims=True)
    return jnp.concatenate([once] * times, axis=0)


def place():
    return lax.axis_index("gz"), lax.axis_index("gy")


def spread_matrix():
    out = np.zeros((256, 4, 128), np.float32)
    for lane in range(128):
        cell = 2 * (lane % 64) + lane // 64
        for dw in range(4):
            w = 2 * cell + dw - 1
            if 0 <= w < 256:
                out[w, dw, lane] = 1
    return out.reshape(256, 512).astype(jnp.bfloat16)


def channel_matrix():
    out = np.zeros((64, 64), np.float32)
    for q in range(64):
        out[q, (q % 2) * 32 + q // 2] = 1
    return out.astype(jnp.bfloat16)


def turn_matrix():
    out = np.zeros((64, 64), np.float32)
    for r in range(16):
        for c in range(4):
            out[r * 4 + c, c * 16 + r] = 1
    return out.astype(jnp.bfloat16)


def gather_matrix():
    out = np.zeros((2, 2, 2, 4, 4, 4, 4, 128), np.float32)
    for pd in range(2):
        for pr in range(2):
            for pw in range(2):
                for r in range(3):
                    for s in range(3):
                        for t in range(3):
                            for c in range(4):
                                out[pd, pr, pw, pd + r, pw + t, pr + s, c, ((r * 3 + s) * 3 + t) * 4 + c] = 1
    return out.reshape(2048, 128).astype(jnp.bfloat16)


def around(dz, dy):
    gz, gy = place()
    return lax.rem(gz + dz + GZ, GZ), lax.rem(gy + dy + GY, GY)


def spread_order(kind):
    xs, ys, zs, cores = (range(n) for n in ((4, 4, 1, 1), (1, 1, 8, 2), (4, 4, 1, 2))[kind])
    all_ = [(x, y, z, c) for x in xs for y in ys for z in zs for c in cores]
    hops = lambda o: min(o[0], 4 - o[0]) + min(o[1], 4 - o[1]) + min(o[2], 8 - o[2]) + 0.5 * o[3]
    return sorted([o for o in all_ if any(o)], key=lambda o: -hops(o))


def shifted(offset):
    gz, gy = place()
    x, y, core = gz // 8, lax.rem(gz // 2, 4), lax.rem(gz, 2)
    dx, dy, dz, dc = offset
    x = lax.rem(x + dx, 4) if dx else x
    y = lax.rem(y + dy, 4) if dy else y
    core = 1 - core if dc else core
    return x * 8 + y * 2 + core, lax.rem(gy + dz, GY) if dz else gy


def rank(kind, gz, gy):
    return (gz // 2, gy * 2 + lax.rem(gz, 2), gz)[kind]


COUNT = (16, 16, 32)


def share(kind, source, landing, send, recv):
    gz, gy = place()
    slot = rank(kind, gz, gy)
    for offset in spread_order(kind):
        to = shifted(offset)
        pltpu.make_async_remote_copy(
            src_ref=source(rank(kind, *to)),
            dst_ref=landing.at[slot],
            send_sem=send,
            recv_sem=recv,
            device_id=to,
            device_id_type=MESH,
        ).start()

    def wait():
        pltpu.make_async_remote_copy(
            src_ref=landing.at[pl.ds(0, COUNT[kind] - 1)],
            dst_ref=landing.at[pl.ds(0, COUNT[kind] - 1)],
            send_sem=send,
            recv_sem=recv,
            device_id=around(1, 0),
            device_id_type=MESH,
        ).wait()

    return wait


def greet():
    gz, gy = place()
    barrier = pltpu.get_barrier_semaphore()

    def tell(to):
        pl.semaphore_signal(barrier, inc=1, device_id=to, device_id_type=MESH)

    far = lax.rem(gz + 2 * lax.rem(gz, 2) - 1 + GZ, GZ)
    for offset in spread_order(1):
        if offset[2]:
            tell(shifted(offset))
    for offset in spread_order(2):
        tell(shifted(offset))
    tell((far, lax.rem(gy + 1, GY)))
    tell((far, lax.rem(gy + GY - 1, GY)))

    def wait():
        pl.semaphore_wait(barrier, 47)

    return wait


def total16(landing):
    value = landing[0].astype(F32)
    for k in range(1, 16):
        value = value + landing[k].astype(F32)
    return value


def body(
    vol_ref, w1_ref, b1_ref, w2_ref, b2_ref, up_ref, spread_ref, chan_ref, turn_ref, gather_ref,
    pool_out, first_out, second_out,
    own, ext, up_stage, up_got, pool_stage, pool_got,
    w1_rows, w1, w2, w2_turned, rows, patch, pre, act, full, gact, ffull,
    sg, sg_one, sg_part, sg_two, sg_done, term, t_one, t_part, t_two,
    send, recv, a_send, a_recv, s_send, s_recv,
):
    gz, gy = place()
    greeted = greet()

    for d in range(4):
        flat = jnp.concatenate([vol_ref[c, d] for c in range(4)], axis=0)
        own[d] = mm(turn_ref[...], flat).astype(BF16)
    for half in range(2):
        for chan in range(2):
            up_stage[:, chan * 2 + half, :] = up_ref[chan, :, half * 128 : half * 128 + 128].astype(F32)
    w1_rows[...] = jnp.zeros((128, 32), F32)
    for i in range(27):
        w1_rows[4 * i : 4 * i + 4, :] = w1_ref[i // 9, i // 3 % 3, i % 3].astype(F32)
    flat = mm_nt(one_hot(32), w1_rows[...].astype(BF16)).astype(BF16)
    for g in range(8):
        w1[g * 32 : g * 32 + 32, :] = mm_nt(flat, gather_ref[g * 256 : g * 256 + 256, :]).astype(BF16)
    b1 = column(b1_ref[...], 8)
    b2 = column(b2_ref[...], 4)
    greeted()

    copies = []
    for dz in (-1, 1, 0):
        src_d, dst_d = {-1: (slice(0, 3), slice(7, 10)), 0: (slice(0, 4), slice(3, 7)), 1: (slice(1, 4), slice(0, 3))}[dz]
        for dy in (-1, 1, 0):
            if dz == 0 and dy == 0:
                continue
            src_r, dst_r = {
                -1: (slice(0, 16), slice(80, 96)),
                0: (slice(0, 64), slice(16, 80)),
                1: (slice(48, 64), slice(0, 16)),
            }[dy]
            copy = pltpu.make_async_remote_copy(
                src_ref=own.at[src_d, src_r],
                dst_ref=ext.at[dst_d, dst_r],
                send_sem=send.at[len(copies)],
                recv_sem=recv.at[len(copies)],
                device_id=around(dz, dy),
                device_id_type=MESH,
            )
            copy.start()
            copies.append(copy)
    up_wait = share(2, lambda j: up_stage.at[j], up_got, a_send.at[0], a_recv.at[0])

    lane = lanes_of((32, 128))
    zero = jnp.zeros((32, 128), F32)
    for t in range(3):
        for r in range(4):
            for s in range(4):
                at = ((r * 3 + t) * 4 + s) * 32
                for pd in range(2):
                    near = w2_ref[r - pd, s, t].astype(F32) if 0 <= r - pd < 3 and s < 3 else None
                    next_ = w2_ref[r - pd, s - 1, t].astype(F32) if 0 <= r - pd < 3 and s > 0 else None
                    left = zero[:, :64] if near is None else near
                    right = zero[:, :64] if next_ is None else next_
                    w2[at : at + 32, pd * 128 : pd * 128 + 128] = jnp.concatenate([left, right], axis=1).astype(BF16)
    w2_turned[...] = mm_nt(one_hot(256), w2[...]).astype(BF16)

    ext[3:7, 16:80] = own[...]
    for copy in copies:
        copy.wait()

    @pl.when(gz == 0)
    def _():
        ext[0:3] = jnp.zeros((3, 96, 256), BF16)

    @pl.when(gz == GZ - 1)
    def _():
        ext[7:10] = jnp.zeros((3, 96, 256), BF16)

    @pl.when(gy == 0)
    def _():
        ext[:, 0:16] = jnp.zeros((10, 16, 256), BF16)

    @pl.when(gy == GY - 1)
    def _():
        ext[:, 80:96] = jnp.zeros((10, 16, 256), BF16)

    def widen(d, _):
        wide = mm(ext[d], spread_ref[...])
        for dw in range(4):
            rows[d, dw] = wide[:, dw * 128 : dw * 128 + 128]
        return 0

    lax.fori_loop(0, 10, widen, 0)

    def inside(d, r):
        ok = jnp.where(d == 0, gz > 0, jnp.where(d == 3, gz < GZ - 1, True))
        if r == 0:
            ok = ok & (gy > 0)
        if r == 9:
            ok = ok & (gy < GY - 1)
        return ok

    def layer_one(d, _):
        for dd in range(4):
            for dw in range(4):
                for r in range(10):
                    patch[d, dd * 64 + dw * 16 : dd * 64 + dw * 16 + 16, r * 128 : r * 128 + 128] = rows[
                        2 * d + dd, dw, 8 * r + 4 : 8 * r + 20, :
                    ].astype(BF16)
        for j in range(5):
            value = mm(w1[...], patch[d, :, j * 256 : j * 256 + 256]) + b1
            pre[d, :, j * 256 : j * 256 + 256] = value.astype(BF16)
            out = jnp.maximum(value, LEAK * value)
            cell = out[0:32]
            for g in range(1, 8):
                cell = cell + out[g * 32 : g * 32 + 32]
            cell = (cell * 0.125).astype(BF16).astype(F32)
            for k in range(2):
                r = 2 * j + k
                one = jnp.where(inside(d, r), cell[:, k * 128 : k * 128 + 128], 0.0)
                act[d, 0, r * 32 : r * 32 + 32, :] = before(one).astype(BF16)
                act[d, 1, r * 32 : r * 32 + 32, :] = one.astype(BF16)
                act[d, 2, r * 32 : r * 32 + 32, :] = after(one).astype(BF16)
        return 0

    lax.fori_loop(0, 4, layer_one, 0)

    up_wait()
    up_got[gz] = up_stage[gz]
    lane = lanes_of((64, 128))
    wide = []
    for half in range(2):
        wide.append(jnp.concatenate([up_got[:, chan * 2 + half, :] for chan in range(2)], axis=0))
    back = mm(chan_ref[...], jnp.concatenate(wide, axis=1).astype(BF16))
    pooled = []
    grads = []
    for h in range(2):
        sides = []
        for k in range(2):
            r = 4 * h + 2 * k
            sides.append(
                jnp.concatenate([act[dd, dw, r * 32 : r * 32 + 128, :] for dd in range(4) for dw in range(3)], axis=0)
            )
        patches = jnp.concatenate(sides, axis=1)
        value = mm(w2_turned[...], patches) + b2
        out = jnp.maximum(value, LEAK * value)
        cell = out[0:64] + out[64:128] + out[128:192] + out[192:256]
        left, right = cell[:, :128], cell[:, 128:]
        left = left + pltpu.roll(left, 64, 1)
        right = right + pltpu.roll(right, 64, 1)
        pooled.append((jnp.where(lane < 64, left, right) * 0.125).astype(BF16))
        up = back[:, h * 128 : h * 128 + 128] * 0.125
        other = pltpu.roll(up, 64, 1)
        both = jnp.concatenate([jnp.where(lane < 64, up, other), jnp.where(lane < 64, other, up)], axis=1)
        weak = both * LEAK
        grad = jnp.concatenate(
            [jnp.where(value[g * 64 : g * 64 + 64] > 0, both, weak).astype(BF16) for g in range(4)], axis=0
        )
        grads.append(grad)
        if h == 0:
            full[...] = mm_nt(patches, grad)
        else:
            full[...] += mm_nt(patches, grad)

    lane = lanes_of((16, 128))
    for r in range(3):
        for t in range(3):
            near = []
            for s in range(4):
                a = ((r * 3 + t) * 4 + s) * 32
                b = (((r + 1) * 3 + t) * 4 + s) * 32
                near.append(full[a : a + 32, 0:128] + full[b : b + 32, 128:256])
            for s in range(3):
                low = near[s][:16] + pltpu.roll(near[s + 1][:16], 64, 1)
                high = pltpu.roll(near[s][16:], 64, 1) + near[s + 1][16:]
                at = (r * 3 + s) * 3 + t
                sg[at // 2, (at % 2) * 16 : (at % 2) * 16 + 16, :] = jnp.where(lane < 64, low, high).astype(SENT)
    sg[13, 16:32, :] = jnp.zeros((16, 128), SENT)
    sg[14:16] = jnp.zeros((2, 32, 128), SENT)
    chip, line = rank(0, gz, gy), rank(1, gz, gy)
    one_wait = share(0, lambda j: sg.at[j], sg_one, s_send.at[0], s_recv.at[0])
    sg_one[chip] = sg[chip]

    turned = lax.dot_general(
        chan_ref[...], jnp.concatenate(pooled, axis=1), (((0,), (0,)), ((), ())), preferred_element_type=F32
    )
    for half in range(2):
        for chan in range(2):
            pool_stage[:, chan * 2 + half, :] = turned[chan * 32 : chan * 32 + 32, half * 128 : half * 128 + 128]
    pool_wait = share(2, lambda j: pool_stage.at[j], pool_got, a_send.at[1], a_recv.at[1])
    pool_got[gz] = pool_stage[gz]

    for h in range(2):
        pulled = mm(w2[...], grads[h])
        for dd in range(4):
            for t in range(3):
                at = (dd * 3 + t) * 128
                for k in range(2):
                    gact[dd, t, 2 * h + k] = pulled[at : at + 128, k * 128 : k * 128 + 128]

    def layer_back(d, _):
        for j in range(5):
            sides = []
            for k in range(2):
                parts = []
                for t in range(3):
                    value = None
                    for r, at in ((j, k * 32), (j - 1, 64 + k * 32)):
                        if 0 <= r < 4:
                            piece = gact[d, t, r, at : at + 32, :]
                            value = piece if value is None else value + piece
                    parts.append(value)
                value = (after(parts[0]) + parts[1] + before(parts[2])) * 0.125
                sides.append(jnp.where(inside(d, 2 * j + k), value, 0.0))
            strong = jnp.concatenate(sides, axis=1)
            weak = strong * LEAK
            seen = pre[d, :, j * 256 : j * 256 + 256].astype(F32)
            grad = jnp.concatenate(
                [jnp.where(seen[g * 32 : g * 32 + 32] > 0, strong, weak).astype(BF16) for g in range(8)], axis=0
            )
            ffull[...] += mm_nt(grad, patch[d, :, j * 256 : j * 256 + 256])
        return 0

    ffull[...] = jnp.zeros((256, 256), F32)
    lax.fori_loop(0, 4, layer_back, 0)
    flat = jnp.concatenate([ffull[g * 32 : g * 32 + 32, :] for g in range(8)], axis=1)
    total = jnp.zeros((32, 128), F32)
    for _ in range(3):
        piece = flat.astype(BF16)
        total = total + mm(piece, gather_ref[...])
        flat = flat - piece.astype(F32)
    term[...] = total.astype(SENT)

    t_wait = share(0, lambda j: term, t_one, s_send.at[3], s_recv.at[3])
    t_one[chip] = term[...]
    one_wait()
    sg_part[...] = total16(sg_one).astype(SENT)
    two_wait = share(1, lambda j: sg_part, sg_two, s_send.at[1], s_recv.at[1])
    sg_two[line] = sg_part[...]
    t_wait()
    t_part[...] = total16(t_one).astype(SENT)
    t_wait = share(1, lambda j: t_part, t_two, s_send.at[4], s_recv.at[4])
    t_two[line] = t_part[...]
    two_wait()
    sg_done[chip] = total16(sg_two).astype(SENT)
    done_wait = share(0, lambda j: sg_done.at[chip], sg_done, s_send.at[2], s_recv.at[2])
    pool_wait()
    for half in range(2):
        for chan in range(2):
            pool_out[chan, :, half * 128 : half * 128 + 128] = pool_got[:, chan * 2 + half, :].astype(BF16)
    t_wait()
    first_out[...] = total16(t_two)
    done_wait()
    second_out[...] = sg_done[...]


def finish(pool_in, first_in, second_in, pool_out, first_out, second_out):
    pool_out[...] = pool_in[...]
    turned = jnp.transpose(first_in[...])
    for i in range(27):
        first_out[i // 9, i // 3 % 3, i % 3] = turned[4 * i : 4 * i + 4, :]
        block = second_in[i // 2, (i % 2) * 16 : (i % 2) * 16 + 16, :].astype(F32)
        second_out[i // 9, i // 3 % 3, i % 3, 0:16, :] = block[:, :64]
        second_out[i // 9, i // 3 % 3, i % 3, 16:32, :] = block[:, 64:]


SENT = BF16


def on_device(volume, first_weight, first_bias, second_weight, second_bias, upstream):
    dma, mem = pltpu.SemaphoreType.DMA, pltpu.VMEM
    constants = [jnp.asarray(m()) for m in (spread_matrix, channel_matrix, turn_matrix, gather_matrix)]
    operands = [volume, first_weight, first_bias, second_weight, second_bias, upstream, *constants]
    results = pl.pallas_call(
        body,
        out_shape=[
            jax.ShapeDtypeStruct((2, 32, 256), BF16),
            jax.ShapeDtypeStruct((32, 128), F32),
            jax.ShapeDtypeStruct((16, 32, 128), SENT),
        ],
        in_specs=[VMEM] * len(operands),
        out_specs=[VMEM] * 3,
        scratch_shapes=[
            mem((4, 64, 256), BF16), mem((10, 96, 256), BF16), mem((32, 4, 128), F32), mem((32, 4, 128), F32),
            mem((32, 4, 128), F32), mem((32, 4, 128), F32),
            mem((128, 32), F32), mem((256, 256), BF16), mem((1536, 256), BF16), mem((256, 1536), BF16),
            mem((10, 4, 96, 128), F32), mem((4, 256, 1280), BF16), mem((4, 256, 1280), BF16), mem((4, 3, 320, 128), BF16),
            mem((1536, 256), F32), mem((4, 3, 4, 128, 128), F32), mem((256, 256), F32),
            mem((16, 32, 128), SENT), mem((16, 32, 128), SENT), mem((32, 128), SENT), mem((16, 32, 128), SENT),
            mem((16, 32, 128), SENT), mem((32, 128), SENT), mem((16, 32, 128), SENT), mem((32, 128), SENT),
            mem((16, 32, 128), SENT),
            dma((8,)), dma((8,)), dma((2,)), dma((2,)), dma((5,)), dma((5,)),
        ],
        compiler_params=pltpu.CompilerParams(vmem_limit_bytes=LIMIT, has_side_effects=True, collective_id=1),
    )(*operands)
    return pl.pallas_call(
        finish,
        out_shape=[
            jax.ShapeDtypeStruct((2, 32, 256), BF16),
            jax.ShapeDtypeStruct((3, 3, 3, 4, 32), F32),
            jax.ShapeDtypeStruct((3, 3, 3, 32, 64), F32),
        ],
        in_specs=[VMEM] * 3,
        out_specs=[VMEM] * 3,
    )(*results)


def solution(mesh):
    placed = (P(None, "gz", "gy", None), P(), P(), P(), P(), P("gz", None, "gy"))
    return jax.shard_map(
        on_device,
        mesh=mesh,
        in_specs=placed,
        out_specs=(P("gz", None, "gy"), P(), P()),
        check_vma=False,
    )
```

```python
import jax
import jax.numpy as jnp
import numpy as np
from jax import lax
from jax.experimental import pallas as pl
from jax.experimental.pallas import tpu as pltpu
from jax.sharding import PartitionSpec as P

LEAK = 0.3
F32 = jnp.float32
BF16 = jnp.bfloat16
MESH = pl.DeviceIdType.MESH
VMEM = pl.BlockSpec(memory_space=pltpu.VMEM)
GZ, GY = 32, 8
LIMIT = 56 * 2**20


def lanes_of(shape):
    return lax.broadcasted_iota(jnp.int32, shape, len(shape) - 1)


def before(x):
    lane = lanes_of(x.shape)
    return jnp.where(lane >= 64, pltpu.roll(x, 64, 1), jnp.where(lane == 0, 0.0, pltpu.roll(x, 65, 1)))


def after(x):
    lane = lanes_of(x.shape)
    return jnp.where(lane < 64, pltpu.roll(x, 64, 1), jnp.where(lane == 127, 0.0, pltpu.roll(x, 63, 1)))


def mm(a, b):
    return jnp.dot(a, b, preferred_element_type=F32)


def mm_nt(a, b):
    return lax.dot_general(a, b, (((1,), (1,)), ((), ())), preferred_element_type=F32)


def eye(n):
    return lax.broadcasted_iota(jnp.int32, (n, n), 0) == lax.broadcasted_iota(jnp.int32, (n, n), 1)


def one_hot(n):
    return jnp.where(eye(n), 1.0, 0.0).astype(BF16)


def column(row, times):
    n = row.shape[0]
    wide = jnp.broadcast_to(row[None, :], (n, n))
    once = jnp.sum(jnp.where(eye(n), wide, 0.0), axis=1, keepdims=True)
    return jnp.concatenate([once] * times, axis=0)


def place():
    return lax.axis_index("gz"), lax.axis_index("gy")


def spread_matrix():
    out = np.zeros((256, 4, 128), np.float32)
    for lane in range(128):
        cell = 2 * (lane % 64) + lane // 64
        for dw in range(4):
            w = 2 * cell + dw - 1
            if 0 <= w < 256:
                out[w, dw, lane] = 1
    return out.reshape(256, 512).astype(jnp.bfloat16)


def channel_matrix():
    out = np.zeros((64, 64), np.float32)
    for q in range(64):
        out[q, (q % 2) * 32 + q // 2] = 1
    return out.astype(jnp.bfloat16)


def turn_matrix():
    out = np.zeros((64, 64), np.float32)
    for r in range(16):
        for c in range(4):
            out[r * 4 + c, c * 16 + r] = 1
    return out.astype(jnp.bfloat16)


def gather_matrix():
    out = np.zeros((2, 2, 2, 4, 4, 4, 4, 128), np.float32)
    for pd in range(2):
        for pr in range(2):
            for pw in range(2):
                for r in range(3):
                    for s in range(3):
                        for t in range(3):
                            for c in range(4):
                                out[pd, pr, pw, pd + r, pw + t, pr + s, c, ((r * 3 + s) * 3 + t) * 4 + c] = 1
    return out.reshape(2048, 128).astype(jnp.bfloat16)


def around(dz, dy):
    gz, gy = place()
    return lax.rem(gz + dz + GZ, GZ), lax.rem(gy + dy + GY, GY)


def spread_order(kind):
    xs, ys, zs, cores = (range(n) for n in ((4, 4, 1, 1), (1, 1, 8, 2), (4, 4, 1, 2))[kind])
    all_ = [(x, y, z, c) for x in xs for y in ys for z in zs for c in cores]
    hops = lambda o: min(o[0], 4 - o[0]) + min(o[1], 4 - o[1]) + min(o[2], 8 - o[2]) + 0.5 * o[3]
    return sorted([o for o in all_ if any(o)], key=lambda o: -hops(o))


def shifted(offset):
    gz, gy = place()
    x, y, core = gz // 8, lax.rem(gz // 2, 4), lax.rem(gz, 2)
    dx, dy, dz, dc = offset
    x = lax.rem(x + dx, 4) if dx else x
    y = lax.rem(y + dy, 4) if dy else y
    core = 1 - core if dc else core
    return x * 8 + y * 2 + core, lax.rem(gy + dz, GY) if dz else gy


def rank(kind, gz, gy):
    return (gz // 2, gy * 2 + lax.rem(gz, 2), gz)[kind]


COUNT = (16, 16, 32)


def share(kind, source, landing, send, recv):
    gz, gy = place()
    slot = rank(kind, gz, gy)
    for offset in spread_order(kind):
        to = shifted(offset)
        pltpu.make_async_remote_copy(
            src_ref=source(rank(kind, *to)),
            dst_ref=landing.at[slot],
            send_sem=send,
            recv_sem=recv,
            device_id=to,
            device_id_type=MESH,
        ).start()

    def wait():
        pltpu.make_async_remote_copy(
            src_ref=landing.at[pl.ds(0, COUNT[kind] - 1)],
            dst_ref=landing.at[pl.ds(0, COUNT[kind] - 1)],
            send_sem=send,
            recv_sem=recv,
            device_id=around(1, 0),
            device_id_type=MESH,
        ).wait()

    return wait


def greet():
    gz, gy = place()
    barrier = pltpu.get_barrier_semaphore()

    def tell(to):
        pl.semaphore_signal(barrier, inc=1, device_id=to, device_id_type=MESH)

    far = lax.rem(gz + 2 * lax.rem(gz, 2) - 1 + GZ, GZ)
    for offset in spread_order(1):
        if offset[2]:
            tell(shifted(offset))
    for offset in spread_order(2):
        tell(shifted(offset))
    tell((far, lax.rem(gy + 1, GY)))
    tell((far, lax.rem(gy + GY - 1, GY)))

    def wait():
        pl.semaphore_wait(barrier, 47)

    return wait


def total16(landing):
    value = landing[0].astype(F32)
    for k in range(1, 16):
        value = value + landing[k].astype(F32)
    return value


def body(
    vol_ref, w1_ref, b1_ref, w2_ref, b2_ref, up_ref, spread_ref, chan_ref, turn_ref, gather_ref,
    pool_out, first_out, second_out,
    own, ext, up_stage, up_got, pool_stage, pool_got,
    w1_rows, w1, w2, w2_turned, rows, patch, pre, act, full, gact, ffull,
    sg, sg_one, sg_part, sg_two, sg_done, term, t_one, t_part, t_two,
    send, recv, a_send, a_recv, s_send, s_recv,
):
    gz, gy = place()
    greeted = greet()

    for d in range(4):
        flat = jnp.concatenate([vol_ref[c, d] for c in range(4)], axis=0)
        own[d] = mm(turn_ref[...], flat).astype(BF16)
    for half in range(2):
        for chan in range(2):
            up_stage[:, chan * 2 + half, :] = up_ref[chan, :, half * 128 : half * 128 + 128].astype(F32)
    w1_rows[...] = jnp.zeros((128, 32), F32)
    for i in range(27):
        w1_rows[4 * i : 4 * i + 4, :] = w1_ref[i // 9, i // 3 % 3, i % 3].astype(F32)
    flat = mm_nt(one_hot(32), w1_rows[...].astype(BF16)).astype(BF16)
    for g in range(8):
        w1[g * 32 : g * 32 + 32, :] = mm_nt(flat, gather_ref[g * 256 : g * 256 + 256, :]).astype(BF16)
    b1 = column(b1_ref[...], 8)
    b2 = column(b2_ref[...], 4)
    greeted()

    copies = []
    for dz in (-1, 1, 0):
        src_d, dst_d = {-1: (slice(0, 3), slice(7, 10)), 0: (slice(0, 4), slice(3, 7)), 1: (slice(1, 4), slice(0, 3))}[dz]
        for dy in (-1, 1, 0):
            if dz == 0 and dy == 0:
                continue
            src_r, dst_r = {
                -1: (slice(0, 16), slice(80, 96)),
                0: (slice(0, 64), slice(16, 80)),
                1: (slice(48, 64), slice(0, 16)),
            }[dy]
            copy = pltpu.make_async_remote_copy(
                src_ref=own.at[src_d, src_r],
                dst_ref=ext.at[dst_d, dst_r],
                send_sem=send.at[len(copies)],
                recv_sem=recv.at[len(copies)],
                device_id=around(dz, dy),
                device_id_type=MESH,
            )
            copy.start()
            copies.append(copy)
    up_wait = share(2, lambda j: up_stage.at[j], up_got, a_send.at[0], a_recv.at[0])

    lane = lanes_of((32, 128))
    zero = jnp.zeros((32, 128), F32)
    for t in range(3):
        for r in range(4):
            for s in range(4):
                at = ((r * 3 + t) * 4 + s) * 32
                for pd in range(2):
                    near = w2_ref[r - pd, s, t].astype(F32) if 0 <= r - pd < 3 and s < 3 else None
                    next_ = w2_ref[r - pd, s - 1, t].astype(F32) if 0 <= r - pd < 3 and s > 0 else None
                    left = zero[:, :64] if near is None else near
                    right = zero[:, :64] if next_ is None else next_
                    w2[at : at + 32, pd * 128 : pd * 128 + 128] = jnp.concatenate([left, right], axis=1).astype(BF16)
    w2_turned[...] = mm_nt(one_hot(256), w2[...]).astype(BF16)

    ext[3:7, 16:80] = own[...]
    for copy in copies:
        copy.wait()

    @pl.when(gz == 0)
    def _():
        ext[0:3] = jnp.zeros((3, 96, 256), BF16)

    @pl.when(gz == GZ - 1)
    def _():
        ext[7:10] = jnp.zeros((3, 96, 256), BF16)

    @pl.when(gy == 0)
    def _():
        ext[:, 0:16] = jnp.zeros((10, 16, 256), BF16)

    @pl.when(gy == GY - 1)
    def _():
        ext[:, 80:96] = jnp.zeros((10, 16, 256), BF16)

    flat = ext[...].reshape(960, 256)
    for side in range(2):
        wide = mm(flat, spread_ref[:, side * 256 : side * 256 + 256])
        for k in range(2):
            rows[:, 2 * side + k] = wide[:, k * 128 : k * 128 + 128].reshape(10, 96, 128)

    def inside(d, r):
        ok = jnp.where(d == 0, gz > 0, jnp.where(d == 3, gz < GZ - 1, True))
        if r == 0:
            ok = ok & (gy > 0)
        if r == 9:
            ok = ok & (gy < GY - 1)
        return ok

    def layer_one(d, _):
        for dd in range(4):
            for dw in range(4):
                for r in range(10):
                    patch[d, dd * 64 + dw * 16 : dd * 64 + dw * 16 + 16, r * 128 : r * 128 + 128] = rows[
                        2 * d + dd, dw, 8 * r + 4 : 8 * r + 20, :
                    ].astype(BF16)
        for j in range(5):
            value = mm(w1[...], patch[d, :, j * 256 : j * 256 + 256]) + b1
            pre[d, :, j * 256 : j * 256 + 256] = value.astype(BF16)
            out = jnp.maximum(value, LEAK * value)
            cell = out[0:32]
            for g in range(1, 8):
                cell = cell + out[g * 32 : g * 32 + 32]
            cell = (cell * 0.125).astype(BF16).astype(F32)
            for k in range(2):
                r = 2 * j + k
                one = jnp.where(inside(d, r), cell[:, k * 128 : k * 128 + 128], 0.0)
                act[d, 0, r * 32 : r * 32 + 32, :] = before(one).astype(BF16)
                act[d, 1, r * 32 : r * 32 + 32, :] = one.astype(BF16)
                act[d, 2, r * 32 : r * 32 + 32, :] = after(one).astype(BF16)
        return 0

    lax.fori_loop(0, 4, layer_one, 0, unroll=True)

    up_wait()
    up_got[gz] = up_stage[gz]
    lane = lanes_of((64, 128))
    wide = []
    for half in range(2):
        wide.append(jnp.concatenate([up_got[:, chan * 2 + half, :] for chan in range(2)], axis=0))
    back = mm(chan_ref[...], jnp.concatenate(wide, axis=1).astype(BF16))
    pooled = []
    grads = []
    for h in range(2):
        sides = []
        for k in range(2):
            r = 4 * h + 2 * k
            sides.append(
                jnp.concatenate([act[dd, dw, r * 32 : r * 32 + 128, :] for dd in range(4) for dw in range(3)], axis=0)
            )
        patches = jnp.concatenate(sides, axis=1)
        value = mm(w2_turned[...], patches) + b2
        out = jnp.maximum(value, LEAK * value)
        cell = out[0:64] + out[64:128] + out[128:192] + out[192:256]
        left, right = cell[:, :128], cell[:, 128:]
        left = left + pltpu.roll(left, 64, 1)
        right = right + pltpu.roll(right, 64, 1)
        pooled.append((jnp.where(lane < 64, left, right) * 0.125).astype(BF16))
        up = back[:, h * 128 : h * 128 + 128] * 0.125
        other = pltpu.roll(up, 64, 1)
        both = jnp.concatenate([jnp.where(lane < 64, up, other), jnp.where(lane < 64, other, up)], axis=1)
        weak = both * LEAK
        grad = jnp.concatenate(
            [jnp.where(value[g * 64 : g * 64 + 64] > 0, both, weak).astype(BF16) for g in range(4)], axis=0
        )
        grads.append(grad)
        if h == 0:
            full[...] = mm_nt(patches, grad)
        else:
            full[...] += mm_nt(patches, grad)

    lane = lanes_of((16, 128))
    for r in range(3):
        for t in range(3):
            near = []
            for s in range(4):
                a = ((r * 3 + t) * 4 + s) * 32
                b = (((r + 1) * 3 + t) * 4 + s) * 32
                near.append(full[a : a + 32, 0:128] + full[b : b + 32, 128:256])
            for s in range(3):
                low = near[s][:16] + pltpu.roll(near[s + 1][:16], 64, 1)
                high = pltpu.roll(near[s][16:], 64, 1) + near[s + 1][16:]
                at = (r * 3 + s) * 3 + t
                sg[at // 2, (at % 2) * 16 : (at % 2) * 16 + 16, :] = jnp.where(lane < 64, low, high).astype(SENT)
    sg[13, 16:32, :] = jnp.zeros((16, 128), SENT)
    sg[14:16] = jnp.zeros((2, 32, 128), SENT)
    chip, line = rank(0, gz, gy), rank(1, gz, gy)
    one_wait = share(0, lambda j: sg.at[j], sg_one, s_send.at[0], s_recv.at[0])
    sg_one[chip] = sg[chip]

    turned = lax.dot_general(
        chan_ref[...], jnp.concatenate(pooled, axis=1), (((0,), (0,)), ((), ())), preferred_element_type=F32
    )
    for half in range(2):
        for chan in range(2):
            pool_stage[:, chan * 2 + half, :] = turned[chan * 32 : chan * 32 + 32, half * 128 : half * 128 + 128]

    for h in range(2):
        pulled = mm(w2[...], grads[h])
        for dd in range(4):
            for t in range(3):
                at = (dd * 3 + t) * 128
                for k in range(2):
                    gact[dd, t, 2 * h + k] = pulled[at : at + 128, k * 128 : k * 128 + 128]

    def layer_back(d, _):
        for j in range(5):
            sides = []
            for k in range(2):
                parts = []
                for t in range(3):
                    value = None
                    for r, at in ((j, k * 32), (j - 1, 64 + k * 32)):
                        if 0 <= r < 4:
                            piece = gact[d, t, r, at : at + 32, :]
                            value = piece if value is None else value + piece
                    parts.append(value)
                value = (after(parts[0]) + parts[1] + before(parts[2])) * 0.125
                sides.append(jnp.where(inside(d, 2 * j + k), value, 0.0))
            strong = jnp.concatenate(sides, axis=1)
            weak = strong * LEAK
            seen = pre[d, :, j * 256 : j * 256 + 256].astype(F32)
            grad = jnp.concatenate(
                [jnp.where(seen[g * 32 : g * 32 + 32] > 0, strong, weak).astype(BF16) for g in range(8)], axis=0
            )
            ffull[...] += mm_nt(grad, patch[d, :, j * 256 : j * 256 + 256])
        return 0

    ffull[...] = jnp.zeros((256, 256), F32)
    lax.fori_loop(0, 4, layer_back, 0, unroll=True)
    flat = jnp.concatenate([ffull[g * 32 : g * 32 + 32, :] for g in range(8)], axis=1)
    pieces = []
    for _ in range(3):
        pieces.append(flat.astype(BF16))
        flat = flat - pieces[-1].astype(F32)
    total = mm(jnp.concatenate(pieces, axis=0), gather_ref[...])
    total = total[0:32] + total[32:64] + total[64:96]
    term[...] = total.astype(SENT)

    t_wait = share(0, lambda j: term, t_one, s_send.at[3], s_recv.at[3])
    t_one[chip] = term[...]
    one_wait()
    sg_part[...] = total16(sg_one).astype(SENT)
    two_wait = share(1, lambda j: sg_part, sg_two, s_send.at[1], s_recv.at[1])
    pool_wait = share(2, lambda j: pool_stage.at[j], pool_got, a_send.at[1], a_recv.at[1])
    pool_got[gz] = pool_stage[gz]
    sg_two[line] = sg_part[...]
    t_wait()
    t_part[...] = total16(t_one).astype(SENT)
    t_wait = share(1, lambda j: t_part, t_two, s_send.at[4], s_recv.at[4])
    t_two[line] = t_part[...]
    two_wait()
    sg_done[chip] = total16(sg_two).astype(SENT)
    done_wait = share(0, lambda j: sg_done.at[chip], sg_done, s_send.at[2], s_recv.at[2])
    pool_wait()
    for half in range(2):
        for chan in range(2):
            pool_out[chan, :, half * 128 : half * 128 + 128] = pool_got[:, chan * 2 + half, :].astype(BF16)
    t_wait()
    first_out[...] = total16(t_two)
    done_wait()
    second_out[...] = sg_done[...]


def finish(pool_in, first_in, second_in, pool_out, first_out, second_out):
    pool_out[...] = pool_in[...]
    turned = jnp.transpose(first_in[...])
    for i in range(27):
        first_out[i // 9, i // 3 % 3, i % 3] = turned[4 * i : 4 * i + 4, :]
        block = second_in[i // 2, (i % 2) * 16 : (i % 2) * 16 + 16, :].astype(F32)
        second_out[i // 9, i // 3 % 3, i % 3, 0:16, :] = block[:, :64]
        second_out[i // 9, i // 3 % 3, i % 3, 16:32, :] = block[:, 64:]


SENT = BF16


def on_device(volume, first_weight, first_bias, second_weight, second_bias, upstream):
    dma, mem = pltpu.SemaphoreType.DMA, pltpu.VMEM
    constants = [jnp.asarray(m()) for m in (spread_matrix, channel_matrix, turn_matrix, gather_matrix)]
    operands = [volume, first_weight, first_bias, second_weight, second_bias, upstream, *constants]
    results = pl.pallas_call(
        body,
        out_shape=[
            jax.ShapeDtypeStruct((2, 32, 256), BF16),
            jax.ShapeDtypeStruct((32, 128), F32),
            jax.ShapeDtypeStruct((16, 32, 128), SENT),
        ],
        in_specs=[VMEM] * len(operands),
        out_specs=[VMEM] * 3,
        scratch_shapes=[
            mem((4, 64, 256), BF16), mem((10, 96, 256), BF16), mem((32, 4, 128), F32), mem((32, 4, 128), F32),
            mem((32, 4, 128), F32), mem((32, 4, 128), F32),
            mem((128, 32), F32), mem((256, 256), BF16), mem((1536, 256), BF16), mem((256, 1536), BF16),
            mem((10, 4, 96, 128), F32), mem((4, 256, 1280), BF16), mem((4, 256, 1280), BF16), mem((4, 3, 320, 128), BF16),
            mem((1536, 256), F32), mem((4, 3, 4, 128, 128), F32), mem((256, 256), F32),
            mem((16, 32, 128), SENT), mem((16, 32, 128), SENT), mem((32, 128), SENT), mem((16, 32, 128), SENT),
            mem((16, 32, 128), SENT), mem((32, 128), SENT), mem((16, 32, 128), SENT), mem((32, 128), SENT),
            mem((16, 32, 128), SENT),
            dma((8,)), dma((8,)), dma((2,)), dma((2,)), dma((5,)), dma((5,)),
        ],
        compiler_params=pltpu.CompilerParams(vmem_limit_bytes=LIMIT, has_side_effects=True, collective_id=1),
    )(*operands)
    return pl.pallas_call(
        finish,
        out_shape=[
            jax.ShapeDtypeStruct((2, 32, 256), BF16),
            jax.ShapeDtypeStruct((3, 3, 3, 4, 32), F32),
            jax.ShapeDtypeStruct((3, 3, 3, 32, 64), F32),
        ],
        in_specs=[VMEM] * 3,
        out_specs=[VMEM] * 3,
    )(*results)


def solution(mesh):
    placed = (P(None, "gz", "gy", None), P(), P(), P(), P(), P("gz", None, "gy"))
    return jax.shard_map(
        on_device,
        mesh=mesh,
        in_specs=placed,
        out_specs=(P("gz", None, "gy"), P(), P()),
        check_vma=False,
    )
```

```python
import jax
import jax.numpy as jnp
import numpy as np
from jax import lax
from jax.experimental import pallas as pl
from jax.experimental.pallas import tpu as pltpu
from jax.sharding import PartitionSpec as P

LEAK = 0.3
F32 = jnp.float32
BF16 = jnp.bfloat16
MESH = pl.DeviceIdType.MESH
VMEM = pl.BlockSpec(memory_space=pltpu.VMEM)
GZ, GY = 32, 8
LIMIT = 56 * 2**20


def lanes_of(shape):
    return lax.broadcasted_iota(jnp.int32, shape, len(shape) - 1)


def before(x):
    lane = lanes_of(x.shape)
    return jnp.where(lane >= 64, pltpu.roll(x, 64, 1), jnp.where(lane == 0, 0.0, pltpu.roll(x, 65, 1)))


def after(x):
    lane = lanes_of(x.shape)
    return jnp.where(lane < 64, pltpu.roll(x, 64, 1), jnp.where(lane == 127, 0.0, pltpu.roll(x, 63, 1)))


def mm(a, b):
    return jnp.dot(a, b, preferred_element_type=F32)


def mm_nt(a, b):
    return lax.dot_general(a, b, (((1,), (1,)), ((), ())), preferred_element_type=F32)


def eye(n):
    return lax.broadcasted_iota(jnp.int32, (n, n), 0) == lax.broadcasted_iota(jnp.int32, (n, n), 1)


def one_hot(n):
    return jnp.where(eye(n), 1.0, 0.0).astype(BF16)


def column(row, times):
    n = row.shape[0]
    wide = jnp.broadcast_to(row[None, :], (n, n))
    once = jnp.sum(jnp.where(eye(n), wide, 0.0), axis=1, keepdims=True)
    return jnp.concatenate([once] * times, axis=0)


def place():
    return lax.axis_index("gz"), lax.axis_index("gy")


def spread_matrix():
    out = np.zeros((256, 4, 128), np.float32)
    for lane in range(128):
        cell = 2 * (lane % 64) + lane // 64
        for dw in range(4):
            w = 2 * cell + dw - 1
            if 0 <= w < 256:
                out[w, dw, lane] = 1
    return out.reshape(256, 512).astype(jnp.bfloat16)


def channel_matrix():
    out = np.zeros((64, 64), np.float32)
    for q in range(64):
        out[q, (q % 2) * 32 + q // 2] = 1
    return out.astype(jnp.bfloat16)


def turn_matrix():
    out = np.zeros((64, 64), np.float32)
    for r in range(16):
        for c in range(4):
            out[r * 4 + c, c * 16 + r] = 1
    return out.astype(jnp.bfloat16)


def gather_matrix():
    out = np.zeros((2, 2, 2, 4, 4, 4, 4, 128), np.float32)
    for pd in range(2):
        for pr in range(2):
            for pw in range(2):
                for r in range(3):
                    for s in range(3):
                        for t in range(3):
                            for c in range(4):
                                out[pd, pr, pw, pd + r, pw + t, pr + s, c, ((r * 3 + s) * 3 + t) * 4 + c] = 1
    return out.reshape(2048, 128).astype(jnp.bfloat16)


def around(dz, dy):
    gz, gy = place()
    return lax.rem(gz + dz + GZ, GZ), lax.rem(gy + dy + GY, GY)


def spread_order(kind):
    xs, ys, zs, cores = (range(n) for n in ((4, 4, 1, 1), (1, 1, 8, 2), (4, 4, 1, 2))[kind])
    all_ = [(x, y, z, c) for x in xs for y in ys for z in zs for c in cores]
    hops = lambda o: min(o[0], 4 - o[0]) + min(o[1], 4 - o[1]) + min(o[2], 8 - o[2]) + 0.5 * o[3]
    return sorted([o for o in all_ if any(o)], key=lambda o: -hops(o))


def shifted(offset):
    gz, gy = place()
    x, y, core = gz // 8, lax.rem(gz // 2, 4), lax.rem(gz, 2)
    dx, dy, dz, dc = offset
    x = lax.rem(x + dx, 4) if dx else x
    y = lax.rem(y + dy, 4) if dy else y
    core = 1 - core if dc else core
    return x * 8 + y * 2 + core, lax.rem(gy + dz, GY) if dz else gy


def rank(kind, gz, gy):
    return (gz // 2, gy * 2 + lax.rem(gz, 2), gz)[kind]


COUNT = (16, 16, 32)


def share(kind, source, landing, send, recv, after=0, then=None):
    gz, gy = place()
    slot = rank(kind, gz, gy)
    for number, offset in enumerate(spread_order(kind)):
        if then is not None and number == after:
            then()
        to = shifted(offset)
        pltpu.make_async_remote_copy(
            src_ref=source(rank(kind, *to)),
            dst_ref=landing.at[slot],
            send_sem=send,
            recv_sem=recv,
            device_id=to,
            device_id_type=MESH,
        ).start()

    def wait():
        pltpu.make_async_remote_copy(
            src_ref=landing.at[pl.ds(0, COUNT[kind] - 1)],
            dst_ref=landing.at[pl.ds(0, COUNT[kind] - 1)],
            send_sem=send,
            recv_sem=recv,
            device_id=around(1, 0),
            device_id_type=MESH,
        ).wait()

    return wait


def greet():
    gz, gy = place()
    barrier = pltpu.get_barrier_semaphore()

    def tell(to):
        pl.semaphore_signal(barrier, inc=1, device_id=to, device_id_type=MESH)

    far = lax.rem(gz + 2 * lax.rem(gz, 2) - 1 + GZ, GZ)
    for offset in spread_order(1):
        if offset[2]:
            tell(shifted(offset))
    for offset in spread_order(2):
        tell(shifted(offset))
    tell((far, lax.rem(gy + 1, GY)))
    tell((far, lax.rem(gy + GY - 1, GY)))

    def wait():
        pl.semaphore_wait(barrier, 47)

    return wait


def total16(landing):
    value = landing[0].astype(F32)
    for k in range(1, 16):
        value = value + landing[k].astype(F32)
    return value


def body(
    vol_in, w1_in, b1_in, w2_in, b2_in, up_in, spread_in, chan_in, turn_in, gather_in,
    pool_out, first_out, second_out,
    vol_ref, w1_ref, b1_ref, w2_ref, b2_ref, up_ref, spread_ref, chan_ref, turn_ref, gather_ref, load, seen,
    own, ext, up_stage, up_got, pool_stage, pool_got,
    w1_rows, w1, w2, w2_turned, rows, patch, pre, act, full, gact, ffull,
    sg, sg_one, sg_part, sg_two, sg_done, term, t_one, t_part, t_two,
    send, recv, a_send, a_recv, s_send, s_recv,
):
    gz, gy = place()
    loads = []
    for source, target in (
        (vol_in, vol_ref), (turn_in, turn_ref), (up_in, up_ref), (w1_in, w1_ref), (gather_in, gather_ref),
        (b1_in, b1_ref), (b2_in, b2_ref), (w2_in, w2_ref), (spread_in, spread_ref), (chan_in, chan_ref),
    ):
        loads.append(pltpu.make_async_copy(source, target, load.at[len(loads)]))
    for one in loads[:3]:
        one.start()
    greeted = greet()
    for one in loads[3:]:
        one.start()
    for one in loads[:3]:
        one.wait()

    for d in range(4):
        flat = jnp.concatenate([vol_ref[c, d] for c in range(4)], axis=0)
        own[d] = mm(turn_ref[...], flat).astype(BF16)
    for half in range(2):
        for chan in range(2):
            up_stage[:, chan * 2 + half, :] = up_ref[chan, :, half * 128 : half * 128 + 128].astype(F32)
    for one in loads[3:7]:
        one.wait()
    w1_rows[...] = jnp.zeros((128, 32), F32)
    for i in range(27):
        w1_rows[4 * i : 4 * i + 4, :] = w1_ref[i // 9, i // 3 % 3, i % 3].astype(F32)
    flat = mm_nt(one_hot(32), w1_rows[...].astype(BF16)).astype(BF16)
    for g in range(8):
        w1[g * 32 : g * 32 + 32, :] = mm_nt(flat, gather_ref[g * 256 : g * 256 + 256, :]).astype(BF16)
    b1 = column(b1_ref[...], 8)
    b2 = column(b2_ref[...], 4)
    greeted()

    copies = []

    def send_halo():
        for dz in (-1, 1, 0):
            src_d, dst_d = {-1: (slice(0, 3), slice(7, 10)), 0: (slice(0, 4), slice(3, 7)), 1: (slice(1, 4), slice(0, 3))}[dz]
            for dy in (-1, 1, 0):
                if dz == 0 and dy == 0:
                    continue
                src_r, dst_r = {
                    -1: (slice(0, 16), slice(80, 96)),
                    0: (slice(0, 64), slice(16, 80)),
                    1: (slice(48, 64), slice(0, 16)),
                }[dy]
                copy = pltpu.make_async_remote_copy(
                    src_ref=own.at[src_d, src_r],
                    dst_ref=ext.at[dst_d, dst_r],
                    send_sem=send.at[len(copies)],
                    recv_sem=recv.at[len(copies)],
                    device_id=around(dz, dy),
                    device_id_type=MESH,
                )
                copy.start()
                copies.append(copy)

    up_wait = share(2, lambda j: up_stage.at[j], up_got, a_send.at[0], a_recv.at[0], 10, send_halo)
    for one in loads[7:]:
        one.wait()

    lane = lanes_of((32, 128))
    zero = jnp.zeros((32, 128), F32)
    for t in range(3):
        for r in range(4):
            for s in range(4):
                at = ((r * 3 + t) * 4 + s) * 32
                for pd in range(2):
                    near = w2_ref[r - pd, s, t].astype(F32) if 0 <= r - pd < 3 and s < 3 else None
                    next_ = w2_ref[r - pd, s - 1, t].astype(F32) if 0 <= r - pd < 3 and s > 0 else None
                    left = zero[:, :64] if near is None else near
                    right = zero[:, :64] if next_ is None else next_
                    w2[at : at + 32, pd * 128 : pd * 128 + 128] = jnp.concatenate([left, right], axis=1).astype(BF16)
    w2_turned[...] = mm_nt(one_hot(256), w2[...]).astype(BF16)

    ext[3:7, 16:80] = own[...]
    for copy in copies:
        copy.wait()

    @pl.when(gz == 0)
    def _():
        ext[0:3] = jnp.zeros((3, 96, 256), BF16)

    @pl.when(gz == GZ - 1)
    def _():
        ext[7:10] = jnp.zeros((3, 96, 256), BF16)

    @pl.when(gy == 0)
    def _():
        ext[:, 0:16] = jnp.zeros((10, 16, 256), BF16)

    @pl.when(gy == GY - 1)
    def _():
        ext[:, 80:96] = jnp.zeros((10, 16, 256), BF16)

    flat = ext[...].reshape(960, 256)
    for side in range(2):
        wide = mm(flat, spread_ref[:, side * 256 : side * 256 + 256])
        for k in range(2):
            rows[:, 2 * side + k] = wide[:, k * 128 : k * 128 + 128].reshape(10, 96, 128)

    def inside(d, r):
        ok = jnp.where(d == 0, gz > 0, jnp.where(d == 3, gz < GZ - 1, True))
        if r == 0:
            ok = ok & (gy > 0)
        if r == 9:
            ok = ok & (gy < GY - 1)
        return ok

    def layer_one(d, _):
        for dd in range(4):
            for dw in range(4):
                for r in range(10):
                    patch[d, dd * 64 + dw * 16 : dd * 64 + dw * 16 + 16, r * 128 : r * 128 + 128] = rows[
                        2 * d + dd, dw, 8 * r + 4 : 8 * r + 20, :
                    ].astype(BF16)
        for j in range(5):
            value = mm(w1[...], patch[d, :, j * 256 : j * 256 + 256]) + b1
            pre[d, :, j * 256 : j * 256 + 256] = value.astype(BF16)
            out = jnp.maximum(value, LEAK * value)
            cell = out[0:32]
            for g in range(1, 8):
                cell = cell + out[g * 32 : g * 32 + 32]
            cell = (cell * 0.125).astype(BF16).astype(F32)
            for k in range(2):
                r = 2 * j + k
                one = jnp.where(inside(d, r), cell[:, k * 128 : k * 128 + 128], 0.0)
                act[d, 0, r * 32 : r * 32 + 32, :] = before(one).astype(BF16)
                act[d, 1, r * 32 : r * 32 + 32, :] = one.astype(BF16)
                act[d, 2, r * 32 : r * 32 + 32, :] = after(one).astype(BF16)
        return 0

    lax.fori_loop(0, 4, layer_one, 0, unroll=True)

    lane = lanes_of((64, 128))
    pooled = []

    def windows(h):
        sides = []
        for k in range(2):
            r = 4 * h + 2 * k
            sides.append(
                jnp.concatenate([act[dd, dw, r * 32 : r * 32 + 128, :] for dd in range(4) for dw in range(3)], axis=0)
            )
        return jnp.concatenate(sides, axis=1)

    for h in range(2):
        value = mm(w2_turned[...], windows(h)) + b2
        seen[h] = value
        out = jnp.maximum(value, LEAK * value)
        cell = out[0:64] + out[64:128] + out[128:192] + out[192:256]
        left, right = cell[:, :128], cell[:, 128:]
        left = left + pltpu.roll(left, 64, 1)
        right = right + pltpu.roll(right, 64, 1)
        pooled.append((jnp.where(lane < 64, left, right) * 0.125).astype(BF16))
    turned = lax.dot_general(
        chan_ref[...], jnp.concatenate(pooled, axis=1), (((0,), (0,)), ((), ())), preferred_element_type=F32
    )
    for half in range(2):
        for chan in range(2):
            pool_stage[:, chan * 2 + half, :] = turned[chan * 32 : chan * 32 + 32, half * 128 : half * 128 + 128]

    up_wait()
    up_got[gz] = up_stage[gz]
    wide = []
    for half in range(2):
        wide.append(jnp.concatenate([up_got[:, chan * 2 + half, :] for chan in range(2)], axis=0))
    back = mm(chan_ref[...], jnp.concatenate(wide, axis=1).astype(BF16))
    grads = []
    for h in range(2):
        up = back[:, h * 128 : h * 128 + 128] * 0.125
        other = pltpu.roll(up, 64, 1)
        both = jnp.concatenate([jnp.where(lane < 64, up, other), jnp.where(lane < 64, other, up)], axis=1)
        weak = both * LEAK
        grad = jnp.concatenate(
            [jnp.where(seen[h, g * 64 : g * 64 + 64] > 0, both, weak).astype(BF16) for g in range(4)], axis=0
        )
        grads.append(grad)
        if h == 0:
            full[...] = mm_nt(windows(h), grad)
        else:
            full[...] += mm_nt(windows(h), grad)

    lane = lanes_of((16, 128))
    for r in range(3):
        for t in range(3):
            near = []
            for s in range(4):
                a = ((r * 3 + t) * 4 + s) * 32
                b = (((r + 1) * 3 + t) * 4 + s) * 32
                near.append(full[a : a + 32, 0:128] + full[b : b + 32, 128:256])
            for s in range(3):
                low = near[s][:16] + pltpu.roll(near[s + 1][:16], 64, 1)
                high = pltpu.roll(near[s][16:], 64, 1) + near[s + 1][16:]
                at = (r * 3 + s) * 3 + t
                sg[at // 2, (at % 2) * 16 : (at % 2) * 16 + 16, :] = jnp.where(lane < 64, low, high).astype(SENT)
    sg[13, 16:32, :] = jnp.zeros((16, 128), SENT)
    sg[14:16] = jnp.zeros((2, 32, 128), SENT)
    chip, line = rank(0, gz, gy), rank(1, gz, gy)
    one_wait = share(0, lambda j: sg.at[j], sg_one, s_send.at[0], s_recv.at[0])
    sg_one[chip] = sg[chip]

    for h in range(2):
        pulled = mm(w2[...], grads[h])
        for dd in range(4):
            for t in range(3):
                at = (dd * 3 + t) * 128
                for k in range(2):
                    gact[dd, t, 2 * h + k] = pulled[at : at + 128, k * 128 : k * 128 + 128]

    def layer_back(d, _):
        for j in range(5):
            sides = []
            for k in range(2):
                parts = []
                for t in range(3):
                    value = None
                    for r, at in ((j, k * 32), (j - 1, 64 + k * 32)):
                        if 0 <= r < 4:
                            piece = gact[d, t, r, at : at + 32, :]
                            value = piece if value is None else value + piece
                    parts.append(value)
                value = (after(parts[0]) + parts[1] + before(parts[2])) * 0.125
                sides.append(jnp.where(inside(d, 2 * j + k), value, 0.0))
            strong = jnp.concatenate(sides, axis=1)
            weak = strong * LEAK
            seen = pre[d, :, j * 256 : j * 256 + 256].astype(F32)
            grad = jnp.concatenate(
                [jnp.where(seen[g * 32 : g * 32 + 32] > 0, strong, weak).astype(BF16) for g in range(8)], axis=0
            )
            ffull[...] += mm_nt(grad, patch[d, :, j * 256 : j * 256 + 256])
        return 0

    ffull[...] = jnp.zeros((256, 256), F32)
    lax.fori_loop(0, 4, layer_back, 0, unroll=True)
    flat = jnp.concatenate([ffull[g * 32 : g * 32 + 32, :] for g in range(8)], axis=1)
    pieces = []
    for _ in range(3):
        pieces.append(flat.astype(BF16))
        flat = flat - pieces[-1].astype(F32)
    total = mm(jnp.concatenate(pieces, axis=0), gather_ref[...])
    total = total[0:32] + total[32:64] + total[64:96]
    term[...] = total.astype(SENT)

    t_wait = share(0, lambda j: term, t_one, s_send.at[3], s_recv.at[3])
    t_one[chip] = term[...]
    one_wait()
    sg_part[...] = total16(sg_one).astype(SENT)
    two_wait = share(1, lambda j: sg_part, sg_two, s_send.at[1], s_recv.at[1])
    pool_wait = share(2, lambda j: pool_stage.at[j], pool_got, a_send.at[1], a_recv.at[1])
    pool_got[gz] = pool_stage[gz]
    sg_two[line] = sg_part[...]
    t_wait()
    t_part[...] = total16(t_one).astype(SENT)
    t_wait = share(1, lambda j: t_part, t_two, s_send.at[4], s_recv.at[4])
    t_two[line] = t_part[...]
    two_wait()
    sg_done[chip] = total16(sg_two).astype(SENT)
    done_wait = share(0, lambda j: sg_done.at[chip], sg_done, s_send.at[2], s_recv.at[2])
    pool_wait()
    for half in range(2):
        for chan in range(2):
            pool_out[chan, :, half * 128 : half * 128 + 128] = pool_got[:, chan * 2 + half, :].astype(BF16)
    t_wait()
    first_out[...] = total16(t_two)
    done_wait()
    second_out[...] = sg_done[...]


def finish(pool_in, first_in, second_in, pool_out, first_out, second_out):
    pool_out[...] = pool_in[...]
    turned = jnp.transpose(first_in[...])
    for i in range(27):
        first_out[i // 9, i // 3 % 3, i % 3] = turned[4 * i : 4 * i + 4, :]
        block = second_in[i // 2, (i % 2) * 16 : (i % 2) * 16 + 16, :].astype(F32)
        second_out[i // 9, i // 3 % 3, i % 3, 0:16, :] = block[:, :64]
        second_out[i // 9, i // 3 % 3, i % 3, 16:32, :] = block[:, 64:]


SENT = BF16


def on_device(volume, first_weight, first_bias, second_weight, second_bias, upstream):
    dma, mem = pltpu.SemaphoreType.DMA, pltpu.VMEM
    constants = [jnp.asarray(m()) for m in (spread_matrix, channel_matrix, turn_matrix, gather_matrix)]
    operands = [volume, first_weight, first_bias, second_weight, second_bias, upstream, *constants]
    results = pl.pallas_call(
        body,
        out_shape=[mem((2, 32, 256), BF16), mem((32, 128), F32), mem((16, 32, 128), SENT)],
        in_specs=[pl.BlockSpec(memory_space=pl.ANY)] * len(operands),
        out_specs=[VMEM] * 3,
        scratch_shapes=[
            *[mem(x.shape, x.dtype) for x in operands], dma((10,)), mem((2, 256, 256), F32),
            mem((4, 64, 256), BF16), mem((10, 96, 256), BF16), mem((32, 4, 128), F32), mem((32, 4, 128), F32),
            mem((32, 4, 128), F32), mem((32, 4, 128), F32),
            mem((128, 32), F32), mem((256, 256), BF16), mem((1536, 256), BF16), mem((256, 1536), BF16),
            mem((10, 4, 96, 128), F32), mem((4, 256, 1280), BF16), mem((4, 256, 1280), BF16), mem((4, 3, 320, 128), BF16),
            mem((1536, 256), F32), mem((4, 3, 4, 128, 128), F32), mem((256, 256), F32),
            mem((16, 32, 128), SENT), mem((16, 32, 128), SENT), mem((32, 128), SENT), mem((16, 32, 128), SENT),
            mem((16, 32, 128), SENT), mem((32, 128), SENT), mem((16, 32, 128), SENT), mem((32, 128), SENT),
            mem((16, 32, 128), SENT),
            dma((8,)), dma((8,)), dma((2,)), dma((2,)), dma((5,)), dma((5,)),
        ],
        compiler_params=pltpu.CompilerParams(vmem_limit_bytes=LIMIT, has_side_effects=True, collective_id=1),
    )(*operands)
    return pl.pallas_call(
        finish,
        out_shape=[
            jax.ShapeDtypeStruct((2, 32, 256), BF16),
            jax.ShapeDtypeStruct((3, 3, 3, 4, 32), F32),
            jax.ShapeDtypeStruct((3, 3, 3, 32, 64), F32),
        ],
        in_specs=[VMEM] * 3,
        out_specs=[VMEM] * 3,
    )(*[pltpu.with_memory_space_constraint(x, pltpu.VMEM) for x in results])


def solution(mesh):
    placed = (P(None, "gz", "gy", None), P(), P(), P(), P(), P("gz", None, "gy"))
    return jax.shard_map(
        on_device,
        mesh=mesh,
        in_specs=placed,
        out_specs=(P("gz", None, "gy"), P(), P()),
        check_vma=False,
    )
```

```python
import jax
import jax.numpy as jnp
import numpy as np
from jax import lax
from jax.experimental import pallas as pl
from jax.experimental.pallas import tpu as pltpu
from jax.sharding import PartitionSpec as P

LEAK = 0.3
F32 = jnp.float32
BF16 = jnp.bfloat16
MESH = pl.DeviceIdType.MESH
VMEM = pl.BlockSpec(memory_space=pltpu.VMEM)
GZ, GY = 32, 8
LIMIT = 56 * 2**20


def lanes_of(shape):
    return lax.broadcasted_iota(jnp.int32, shape, len(shape) - 1)


def before(x):
    lane = lanes_of(x.shape)
    return jnp.where(lane >= 64, pltpu.roll(x, 64, 1), jnp.where(lane == 0, 0.0, pltpu.roll(x, 65, 1)))


def after(x):
    lane = lanes_of(x.shape)
    return jnp.where(lane < 64, pltpu.roll(x, 64, 1), jnp.where(lane == 127, 0.0, pltpu.roll(x, 63, 1)))


def mm(a, b):
    return jnp.dot(a, b, preferred_element_type=F32)


def mm_nt(a, b):
    return lax.dot_general(a, b, (((1,), (1,)), ((), ())), preferred_element_type=F32)


def eye(n):
    return lax.broadcasted_iota(jnp.int32, (n, n), 0) == lax.broadcasted_iota(jnp.int32, (n, n), 1)


def one_hot(n):
    return jnp.where(eye(n), 1.0, 0.0).astype(BF16)


def column(row, times):
    n = row.shape[0]
    wide = jnp.broadcast_to(row[None, :], (n, n))
    once = jnp.sum(jnp.where(eye(n), wide, 0.0), axis=1, keepdims=True)
    return jnp.concatenate([once] * times, axis=0)


def place():
    return lax.axis_index("gz"), lax.axis_index("gy")


def spread_matrix():
    out = np.zeros((256, 4, 128), np.float32)
    for lane in range(128):
        cell = 2 * (lane % 64) + lane // 64
        for dw in range(4):
            w = 2 * cell + dw - 1
            if 0 <= w < 256:
                out[w, dw, lane] = 1
    return out.reshape(256, 512).astype(jnp.bfloat16)


def channel_matrix():
    out = np.zeros((64, 64), np.float32)
    for q in range(64):
        out[q, (q % 2) * 32 + q // 2] = 1
    return out.astype(jnp.bfloat16)


def turn_matrix():
    out = np.zeros((64, 64), np.float32)
    for r in range(16):
        for c in range(4):
            out[r * 4 + c, c * 16 + r] = 1
    return out.astype(jnp.bfloat16)


def gather_matrix():
    out = np.zeros((2, 2, 2, 4, 4, 4, 4, 128), np.float32)
    for pd in range(2):
        for pr in range(2):
            for pw in range(2):
                for r in range(3):
                    for s in range(3):
                        for t in range(3):
                            for c in range(4):
                                out[pd, pr, pw, pd + r, pw + t, pr + s, c, ((r * 3 + s) * 3 + t) * 4 + c] = 1
    out = out.reshape(2048, 128)
    mirrored = np.zeros_like(out)
    for r in range(3):
        mirrored[:, r * 36 : r * 36 + 36] = out[:, (2 - r) * 36 : (2 - r) * 36 + 36]
    return np.stack([out, mirrored]).astype(jnp.bfloat16)


def around(dz, dy):
    gz, gy = place()
    return lax.rem(gz + dz + GZ, GZ), lax.rem(gy + dy + GY, GY)


def hops(offset):
    x, y, z, core = offset
    return min(x, 4 - x) + min(y, 4 - y) + min(z, 8 - z) + 0.5 * core


def spread_order(kind):
    xs, ys, zs, cores = (range(n) for n in ((4, 4, 1, 1), (1, 1, 8, 2), (4, 4, 1, 2))[kind])
    all_ = [(x, y, z, c) for x in xs for y in ys for z in zs for c in cores]
    return sorted([o for o in all_ if any(o)], key=lambda o: -hops(o))


def shifted(offset):
    gz, gy = place()
    x, y, core = gz // 8, lax.rem(gz // 2, 4), lax.rem(gz, 2)
    dx, dy, dz, dc = offset
    x = lax.rem(x + dx, 4) if dx else x
    y = lax.rem(y + dy, 4) if dy else y
    core = 1 - core if dc else core
    return x * 8 + y * 2 + core, lax.rem(gy + dz, GY) if dz else gy


def rank(kind, gz, gy):
    return (gz // 2, gy * 2 + lax.rem(gz, 2), gz)[kind]


COUNT = (16, 16, 32)


def share(kind, source, landing, send, recv, after=0, then=None):
    gz, gy = place()
    slot = rank(kind, gz, gy)
    for number, offset in enumerate(spread_order(kind)):
        if then is not None and number == after:
            then()
        to = shifted(offset)
        pltpu.make_async_remote_copy(
            src_ref=source(rank(kind, *to)),
            dst_ref=landing.at[slot],
            send_sem=send,
            recv_sem=recv,
            device_id=to,
            device_id_type=MESH,
        ).start()

    def wait():
        pltpu.make_async_remote_copy(
            src_ref=landing.at[pl.ds(0, COUNT[kind] - 1)],
            dst_ref=landing.at[pl.ds(0, COUNT[kind] - 1)],
            send_sem=send,
            recv_sem=recv,
            device_id=around(1, 0),
            device_id_type=MESH,
        ).wait()

    return wait


def greet():
    gz, gy = place()
    barrier = pltpu.get_barrier_semaphore()

    def tell(to):
        pl.semaphore_signal(barrier, inc=1, device_id=to, device_id_type=MESH)

    far = lax.rem(gz + 2 * lax.rem(gz, 2) - 1 + GZ, GZ)
    tell((far, lax.rem(gy + 1, GY)))
    tell((far, lax.rem(gy + GY - 1, GY)))
    offsets = [o for o in spread_order(1) if o[2]] + spread_order(2)
    for offset in sorted(offsets, key=lambda o: -hops(o)):
        tell(shifted(offset))

    def wait():
        pl.semaphore_wait(barrier, 47)

    return wait


def total16(landing):
    value = landing[0].astype(F32)
    for k in range(1, 16):
        value = value + landing[k].astype(F32)
    return value


def body(
    vol_in, w1_in, b1_in, w2_in, b2_in, up_in, spread_in, chan_in, turn_in, gather_in,
    pool_out, first_out, second_out,
    vol_ref, w1_ref, b1_ref, w2_ref, b2_ref, up_ref, spread_ref, chan_ref, turn_ref, gather_ref, load, seen,
    own, ext, up_stage, up_got, pool_stage, pool_got,
    w1_rows, w1, w2, w2_turned, rows, patch, pre, act, full, gact, ffull,
    sg, sg_one, sg_part, sg_two, sg_done, term, t_one, t_part, t_two,
    send, recv, a_send, a_recv, s_send, s_recv,
):
    gz, gy = place()
    core = lax.rem(gz, 2)
    near, far = gz + 1 - 2 * core, lax.rem(gz + 2 * core - 1 + GZ, GZ)
    edge = (gz == 0) | (gz == GZ - 1)

    def depth(d, count):
        return jnp.where(core == 0, count - 1 - d, d)

    loads = []
    for source, target in (
        (vol_in, vol_ref), (turn_in, turn_ref), (up_in, up_ref), (w1_in, w1_ref), (gather_in.at[1 - core], gather_ref),
        (b1_in, b1_ref), (b2_in, b2_ref), (w2_in, w2_ref), (spread_in, spread_ref), (chan_in, chan_ref),
    ):
        loads.append(pltpu.make_async_copy(source, target, load.at[len(loads)]))
    greeted = greet()
    for one in loads:
        one.start()
    for one in loads[:3]:
        one.wait()

    for d in range(4):
        flat = jnp.concatenate([vol_ref[c, depth(d, 4)] for c in range(4)], axis=0)
        own[d] = mm(turn_ref[...], flat).astype(BF16)
    for half in range(2):
        for chan in range(2):
            up_stage[:, chan * 2 + half, :] = up_ref[chan, :, half * 128 : half * 128 + 128].astype(F32)
    for one in loads[3:7]:
        one.wait()
    w1_rows[...] = jnp.zeros((128, 32), F32)
    for i in range(27):
        w1_rows[4 * i : 4 * i + 4, :] = w1_ref[i // 9, i // 3 % 3, i % 3].astype(F32)
    flat = mm_nt(one_hot(32), w1_rows[...].astype(BF16)).astype(BF16)
    for g in range(8):
        w1[g * 32 : g * 32 + 32, :] = mm_nt(flat, gather_ref[g * 256 : g * 256 + 256, :]).astype(BF16)
    b1 = column(b1_ref[...], 8)
    b2 = column(b2_ref[...], 4)
    greeted()

    copies = []

    def send_halo():
        sides = (
            (far, slice(1, 4), slice(7, 10), (1, -1, 0)),
            (near, slice(0, 3), slice(0, 3), (1, -1, 0)),
            (gz, slice(0, 4), slice(3, 7), (1, -1)),
        )
        for to, src_d, dst_d, steps in sides:
            for dy in steps:
                src_r, dst_r = {
                    -1: (slice(0, 16), slice(80, 96)),
                    0: (slice(0, 64), slice(16, 80)),
                    1: (slice(48, 64), slice(0, 16)),
                }[dy]
                copy = pltpu.make_async_remote_copy(
                    src_ref=own.at[src_d, src_r],
                    dst_ref=ext.at[dst_d, dst_r],
                    send_sem=send.at[len(copies)],
                    recv_sem=recv.at[len(copies)],
                    device_id=(to, lax.rem(gy + dy + GY, GY)),
                    device_id_type=MESH,
                )
                copy.start()
                copies.append(copy)

    up_wait = share(2, lambda j: up_stage.at[j], up_got, a_send.at[0], a_recv.at[0], 0, send_halo)
    for one in loads[7:]:
        one.wait()

    lane = lanes_of((32, 128))
    zero = jnp.zeros((32, 128), F32)
    for t in range(3):
        for r in range(4):
            for s in range(4):
                at = ((r * 3 + t) * 4 + s) * 32
                for pd in range(2):
                    here = w2_ref[depth(r - pd, 3), s, t].astype(F32) if 0 <= r - pd < 3 and s < 3 else None
                    next_ = w2_ref[depth(r - pd, 3), s - 1, t].astype(F32) if 0 <= r - pd < 3 and s > 0 else None
                    left = zero[:, :64] if here is None else here
                    right = zero[:, :64] if next_ is None else next_
                    w2[at : at + 32, pd * 128 : pd * 128 + 128] = jnp.concatenate([left, right], axis=1).astype(BF16)
    w2_turned[...] = mm_nt(one_hot(256), w2[...]).astype(BF16)

    def widen(value, targets, at):
        many, high, _ = value.shape
        flat = value.reshape(many * high, 256)
        for side in range(2):
            wide = mm(flat, spread_ref[:, side * 256 : side * 256 + 256])
            for k in range(2):
                for i, d in enumerate(targets):
                    rows[d, 2 * side + k, at : at + high] = wide[i * high : i * high + high, k * 128 : k * 128 + 128]

    def clear(deps, at):
        ext[deps, at : at + 16] = jnp.zeros((deps.stop - deps.start, 16, 256), BF16)

    def inside(d, r):
        ok = None
        if d == 3:
            ok = jnp.logical_not(edge)
        if r in (0, 9):
            side = gy > 0 if r == 0 else gy < GY - 1
            ok = side if ok is None else ok & side
        return ok

    def keep(ok, value):
        return value if ok is None else jnp.where(ok, value, 0.0)

    def layer_one(d):
        for dd in range(4):
            for dw in range(4):
                for r in range(10):
                    patch[d, dd * 64 + dw * 16 : dd * 64 + dw * 16 + 16, r * 128 : r * 128 + 128] = rows[
                        2 * d + dd, dw, 8 * r + 4 : 8 * r + 20, :
                    ].astype(BF16)
        for j in range(5):
            value = mm(w1[...], patch[d, :, j * 256 : j * 256 + 256]) + b1
            pre[d, :, j * 256 : j * 256 + 256] = value.astype(BF16)
            out = jnp.maximum(value, LEAK * value)
            cell = out[0:32]
            for g in range(1, 8):
                cell = cell + out[g * 32 : g * 32 + 32]
            cell = (cell * 0.125).astype(BF16).astype(F32)
            for k in range(2):
                r = 2 * j + k
                one = keep(inside(d, r), cell[:, k * 128 : k * 128 + 128])
                act[d, 0, r * 32 : r * 32 + 32, :] = before(one).astype(BF16)
                act[d, 1, r * 32 : r * 32 + 32, :] = one.astype(BF16)
                act[d, 2, r * 32 : r * 32 + 32, :] = after(one).astype(BF16)

    def windows(h, deps):
        sides = []
        for k in range(2):
            r = 4 * h + 2 * k
            sides.append(jnp.concatenate([act[dd, dw, r * 32 : r * 32 + 128, :] for dd in deps for dw in range(3)], axis=0))
        return jnp.concatenate(sides, axis=1)

    widen(own[...], (3, 4, 5, 6), 16)
    for copy in copies[3:]:
        copy.wait()

    @pl.when(gy == 0)
    def _():
        clear(slice(0, 7), 0)

    @pl.when(gy == GY - 1)
    def _():
        clear(slice(0, 7), 80)

    widen(ext[0:3], (2, 1, 0), 0)
    for at in (0, 80):
        widen(ext[3:7, at : at + 16], (3, 4, 5, 6), at)
    for d in range(2):
        layer_one(d)
    for h in range(2):
        seen[h] = mm(w2_turned[:, :768], windows(h, (0, 1))) + b2

    for copy in copies[:3]:
        copy.wait()

    @pl.when(gy == 0)
    def _():
        clear(slice(7, 10), 0)

    @pl.when(gy == GY - 1)
    def _():
        clear(slice(7, 10), 80)

    @pl.when(edge)
    def _():
        ext[7:10] = jnp.zeros((3, 96, 256), BF16)

    widen(ext[7:10], (9, 8, 7), 0)
    for d in range(2, 4):
        layer_one(d)

    lane = lanes_of((64, 128))
    pooled = []
    for h in range(2):
        value = seen[h] + mm(w2_turned[:, 768:], windows(h, (2, 3)))
        seen[h] = value
        out = jnp.maximum(value, LEAK * value)
        cell = out[0:64] + out[64:128] + out[128:192] + out[192:256]
        left, right = cell[:, :128], cell[:, 128:]
        left = left + pltpu.roll(left, 64, 1)
        right = right + pltpu.roll(right, 64, 1)
        pooled.append((jnp.where(lane < 64, left, right) * 0.125).astype(BF16))
    turned = lax.dot_general(
        chan_ref[...], jnp.concatenate(pooled, axis=1), (((0,), (0,)), ((), ())), preferred_element_type=F32
    )
    for half in range(2):
        for chan in range(2):
            pool_stage[:, chan * 2 + half, :] = turned[chan * 32 : chan * 32 + 32, half * 128 : half * 128 + 128]

    up_wait()
    up_got[gz] = up_stage[gz]
    wide = []
    for half in range(2):
        wide.append(jnp.concatenate([up_got[:, chan * 2 + half, :] for chan in range(2)], axis=0))
    back = mm(chan_ref[...], jnp.concatenate(wide, axis=1).astype(BF16))
    grads = []
    for h in range(2):
        up = back[:, h * 128 : h * 128 + 128] * 0.125
        other = pltpu.roll(up, 64, 1)
        both = jnp.concatenate([jnp.where(lane < 64, up, other), jnp.where(lane < 64, other, up)], axis=1)
        weak = both * LEAK
        grad = jnp.concatenate(
            [jnp.where(seen[h, g * 64 : g * 64 + 64] > 0, both, weak).astype(BF16) for g in range(4)], axis=0
        )
        grads.append(grad)
        if h == 0:
            full[...] = mm_nt(windows(h, range(4)), grad)
        else:
            full[...] += mm_nt(windows(h, range(4)), grad)

    lane = lanes_of((16, 128))
    for r in range(3):
        for t in range(3):
            near = []
            for s in range(4):
                a = ((r * 3 + t) * 4 + s) * 32
                b = (((r + 1) * 3 + t) * 4 + s) * 32
                near.append(full[a : a + 32, 0:128] + full[b : b + 32, 128:256])
            for s in range(3):
                low = near[s][:16] + pltpu.roll(near[s + 1][:16], 64, 1)
                high = pltpu.roll(near[s][16:], 64, 1) + near[s + 1][16:]
                at = (depth(r, 3) * 3 + s) * 3 + t
                sg[pl.ds(pl.multiple_of(at * 16, 16), 16), :] = jnp.where(lane < 64, low, high).astype(SENT)
    sg[432:512] = jnp.zeros((80, 128), SENT)
    chip, line = rank(0, gz, gy), rank(1, gz, gy)
    one_wait = share(0, lambda j: sg.at[pl.ds(pl.multiple_of(j * 32, 32), 32)], sg_one, s_send.at[0], s_recv.at[0])
    sg_one[chip] = sg[pl.ds(pl.multiple_of(chip * 32, 32), 32), :]

    for h in range(2):
        pulled = mm(w2[...], grads[h])
        for dd in range(4):
            for t in range(3):
                at = (dd * 3 + t) * 128
                for k in range(2):
                    gact[dd, t, 2 * h + k] = pulled[at : at + 128, k * 128 : k * 128 + 128]

    def layer_back(d):
        for j in range(5):
            sides = []
            for k in range(2):
                parts = []
                for t in range(3):
                    value = None
                    for r, at in ((j, k * 32), (j - 1, 64 + k * 32)):
                        if 0 <= r < 4:
                            piece = gact[d, t, r, at : at + 32, :]
                            value = piece if value is None else value + piece
                    parts.append(value)
                value = (after(parts[0]) + parts[1] + before(parts[2])) * 0.125
                sides.append(keep(inside(d, 2 * j + k), value))
            strong = jnp.concatenate(sides, axis=1)
            weak = strong * LEAK
            seen = pre[d, :, j * 256 : j * 256 + 256].astype(F32)
            grad = jnp.concatenate(
                [jnp.where(seen[g * 32 : g * 32 + 32] > 0, strong, weak).astype(BF16) for g in range(8)], axis=0
            )
            ffull[...] += mm_nt(grad, patch[d, :, j * 256 : j * 256 + 256])

    ffull[...] = jnp.zeros((256, 256), F32)
    for d in range(4):
        layer_back(d)
    flat = jnp.concatenate([ffull[g * 32 : g * 32 + 32, :] for g in range(8)], axis=1)
    pieces = []
    for _ in range(3):
        pieces.append(flat.astype(BF16))
        flat = flat - pieces[-1].astype(F32)
    total = mm(jnp.concatenate(pieces, axis=0), gather_ref[...])
    total = total[0:32] + total[32:64] + total[64:96]
    term[...] = total.astype(SENT)

    t_wait = share(0, lambda j: term, t_one, s_send.at[3], s_recv.at[3])
    t_one[chip] = term[...]
    one_wait()
    sg_part[...] = total16(sg_one).astype(SENT)
    two_wait = share(1, lambda j: sg_part, sg_two, s_send.at[1], s_recv.at[1])
    pool_wait = share(2, lambda j: pool_stage.at[j], pool_got, a_send.at[1], a_recv.at[1])
    pool_got[gz] = pool_stage[gz]
    sg_two[line] = sg_part[...]
    t_wait()
    t_part[...] = total16(t_one).astype(SENT)
    t_wait = share(1, lambda j: t_part, t_two, s_send.at[4], s_recv.at[4])
    t_two[line] = t_part[...]
    two_wait()
    sg_done[chip] = total16(sg_two).astype(SENT)
    done_wait = share(0, lambda j: sg_done.at[chip], sg_done, s_send.at[2], s_recv.at[2])
    pool_wait()
    for half in range(2):
        for chan in range(2):
            pool_out[chan, :, half * 128 : half * 128 + 128] = pool_got[:, chan * 2 + half, :].astype(BF16)
    t_wait()
    first_out[...] = total16(t_two)
    done_wait()
    second_out[...] = sg_done[...]


def finish(pool_in, first_in, second_in, pool_out, first_out, second_out):
    pool_out[...] = pool_in[...]
    turned = jnp.transpose(first_in[...])
    for i in range(27):
        first_out[i // 9, i // 3 % 3, i % 3] = turned[4 * i : 4 * i + 4, :]
        block = second_in[i // 2, (i % 2) * 16 : (i % 2) * 16 + 16, :].astype(F32)
        second_out[i // 9, i // 3 % 3, i % 3, 0:16, :] = block[:, :64]
        second_out[i // 9, i // 3 % 3, i % 3, 16:32, :] = block[:, 64:]


SENT = BF16


def on_device(volume, first_weight, first_bias, second_weight, second_bias, upstream):
    dma, mem = pltpu.SemaphoreType.DMA, pltpu.VMEM
    constants = [jnp.asarray(m()) for m in (spread_matrix, channel_matrix, turn_matrix, gather_matrix)]
    operands = [volume, first_weight, first_bias, second_weight, second_bias, upstream, *constants]
    results = pl.pallas_call(
        body,
        out_shape=[mem((2, 32, 256), BF16), mem((32, 128), F32), mem((16, 32, 128), SENT)],
        in_specs=[pl.BlockSpec(memory_space=pl.ANY)] * len(operands),
        out_specs=[VMEM] * 3,
        scratch_shapes=[
            *[mem(x.shape, x.dtype) for x in operands[:-1]], mem((2048, 128), BF16), dma((10,)), mem((2, 256, 256), F32),
            mem((4, 64, 256), BF16), mem((10, 96, 256), BF16), mem((32, 4, 128), F32), mem((32, 4, 128), F32),
            mem((32, 4, 128), F32), mem((32, 4, 128), F32),
            mem((128, 32), F32), mem((256, 256), BF16), mem((1536, 256), BF16), mem((256, 1536), BF16),
            mem((10, 4, 96, 128), F32), mem((4, 256, 1280), BF16), mem((4, 256, 1280), BF16), mem((4, 3, 320, 128), BF16),
            mem((1536, 256), F32), mem((4, 3, 4, 128, 128), F32), mem((256, 256), F32),
            mem((512, 128), SENT), mem((16, 32, 128), SENT), mem((32, 128), SENT), mem((16, 32, 128), SENT),
            mem((16, 32, 128), SENT), mem((32, 128), SENT), mem((16, 32, 128), SENT), mem((32, 128), SENT),
            mem((16, 32, 128), SENT),
            dma((8,)), dma((8,)), dma((2,)), dma((2,)), dma((5,)), dma((5,)),
        ],
        compiler_params=pltpu.CompilerParams(vmem_limit_bytes=LIMIT, has_side_effects=True, collective_id=1),
    )(*operands)
    return pl.pallas_call(
        finish,
        out_shape=[
            jax.ShapeDtypeStruct((2, 32, 256), BF16),
            jax.ShapeDtypeStruct((3, 3, 3, 4, 32), F32),
            jax.ShapeDtypeStruct((3, 3, 3, 32, 64), F32),
        ],
        in_specs=[VMEM] * 3,
        out_specs=[VMEM] * 3,
    )(*[pltpu.with_memory_space_constraint(x, pltpu.VMEM) for x in results])


def solution(mesh):
    placed = (P(None, "gz", "gy", None), P(), P(), P(), P(), P("gz", None, "gy"))
    return jax.shard_map(
        on_device,
        mesh=mesh,
        in_specs=placed,
        out_specs=(P("gz", None, "gy"), P(), P()),
        check_vma=False,
    )
```

```python
import jax
import jax.numpy as jnp
import numpy as np
from jax import lax
from jax.experimental import pallas as pl
from jax.experimental.pallas import tpu as pltpu
from jax.sharding import PartitionSpec as P

LEAK = 0.3
F32 = jnp.float32
BF16 = jnp.bfloat16
MESH = pl.DeviceIdType.MESH
VMEM = pl.BlockSpec(memory_space=pltpu.VMEM)
GZ, GY = 32, 8
LIMIT = 56 * 2**20


def lanes_of(shape):
    return lax.broadcasted_iota(jnp.int32, shape, len(shape) - 1)


def before(x):
    lane = lanes_of(x.shape)
    return jnp.where(lane >= 64, pltpu.roll(x, 64, 1), jnp.where(lane == 0, 0.0, pltpu.roll(x, 65, 1)))


def after(x):
    lane = lanes_of(x.shape)
    return jnp.where(lane < 64, pltpu.roll(x, 64, 1), jnp.where(lane == 127, 0.0, pltpu.roll(x, 63, 1)))


def mm(a, b):
    return jnp.dot(a, b, preferred_element_type=F32)


def mm_nt(a, b):
    return lax.dot_general(a, b, (((1,), (1,)), ((), ())), preferred_element_type=F32)


def eye(n):
    return lax.broadcasted_iota(jnp.int32, (n, n), 0) == lax.broadcasted_iota(jnp.int32, (n, n), 1)


def one_hot(n):
    return jnp.where(eye(n), 1.0, 0.0).astype(BF16)


def column(row, times):
    n = row.shape[0]
    wide = jnp.broadcast_to(row[None, :], (n, n))
    once = jnp.sum(jnp.where(eye(n), wide, 0.0), axis=1, keepdims=True)
    return jnp.concatenate([once] * times, axis=0)


def place():
    return lax.axis_index("gz"), lax.axis_index("gy")


def spread_matrix():
    out = np.zeros((256, 4, 128), np.float32)
    for lane in range(128):
        cell = 2 * (lane % 64) + lane // 64
        for dw in range(4):
            w = 2 * cell + dw - 1
            if 0 <= w < 256:
                out[w, dw, lane] = 1
    return out.reshape(256, 512).astype(jnp.bfloat16)


def channel_matrix():
    out = np.zeros((64, 64), np.float32)
    for q in range(64):
        out[q, (q % 2) * 32 + q // 2] = 1
    return out.astype(jnp.bfloat16)


def turn_matrix():
    out = np.zeros((64, 64), np.float32)
    for r in range(16):
        for c in range(4):
            out[r * 4 + c, c * 16 + r] = 1
    return out.astype(jnp.bfloat16)


def gather_matrix():
    out = np.zeros((2, 2, 2, 4, 4, 4, 4, 128), np.float32)
    for pd in range(2):
        for pr in range(2):
            for pw in range(2):
                for r in range(3):
                    for s in range(3):
                        for t in range(3):
                            for c in range(4):
                                out[pd, pr, pw, pd + r, pw + t, pr + s, c, ((r * 3 + s) * 3 + t) * 4 + c] = 1
    out = out.reshape(2048, 128)
    mirrored = np.zeros_like(out)
    for r in range(3):
        mirrored[:, r * 36 : r * 36 + 36] = out[:, (2 - r) * 36 : (2 - r) * 36 + 36]
    return np.stack([out, mirrored]).astype(jnp.bfloat16)


def around(dz, dy):
    gz, gy = place()
    return lax.rem(gz + dz + GZ, GZ), lax.rem(gy + dy + GY, GY)


def hops(offset):
    x, y, z, core = offset
    return min(x, 4 - x) + min(y, 4 - y) + min(z, 8 - z) + 0.5 * core


def spread_order(kind):
    xs, ys, zs, cores = (range(n) for n in ((4, 4, 1, 1), (1, 1, 8, 2), (4, 4, 1, 2))[kind])
    all_ = [(x, y, z, c) for x in xs for y in ys for z in zs for c in cores]
    return sorted([o for o in all_ if any(o)], key=lambda o: -hops(o))


def shifted(offset):
    gz, gy = place()
    x, y, core = gz // 8, lax.rem(gz // 2, 4), lax.rem(gz, 2)
    dx, dy, dz, dc = offset
    x = lax.rem(x + dx, 4) if dx else x
    y = lax.rem(y + dy, 4) if dy else y
    core = 1 - core if dc else core
    return x * 8 + y * 2 + core, lax.rem(gy + dz, GY) if dz else gy


def rank(kind, gz, gy):
    return (gz // 2, gy * 2 + lax.rem(gz, 2), gz)[kind]


COUNT = (16, 16, 32)


def share(kind, source, landing, send, recv, after=0, then=None):
    gz, gy = place()
    slot = rank(kind, gz, gy)
    for number, offset in enumerate(spread_order(kind)):
        if then is not None and number == after:
            then()
        to = shifted(offset)
        pltpu.make_async_remote_copy(
            src_ref=source(rank(kind, *to)),
            dst_ref=landing.at[slot],
            send_sem=send,
            recv_sem=recv,
            device_id=to,
            device_id_type=MESH,
        ).start()

    def wait():
        pltpu.make_async_remote_copy(
            src_ref=landing.at[pl.ds(0, COUNT[kind] - 1)],
            dst_ref=landing.at[pl.ds(0, COUNT[kind] - 1)],
            send_sem=send,
            recv_sem=recv,
            device_id=around(1, 0),
            device_id_type=MESH,
        ).wait()

    return wait


def greet():
    gz, gy = place()
    barrier = pltpu.get_barrier_semaphore()

    def tell(to):
        pl.semaphore_signal(barrier, inc=1, device_id=to, device_id_type=MESH)

    far = lax.rem(gz + 2 * lax.rem(gz, 2) - 1 + GZ, GZ)
    tell((far, lax.rem(gy + 1, GY)))
    tell((far, lax.rem(gy + GY - 1, GY)))
    offsets = [o for o in spread_order(1) if o[2]] + spread_order(2)
    for offset in sorted(offsets, key=lambda o: -hops(o)):
        tell(shifted(offset))

    def wait():
        pl.semaphore_wait(barrier, 47)

    return wait


def total16(landing):
    value = landing[0].astype(F32)
    for k in range(1, 16):
        value = value + landing[k].astype(F32)
    return value


def body(
    vol_in, w1_in, b1_in, w2_in, b2_in, up_in, spread_in, chan_in, turn_in, gather_in,
    pool_out, first_out, second_out,
    vol_ref, w1_ref, b1_ref, w2_ref, b2_ref, up_ref, spread_ref, chan_ref, turn_ref, gather_ref, load, seen,
    own, ext, up_stage, up_got, pool_stage, pool_got,
    w1_rows, w1, w2, w2_turned, rows, patch, pre, act, full, gact, ffull,
    sg, sg_one, sg_part, sg_two, sg_done, term, t_one, t_part, t_two,
    send, recv, a_send, a_recv, s_send, s_recv,
):
    gz, gy = place()
    core = lax.rem(gz, 2)
    near, far = gz + 1 - 2 * core, lax.rem(gz + 2 * core - 1 + GZ, GZ)
    edge = (gz == 0) | (gz == GZ - 1)

    def depth(d, count):
        return jnp.where(core == 0, count - 1 - d, d)

    loads = []
    for source, target in (
        (vol_in, vol_ref), (turn_in, turn_ref), (up_in, up_ref), (w1_in, w1_ref), (gather_in.at[1 - core], gather_ref),
        (b1_in, b1_ref), (b2_in, b2_ref), (w2_in, w2_ref), (spread_in, spread_ref), (chan_in, chan_ref),
    ):
        loads.append(pltpu.make_async_copy(source, target, load.at[len(loads)]))
    greeted = greet()
    for one in loads:
        one.start()
    for one in loads[:3]:
        one.wait()

    for d in range(4):
        flat = jnp.concatenate([vol_ref[c, depth(d, 4)] for c in range(4)], axis=0)
        own[d] = mm(turn_ref[...], flat).astype(BF16)
    for half in range(2):
        for chan in range(2):
            up_stage[:, chan * 2 + half, :] = up_ref[chan, :, half * 128 : half * 128 + 128].astype(F32)
    for one in loads[3:7]:
        one.wait()
    w1_rows[...] = jnp.zeros((128, 32), F32)
    for i in range(27):
        w1_rows[4 * i : 4 * i + 4, :] = w1_ref[i // 9, i // 3 % 3, i % 3].astype(F32)
    flat = mm_nt(one_hot(32), w1_rows[...].astype(BF16)).astype(BF16)
    for g in range(8):
        w1[g * 32 : g * 32 + 32, :] = mm_nt(flat, gather_ref[g * 256 : g * 256 + 256, :]).astype(BF16)
    b1 = column(b1_ref[...], 8)
    b2 = column(b2_ref[...], 4)
    greeted()

    copies = []

    def send_halo():
        sides = (
            (far, slice(1, 4), slice(7, 10), (1, -1, 0)),
            (near, slice(0, 3), slice(0, 3), (1, -1, 0)),
            (gz, slice(0, 4), slice(3, 7), (1, -1)),
        )
        for to, src_d, dst_d, steps in sides:
            for dy in steps:
                src_r, dst_r = {
                    -1: (slice(0, 16), slice(80, 96)),
                    0: (slice(0, 64), slice(16, 80)),
                    1: (slice(48, 64), slice(0, 16)),
                }[dy]
                copy = pltpu.make_async_remote_copy(
                    src_ref=own.at[src_d, src_r],
                    dst_ref=ext.at[dst_d, dst_r],
                    send_sem=send.at[len(copies)],
                    recv_sem=recv.at[len(copies)],
                    device_id=(to, lax.rem(gy + dy + GY, GY)),
                    device_id_type=MESH,
                )
                copy.start()
                copies.append(copy)

    up_wait = share(2, lambda j: up_stage.at[j], up_got, a_send.at[0], a_recv.at[0], 0, send_halo)
    for one in loads[7:]:
        one.wait()

    lane = lanes_of((32, 128))
    zero = jnp.zeros((32, 128), F32)
    for t in range(3):
        for r in range(4):
            for s in range(4):
                at = ((r * 3 + t) * 4 + s) * 32
                for pd in range(2):
                    here = w2_ref[depth(r - pd, 3), s, t].astype(F32) if 0 <= r - pd < 3 and s < 3 else None
                    next_ = w2_ref[depth(r - pd, 3), s - 1, t].astype(F32) if 0 <= r - pd < 3 and s > 0 else None
                    left = zero[:, :64] if here is None else here
                    right = zero[:, :64] if next_ is None else next_
                    w2[at : at + 32, pd * 128 : pd * 128 + 128] = jnp.concatenate([left, right], axis=1).astype(BF16)
    w2_turned[...] = mm_nt(one_hot(256), w2[...]).astype(BF16)

    def widen(value, targets, at):
        many, high, _ = value.shape
        flat = value.reshape(many * high, 256)
        for side in range(2):
            wide = mm(flat, spread_ref[:, side * 256 : side * 256 + 256])
            for k in range(2):
                for i, d in enumerate(targets):
                    rows[d, 2 * side + k, at : at + high] = wide[i * high : i * high + high, k * 128 : k * 128 + 128]

    def clear(deps, at):
        ext[deps, at : at + 16] = jnp.zeros((deps.stop - deps.start, 16, 256), BF16)

    def inside(d, r):
        ok = None
        if d == 3:
            ok = jnp.logical_not(edge)
        if r in (0, 9):
            side = gy > 0 if r == 0 else gy < GY - 1
            ok = side if ok is None else ok & side
        return ok

    def keep(ok, value):
        return value if ok is None else jnp.where(ok, value, 0.0)

    def layer_one(d):
        for dd in range(4):
            for dw in range(4):
                for r in range(10):
                    patch[d, dd * 64 + dw * 16 : dd * 64 + dw * 16 + 16, r * 128 : r * 128 + 128] = rows[
                        2 * d + dd, dw, 8 * r + 4 : 8 * r + 20, :
                    ].astype(BF16)
        for j in range(5):
            value = mm(w1[...], patch[d, :, j * 256 : j * 256 + 256]) + b1
            pre[d, :, j * 256 : j * 256 + 256] = value.astype(BF16)
            out = jnp.maximum(value, LEAK * value)
            cell = out[0:32]
            for g in range(1, 8):
                cell = cell + out[g * 32 : g * 32 + 32]
            cell = (cell * 0.125).astype(BF16).astype(F32)
            for k in range(2):
                r = 2 * j + k
                one = keep(inside(d, r), cell[:, k * 128 : k * 128 + 128])
                act[d, 0, r * 32 : r * 32 + 32, :] = before(one).astype(BF16)
                act[d, 1, r * 32 : r * 32 + 32, :] = one.astype(BF16)
                act[d, 2, r * 32 : r * 32 + 32, :] = after(one).astype(BF16)

    def windows(h, deps):
        sides = []
        for k in range(2):
            r = 4 * h + 2 * k
            sides.append(jnp.concatenate([act[dd, dw, r * 32 : r * 32 + 128, :] for dd in deps for dw in range(3)], axis=0))
        return jnp.concatenate(sides, axis=1)

    widen(own[...], (3, 4, 5, 6), 16)
    for copy in copies[3:]:
        copy.wait()

    @pl.when(gy == 0)
    def _():
        clear(slice(0, 7), 0)

    @pl.when(gy == GY - 1)
    def _():
        clear(slice(0, 7), 80)

    widen(ext[0:3], (2, 1, 0), 0)
    for at in (0, 80):
        widen(ext[3:7, at : at + 16], (3, 4, 5, 6), at)
    for d in range(2):
        layer_one(d)
    for h in range(2):
        seen[h] = mm(w2_turned[:, :768], windows(h, (0, 1))) + b2

    for copy in copies[:3]:
        copy.wait()

    @pl.when(gy == 0)
    def _():
        clear(slice(7, 10), 0)

    @pl.when(gy == GY - 1)
    def _():
        clear(slice(7, 10), 80)

    @pl.when(edge)
    def _():
        ext[7:10] = jnp.zeros((3, 96, 256), BF16)

    widen(ext[7:10], (9, 8, 7), 0)
    for d in range(2, 4):
        layer_one(d)

    up_wait()
    up_got[gz] = up_stage[gz]
    wide = []
    for half in range(2):
        wide.append(jnp.concatenate([up_got[:, chan * 2 + half, :] for chan in range(2)], axis=0))
    back = mm(chan_ref[...], jnp.concatenate(wide, axis=1).astype(BF16))
    lane = lanes_of((64, 128))
    grads = []
    for h in range(2):
        value = seen[h] + mm(w2_turned[:, 768:], windows(h, (2, 3)))
        seen[h] = value
        up = back[:, h * 128 : h * 128 + 128] * 0.125
        other = pltpu.roll(up, 64, 1)
        both = jnp.concatenate([jnp.where(lane < 64, up, other), jnp.where(lane < 64, other, up)], axis=1)
        weak = both * LEAK
        grad = jnp.concatenate(
            [jnp.where(value[g * 64 : g * 64 + 64] > 0, both, weak).astype(BF16) for g in range(4)], axis=0
        )
        grads.append(grad)
        if h == 0:
            full[...] = mm_nt(windows(h, range(4)), grad)
        else:
            full[...] += mm_nt(windows(h, range(4)), grad)

    lane = lanes_of((16, 128))
    for r in range(3):
        for t in range(3):
            near = []
            for s in range(4):
                a = ((r * 3 + t) * 4 + s) * 32
                b = (((r + 1) * 3 + t) * 4 + s) * 32
                near.append(full[a : a + 32, 0:128] + full[b : b + 32, 128:256])
            for s in range(3):
                low = near[s][:16] + pltpu.roll(near[s + 1][:16], 64, 1)
                high = pltpu.roll(near[s][16:], 64, 1) + near[s + 1][16:]
                at = (depth(r, 3) * 3 + s) * 3 + t
                sg[pl.ds(pl.multiple_of(at * 16, 16), 16), :] = jnp.where(lane < 64, low, high).astype(SENT)
    sg[432:512] = jnp.zeros((80, 128), SENT)
    chip, line = rank(0, gz, gy), rank(1, gz, gy)
    one_wait = share(0, lambda j: sg.at[pl.ds(pl.multiple_of(j * 32, 32), 32)], sg_one, s_send.at[0], s_recv.at[0])
    sg_one[chip] = sg[pl.ds(pl.multiple_of(chip * 32, 32), 32), :]

    lane = lanes_of((64, 128))
    pooled = []
    for h in range(2):
        value = seen[h]
        out = jnp.maximum(value, LEAK * value)
        cell = out[0:64] + out[64:128] + out[128:192] + out[192:256]
        left, right = cell[:, :128], cell[:, 128:]
        left = left + pltpu.roll(left, 64, 1)
        right = right + pltpu.roll(right, 64, 1)
        pooled.append((jnp.where(lane < 64, left, right) * 0.125).astype(BF16))
    turned = lax.dot_general(
        chan_ref[...], jnp.concatenate(pooled, axis=1), (((0,), (0,)), ((), ())), preferred_element_type=F32
    )
    for half in range(2):
        for chan in range(2):
            pool_stage[:, chan * 2 + half, :] = turned[chan * 32 : chan * 32 + 32, half * 128 : half * 128 + 128]

    for h in range(2):
        pulled = mm(w2[...], grads[h])
        for dd in range(4):
            for t in range(3):
                at = (dd * 3 + t) * 128
                for k in range(2):
                    gact[dd, t, 2 * h + k] = pulled[at : at + 128, k * 128 : k * 128 + 128]

    def layer_back(d):
        for j in range(5):
            sides = []
            for k in range(2):
                parts = []
                for t in range(3):
                    value = None
                    for r, at in ((j, k * 32), (j - 1, 64 + k * 32)):
                        if 0 <= r < 4:
                            piece = gact[d, t, r, at : at + 32, :]
                            value = piece if value is None else value + piece
                    parts.append(value)
                value = (after(parts[0]) + parts[1] + before(parts[2])) * 0.125
                sides.append(keep(inside(d, 2 * j + k), value))
            strong = jnp.concatenate(sides, axis=1)
            weak = strong * LEAK
            seen = pre[d, :, j * 256 : j * 256 + 256].astype(F32)
            grad = jnp.concatenate(
                [jnp.where(seen[g * 32 : g * 32 + 32] > 0, strong, weak).astype(BF16) for g in range(8)], axis=0
            )
            ffull[...] += mm_nt(grad, patch[d, :, j * 256 : j * 256 + 256])

    ffull[...] = jnp.zeros((256, 256), F32)
    for d in range(4):
        layer_back(d)
    flat = jnp.concatenate([ffull[g * 32 : g * 32 + 32, :] for g in range(8)], axis=1)
    pieces = []
    for _ in range(3):
        pieces.append(flat.astype(BF16))
        flat = flat - pieces[-1].astype(F32)
    total = mm(jnp.concatenate(pieces, axis=0), gather_ref[...])
    total = total[0:32] + total[32:64] + total[64:96]
    term[...] = total.astype(SENT)

    t_wait = share(0, lambda j: term, t_one, s_send.at[3], s_recv.at[3])
    t_one[chip] = term[...]
    one_wait()
    sg_part[...] = total16(sg_one).astype(SENT)
    two_wait = share(1, lambda j: sg_part, sg_two, s_send.at[1], s_recv.at[1])
    pool_wait = share(2, lambda j: pool_stage.at[j], pool_got, a_send.at[1], a_recv.at[1])
    pool_got[gz] = pool_stage[gz]
    sg_two[line] = sg_part[...]
    t_wait()
    t_part[...] = total16(t_one).astype(SENT)
    t_wait = share(1, lambda j: t_part, t_two, s_send.at[4], s_recv.at[4])
    t_two[line] = t_part[...]
    two_wait()
    sg_done[chip] = total16(sg_two).astype(SENT)
    done_wait = share(0, lambda j: sg_done.at[chip], sg_done, s_send.at[2], s_recv.at[2])
    pool_wait()
    for half in range(2):
        for chan in range(2):
            pool_out[chan, :, half * 128 : half * 128 + 128] = pool_got[:, chan * 2 + half, :].astype(BF16)
    t_wait()
    first_out[...] = total16(t_two)
    done_wait()
    second_out[...] = sg_done[...]


def finish(pool_in, first_in, second_in, pool_out, first_out, second_out):
    pool_out[...] = pool_in[...]
    turned = jnp.transpose(first_in[...])
    for i in range(27):
        first_out[i // 9, i // 3 % 3, i % 3] = turned[4 * i : 4 * i + 4, :]
        block = second_in[i // 2, (i % 2) * 16 : (i % 2) * 16 + 16, :].astype(F32)
        second_out[i // 9, i // 3 % 3, i % 3, 0:16, :] = block[:, :64]
        second_out[i // 9, i // 3 % 3, i % 3, 16:32, :] = block[:, 64:]


SENT = BF16


def on_device(volume, first_weight, first_bias, second_weight, second_bias, upstream):
    dma, mem = pltpu.SemaphoreType.DMA, pltpu.VMEM
    constants = [jnp.asarray(m()) for m in (spread_matrix, channel_matrix, turn_matrix, gather_matrix)]
    operands = [volume, first_weight, first_bias, second_weight, second_bias, upstream, *constants]
    results = pl.pallas_call(
        body,
        out_shape=[mem((2, 32, 256), BF16), mem((32, 128), F32), mem((16, 32, 128), SENT)],
        in_specs=[pl.BlockSpec(memory_space=pl.ANY)] * len(operands),
        out_specs=[VMEM] * 3,
        scratch_shapes=[
            *[mem(x.shape, x.dtype) for x in operands[:-1]], mem((2048, 128), BF16), dma((10,)), mem((2, 256, 256), F32),
            mem((4, 64, 256), BF16), mem((10, 96, 256), BF16), mem((32, 4, 128), F32), mem((32, 4, 128), F32),
            mem((32, 4, 128), F32), mem((32, 4, 128), F32),
            mem((128, 32), F32), mem((256, 256), BF16), mem((1536, 256), BF16), mem((256, 1536), BF16),
            mem((10, 4, 96, 128), F32), mem((4, 256, 1280), BF16), mem((4, 256, 1280), BF16), mem((4, 3, 320, 128), BF16),
            mem((1536, 256), F32), mem((4, 3, 4, 128, 128), F32), mem((256, 256), F32),
            mem((512, 128), SENT), mem((16, 32, 128), SENT), mem((32, 128), SENT), mem((16, 32, 128), SENT),
            mem((16, 32, 128), SENT), mem((32, 128), SENT), mem((16, 32, 128), SENT), mem((32, 128), SENT),
            mem((16, 32, 128), SENT),
            dma((8,)), dma((8,)), dma((2,)), dma((2,)), dma((5,)), dma((5,)),
        ],
        compiler_params=pltpu.CompilerParams(vmem_limit_bytes=LIMIT, has_side_effects=True, collective_id=1),
    )(*operands)
    return pl.pallas_call(
        finish,
        out_shape=[
            jax.ShapeDtypeStruct((2, 32, 256), BF16),
            jax.ShapeDtypeStruct((3, 3, 3, 4, 32), F32),
            jax.ShapeDtypeStruct((3, 3, 3, 32, 64), F32),
        ],
        in_specs=[VMEM] * 3,
        out_specs=[VMEM] * 3,
    )(*[pltpu.with_memory_space_constraint(x, pltpu.VMEM) for x in results])


def solution(mesh):
    placed = (P(None, "gz", "gy", None), P(), P(), P(), P(), P("gz", None, "gy"))
    return jax.shard_map(
        on_device,
        mesh=mesh,
        in_specs=placed,
        out_specs=(P("gz", None, "gy"), P(), P()),
        check_vma=False,
    )
```

```python
import jax
import jax.numpy as jnp
import numpy as np
from jax import lax
from jax.experimental import pallas as pl
from jax.experimental.pallas import tpu as pltpu
from jax.sharding import PartitionSpec as P

LEAK = 0.3
F32 = jnp.float32
BF16 = jnp.bfloat16
MESH = pl.DeviceIdType.MESH
VMEM = pl.BlockSpec(memory_space=pltpu.VMEM)
GZ, GY = 32, 8
LIMIT = 56 * 2**20


def lanes_of(shape):
    return lax.broadcasted_iota(jnp.int32, shape, len(shape) - 1)


def before(x):
    lane = lanes_of(x.shape)
    return jnp.where(lane >= 64, pltpu.roll(x, 64, 1), jnp.where(lane == 0, 0.0, pltpu.roll(x, 65, 1)))


def after(x):
    lane = lanes_of(x.shape)
    return jnp.where(lane < 64, pltpu.roll(x, 64, 1), jnp.where(lane == 127, 0.0, pltpu.roll(x, 63, 1)))


def mm(a, b):
    return jnp.dot(a, b, preferred_element_type=F32)


def mm_nt(a, b):
    return lax.dot_general(a, b, (((1,), (1,)), ((), ())), preferred_element_type=F32)


def eye(n):
    return lax.broadcasted_iota(jnp.int32, (n, n), 0) == lax.broadcasted_iota(jnp.int32, (n, n), 1)


def one_hot(n):
    return jnp.where(eye(n), 1.0, 0.0).astype(BF16)


def column(row, times):
    n = row.shape[0]
    wide = jnp.broadcast_to(row[None, :], (n, n))
    once = jnp.sum(jnp.where(eye(n), wide, 0.0), axis=1, keepdims=True)
    return jnp.concatenate([once] * times, axis=0)


def place():
    return lax.axis_index("gz"), lax.axis_index("gy")


def spread_matrix():
    out = np.zeros((256, 4, 128), np.float32)
    for lane in range(128):
        cell = 2 * (lane % 64) + lane // 64
        for dw in range(4):
            w = 2 * cell + dw - 1
            if 0 <= w < 256:
                out[w, dw, lane] = 1
    return out.reshape(256, 512).astype(jnp.bfloat16)


def channel_matrix():
    out = np.zeros((64, 64), np.float32)
    for q in range(64):
        out[q, (q % 2) * 32 + q // 2] = 1
    return out.astype(jnp.bfloat16)


def turn_matrix():
    out = np.zeros((64, 64), np.float32)
    for r in range(16):
        for c in range(4):
            out[r * 4 + c, c * 16 + r] = 1
    return out.astype(jnp.bfloat16)


def gather_matrix():
    out = np.zeros((2, 2, 2, 4, 4, 4, 4, 128), np.float32)
    for pd in range(2):
        for pr in range(2):
            for pw in range(2):
                for r in range(3):
                    for s in range(3):
                        for t in range(3):
                            for c in range(4):
                                out[pd, pr, pw, pd + r, pw + t, pr + s, c, ((r * 3 + s) * 3 + t) * 4 + c] = 1
    out = out.reshape(2048, 128)
    mirrored = np.zeros_like(out)
    for r in range(3):
        mirrored[:, r * 36 : r * 36 + 36] = out[:, (2 - r) * 36 : (2 - r) * 36 + 36]
    return np.stack([out, mirrored]).astype(jnp.bfloat16)


def around(dz, dy):
    gz, gy = place()
    return lax.rem(gz + dz + GZ, GZ), lax.rem(gy + dy + GY, GY)


def hops(offset):
    x, y, z, core = offset
    return min(x, 4 - x) + min(y, 4 - y) + min(z, 8 - z) + 0.5 * core


def spread_order(kind):
    xs, ys, zs, cores = (range(n) for n in ((4, 4, 1, 1), (1, 1, 8, 2), (4, 4, 1, 2))[kind])
    all_ = [(x, y, z, c) for x in xs for y in ys for z in zs for c in cores]
    return sorted([o for o in all_ if any(o)], key=lambda o: -hops(o))


def shifted(offset):
    gz, gy = place()
    x, y, core = gz // 8, lax.rem(gz // 2, 4), lax.rem(gz, 2)
    dx, dy, dz, dc = offset
    x = lax.rem(x + dx, 4) if dx else x
    y = lax.rem(y + dy, 4) if dy else y
    core = 1 - core if dc else core
    return x * 8 + y * 2 + core, lax.rem(gy + dz, GY) if dz else gy


def rank(kind, gz, gy):
    return (gz // 2, gy * 2 + lax.rem(gz, 2), gz)[kind]


COUNT = (16, 16, 32)


def share(kind, source, landing, send, recv, after=0, then=None):
    gz, gy = place()
    slot = rank(kind, gz, gy)
    for number, offset in enumerate(spread_order(kind)):
        if then is not None and number == after:
            then()
        to = shifted(offset)
        pltpu.make_async_remote_copy(
            src_ref=source(rank(kind, *to)),
            dst_ref=landing.at[slot],
            send_sem=send,
            recv_sem=recv,
            device_id=to,
            device_id_type=MESH,
        ).start()

    def wait():
        pltpu.make_async_remote_copy(
            src_ref=landing.at[pl.ds(0, COUNT[kind] - 1)],
            dst_ref=landing.at[pl.ds(0, COUNT[kind] - 1)],
            send_sem=send,
            recv_sem=recv,
            device_id=around(1, 0),
            device_id_type=MESH,
        ).wait()

    return wait


def greet():
    gz, gy = place()
    barrier = pltpu.get_barrier_semaphore()

    def tell(to):
        pl.semaphore_signal(barrier, inc=1, device_id=to, device_id_type=MESH)

    far = lax.rem(gz + 2 * lax.rem(gz, 2) - 1 + GZ, GZ)
    tell((far, lax.rem(gy + 1, GY)))
    tell((far, lax.rem(gy + GY - 1, GY)))
    offsets = [o for o in spread_order(1) if o[2]] + spread_order(2)
    for offset in sorted(offsets, key=lambda o: -hops(o)):
        tell(shifted(offset))

    def wait():
        pl.semaphore_wait(barrier, 47)

    return wait


def total16(landing):
    value = landing[0].astype(F32)
    for k in range(1, 16):
        value = value + landing[k].astype(F32)
    return value


def body(
    vol_in, w1_in, b1_in, w2_in, b2_in, up_in, spread_in, chan_in, turn_in, gather_in,
    pool_out, first_out, second_out,
    vol_ref, w1_ref, b1_ref, w2_ref, b2_ref, up_ref, spread_ref, chan_ref, turn_ref, gather_ref, load, seen,
    own, ext, up_stage, up_got, pool_stage, pool_got,
    w1_rows, w1, w2, w2_turned, rows, patch, pre, act, full, gact, ffull,
    sg, sg_one, sg_part, sg_two, sg_done, term, t_one, t_part, t_two,
    send, recv, a_send, a_recv, s_send, s_recv,
):
    gz, gy = place()
    core = lax.rem(gz, 2)
    near, far = gz + 1 - 2 * core, lax.rem(gz + 2 * core - 1 + GZ, GZ)
    edge = (gz == 0) | (gz == GZ - 1)

    def depth(d, count):
        return jnp.where(core == 0, count - 1 - d, d)

    loads = []
    for source, target in (
        (vol_in, vol_ref), (turn_in, turn_ref), (up_in, up_ref), (w1_in, w1_ref), (gather_in.at[1 - core], gather_ref),
        (b1_in, b1_ref), (b2_in, b2_ref), (w2_in, w2_ref), (spread_in, spread_ref), (chan_in, chan_ref),
    ):
        loads.append(pltpu.make_async_copy(source, target, load.at[len(loads)]))
    greeted = greet()
    for one in loads:
        one.start()
    for one in loads[:3]:
        one.wait()

    for d in range(4):
        flat = jnp.concatenate([vol_ref[c, depth(d, 4)] for c in range(4)], axis=0)
        own[d] = mm(turn_ref[...], flat).astype(BF16)
    for half in range(2):
        for chan in range(2):
            up_stage[:, chan * 2 + half, :] = up_ref[chan, :, half * 128 : half * 128 + 128].astype(F32)
    for one in loads[3:7]:
        one.wait()
    w1_rows[...] = jnp.zeros((128, 32), F32)
    for i in range(27):
        w1_rows[4 * i : 4 * i + 4, :] = w1_ref[i // 9, i // 3 % 3, i % 3].astype(F32)
    flat = mm_nt(one_hot(32), w1_rows[...].astype(BF16)).astype(BF16)
    for g in range(8):
        w1[g * 32 : g * 32 + 32, :] = mm_nt(flat, gather_ref[g * 256 : g * 256 + 256, :]).astype(BF16)
    b1 = column(b1_ref[...], 8)
    b2 = column(b2_ref[...], 4)
    greeted()

    copies = []

    def send_halo():
        sides = (
            (far, slice(1, 4), slice(7, 10), (1, -1, 0)),
            (near, slice(0, 3), slice(0, 3), (1, -1, 0)),
            (gz, slice(0, 4), slice(3, 7), (1, -1)),
        )
        for to, src_d, dst_d, steps in sides:
            for dy in steps:
                src_r, dst_r = {
                    -1: (slice(0, 16), slice(80, 96)),
                    0: (slice(0, 64), slice(16, 80)),
                    1: (slice(48, 64), slice(0, 16)),
                }[dy]
                copy = pltpu.make_async_remote_copy(
                    src_ref=own.at[src_d, src_r],
                    dst_ref=ext.at[dst_d, dst_r],
                    send_sem=send.at[len(copies)],
                    recv_sem=recv.at[len(copies)],
                    device_id=(to, lax.rem(gy + dy + GY, GY)),
                    device_id_type=MESH,
                )
                copy.start()
                copies.append(copy)

    up_wait = share(2, lambda j: up_stage.at[j], up_got, a_send.at[0], a_recv.at[0], 10, send_halo)
    for one in loads[7:]:
        one.wait()

    lane = lanes_of((32, 128))
    zero = jnp.zeros((32, 128), F32)
    for t in range(3):
        for r in range(4):
            for s in range(4):
                at = ((r * 3 + t) * 4 + s) * 32
                for pd in range(2):
                    here = w2_ref[depth(r - pd, 3), s, t].astype(F32) if 0 <= r - pd < 3 and s < 3 else None
                    next_ = w2_ref[depth(r - pd, 3), s - 1, t].astype(F32) if 0 <= r - pd < 3 and s > 0 else None
                    left = zero[:, :64] if here is None else here
                    right = zero[:, :64] if next_ is None else next_
                    w2[at : at + 32, pd * 128 : pd * 128 + 128] = jnp.concatenate([left, right], axis=1).astype(BF16)
    w2_turned[...] = mm_nt(one_hot(256), w2[...]).astype(BF16)

    def widen(value, targets, at):
        many, high, _ = value.shape
        flat = value.reshape(many * high, 256)
        for side in range(2):
            wide = mm(flat, spread_ref[:, side * 256 : side * 256 + 256])
            for k in range(2):
                for i, d in enumerate(targets):
                    rows[d, 2 * side + k, at : at + high] = wide[i * high : i * high + high, k * 128 : k * 128 + 128]

    def clear(deps, at):
        ext[deps, at : at + 16] = jnp.zeros((deps.stop - deps.start, 16, 256), BF16)

    def inside(d, r):
        ok = None
        if d == 3:
            ok = jnp.logical_not(edge)
        if r in (0, 9):
            side = gy > 0 if r == 0 else gy < GY - 1
            ok = side if ok is None else ok & side
        return ok

    def keep(ok, value):
        return value if ok is None else jnp.where(ok, value, 0.0)

    def layer_one(d):
        for dd in range(4):
            for dw in range(4):
                for r in range(10):
                    patch[d, dd * 64 + dw * 16 : dd * 64 + dw * 16 + 16, r * 128 : r * 128 + 128] = rows[
                        2 * d + dd, dw, 8 * r + 4 : 8 * r + 20, :
                    ].astype(BF16)
        for j in range(5):
            value = mm(w1[...], patch[d, :, j * 256 : j * 256 + 256]) + b1
            pre[d, :, j * 256 : j * 256 + 256] = value.astype(BF16)
            out = jnp.maximum(value, LEAK * value)
            cell = out[0:32]
            for g in range(1, 8):
                cell = cell + out[g * 32 : g * 32 + 32]
            cell = (cell * 0.125).astype(BF16).astype(F32)
            for k in range(2):
                r = 2 * j + k
                one = keep(inside(d, r), cell[:, k * 128 : k * 128 + 128])
                act[d, 0, r * 32 : r * 32 + 32, :] = before(one).astype(BF16)
                act[d, 1, r * 32 : r * 32 + 32, :] = one.astype(BF16)
                act[d, 2, r * 32 : r * 32 + 32, :] = after(one).astype(BF16)

    def windows(h, deps):
        sides = []
        for k in range(2):
            r = 4 * h + 2 * k
            sides.append(jnp.concatenate([act[dd, dw, r * 32 : r * 32 + 128, :] for dd in deps for dw in range(3)], axis=0))
        return jnp.concatenate(sides, axis=1)

    widen(own[...], (3, 4, 5, 6), 16)
    for copy in copies[3:]:
        copy.wait()

    @pl.when(gy == 0)
    def _():
        clear(slice(0, 7), 0)

    @pl.when(gy == GY - 1)
    def _():
        clear(slice(0, 7), 80)

    widen(ext[0:3], (2, 1, 0), 0)
    for at in (0, 80):
        widen(ext[3:7, at : at + 16], (3, 4, 5, 6), at)
    for d in range(2):
        layer_one(d)
    for h in range(2):
        seen[h] = mm(w2_turned[:, :768], windows(h, (0, 1))) + b2

    for copy in copies[:3]:
        copy.wait()

    @pl.when(gy == 0)
    def _():
        clear(slice(7, 10), 0)

    @pl.when(gy == GY - 1)
    def _():
        clear(slice(7, 10), 80)

    @pl.when(edge)
    def _():
        ext[7:10] = jnp.zeros((3, 96, 256), BF16)

    widen(ext[7:10], (9, 8, 7), 0)
    for d in range(2, 4):
        layer_one(d)

    up_wait()
    up_got[gz] = up_stage[gz]
    wide = []
    for half in range(2):
        wide.append(jnp.concatenate([up_got[:, chan * 2 + half, :] for chan in range(2)], axis=0))
    back = mm(chan_ref[...], jnp.concatenate(wide, axis=1).astype(BF16))
    lane = lanes_of((64, 128))
    grads = []
    for h in range(2):
        value = seen[h] + mm(w2_turned[:, 768:], windows(h, (2, 3)))
        seen[h] = value
        up = back[:, h * 128 : h * 128 + 128] * 0.125
        other = pltpu.roll(up, 64, 1)
        both = jnp.concatenate([jnp.where(lane < 64, up, other), jnp.where(lane < 64, other, up)], axis=1)
        weak = both * LEAK
        grad = jnp.concatenate(
            [jnp.where(value[g * 64 : g * 64 + 64] > 0, both, weak).astype(BF16) for g in range(4)], axis=0
        )
        grads.append(grad)
        full[h] = mm_nt(windows(h, range(4)), grad)

    lane = lanes_of((16, 128))
    for r in range(3):
        for t in range(3):
            near = []
            for s in range(4):
                a = ((r * 3 + t) * 4 + s) * 32
                b = (((r + 1) * 3 + t) * 4 + s) * 32
                near.append(
                    full[0, a : a + 32, 0:128]
                    + full[1, a : a + 32, 0:128]
                    + (full[0, b : b + 32, 128:256] + full[1, b : b + 32, 128:256])
                )
            for s in range(3):
                low = near[s][:16] + pltpu.roll(near[s + 1][:16], 64, 1)
                high = pltpu.roll(near[s][16:], 64, 1) + near[s + 1][16:]
                at = (depth(r, 3) * 3 + s) * 3 + t
                sg[pl.ds(pl.multiple_of(at * 16, 16), 16), :] = jnp.where(lane < 64, low, high).astype(SENT)
    sg[432:512] = jnp.zeros((80, 128), SENT)
    chip, line = rank(0, gz, gy), rank(1, gz, gy)
    one_wait = share(0, lambda j: sg.at[pl.ds(pl.multiple_of(j * 32, 32), 32)], sg_one, s_send.at[0], s_recv.at[0])
    sg_one[chip] = sg[pl.ds(pl.multiple_of(chip * 32, 32), 32), :]

    lane = lanes_of((64, 128))
    pooled = []
    for h in range(2):
        value = seen[h]
        out = jnp.maximum(value, LEAK * value)
        cell = out[0:64] + out[64:128] + out[128:192] + out[192:256]
        left, right = cell[:, :128], cell[:, 128:]
        left = left + pltpu.roll(left, 64, 1)
        right = right + pltpu.roll(right, 64, 1)
        pooled.append((jnp.where(lane < 64, left, right) * 0.125).astype(BF16))
    turned = lax.dot_general(
        chan_ref[...], jnp.concatenate(pooled, axis=1), (((0,), (0,)), ((), ())), preferred_element_type=F32
    )
    for half in range(2):
        for chan in range(2):
            pool_stage[:, chan * 2 + half, :] = turned[chan * 32 : chan * 32 + 32, half * 128 : half * 128 + 128]

    for h in range(2):
        pulled = mm(w2[...], grads[h])
        for dd in range(4):
            for t in range(3):
                at = (dd * 3 + t) * 128
                for k in range(2):
                    gact[dd, t, 2 * h + k] = pulled[at : at + 128, k * 128 : k * 128 + 128]

    def layer_back(d):
        for j in range(5):
            sides = []
            for k in range(2):
                parts = []
                for t in range(3):
                    value = None
                    for r, at in ((j, k * 32), (j - 1, 64 + k * 32)):
                        if 0 <= r < 4:
                            piece = gact[d, t, r, at : at + 32, :]
                            value = piece if value is None else value + piece
                    parts.append(value)
                value = (after(parts[0]) + parts[1] + before(parts[2])) * 0.125
                sides.append(keep(inside(d, 2 * j + k), value))
            strong = jnp.concatenate(sides, axis=1)
            weak = strong * LEAK
            seen = pre[d, :, j * 256 : j * 256 + 256].astype(F32)
            grad = jnp.concatenate(
                [jnp.where(seen[g * 32 : g * 32 + 32] > 0, strong, weak).astype(BF16) for g in range(8)], axis=0
            )
            ffull[...] += mm_nt(grad, patch[d, :, j * 256 : j * 256 + 256])

    ffull[...] = jnp.zeros((256, 256), F32)
    for d in range(4):
        layer_back(d)
    flat = jnp.concatenate([ffull[g * 32 : g * 32 + 32, :] for g in range(8)], axis=1)
    pieces = []
    for _ in range(3):
        pieces.append(flat.astype(BF16))
        flat = flat - pieces[-1].astype(F32)
    total = mm(jnp.concatenate(pieces, axis=0), gather_ref[...])
    total = total[0:32] + total[32:64] + total[64:96]
    term[...] = total.astype(SENT)

    t_wait = share(0, lambda j: term, t_one, s_send.at[3], s_recv.at[3])
    t_one[chip] = term[...]
    one_wait()
    sg_part[...] = total16(sg_one).astype(SENT)
    two_wait = share(1, lambda j: sg_part, sg_two, s_send.at[1], s_recv.at[1])
    pool_wait = share(2, lambda j: pool_stage.at[j], pool_got, a_send.at[1], a_recv.at[1])
    pool_got[gz] = pool_stage[gz]
    sg_two[line] = sg_part[...]
    t_wait()
    t_part[...] = total16(t_one).astype(SENT)
    t_wait = share(1, lambda j: t_part, t_two, s_send.at[4], s_recv.at[4])
    t_two[line] = t_part[...]
    two_wait()
    sg_done[chip] = total16(sg_two).astype(SENT)
    done_wait = share(0, lambda j: sg_done.at[chip], sg_done, s_send.at[2], s_recv.at[2])
    pool_wait()
    for half in range(2):
        for chan in range(2):
            pool_out[chan, :, half * 128 : half * 128 + 128] = pool_got[:, chan * 2 + half, :].astype(BF16)
    t_wait()
    first_out[...] = jnp.transpose(total16(t_two))
    done_wait()
    second_out[...] = sg_done[...]


def finish(pool_in, first_in, second_in, pool_out, first_out, second_out):
    pool_out[...] = pool_in[...]
    for i in range(27):
        first_out[i // 9, i // 3 % 3, i % 3] = first_in[4 * i : 4 * i + 4, :]
        block = second_in[i // 2, (i % 2) * 16 : (i % 2) * 16 + 16, :].astype(F32)
        second_out[i // 9, i // 3 % 3, i % 3, 0:16, :] = block[:, :64]
        second_out[i // 9, i // 3 % 3, i % 3, 16:32, :] = block[:, 64:]


SENT = BF16


def on_device(volume, first_weight, first_bias, second_weight, second_bias, upstream):
    dma, mem = pltpu.SemaphoreType.DMA, pltpu.VMEM
    constants = [jnp.asarray(m()) for m in (spread_matrix, channel_matrix, turn_matrix, gather_matrix)]
    operands = [volume, first_weight, first_bias, second_weight, second_bias, upstream, *constants]
    results = pl.pallas_call(
        body,
        out_shape=[mem((2, 32, 256), BF16), mem((128, 32), F32), mem((16, 32, 128), SENT)],
        in_specs=[pl.BlockSpec(memory_space=pl.ANY)] * len(operands),
        out_specs=[VMEM] * 3,
        scratch_shapes=[
            *[mem(x.shape, x.dtype) for x in operands[:-1]], mem((2048, 128), BF16), dma((10,)), mem((2, 256, 256), F32),
            mem((4, 64, 256), BF16), mem((10, 96, 256), BF16), mem((32, 4, 128), F32), mem((32, 4, 128), F32),
            mem((32, 4, 128), F32), mem((32, 4, 128), F32),
            mem((128, 32), F32), mem((256, 256), BF16), mem((1536, 256), BF16), mem((256, 1536), BF16),
            mem((10, 4, 96, 128), F32), mem((4, 256, 1280), BF16), mem((4, 256, 1280), BF16), mem((4, 3, 320, 128), BF16),
            mem((2, 1536, 256), F32), mem((4, 3, 4, 128, 128), F32), mem((256, 256), F32),
            mem((512, 128), SENT), mem((16, 32, 128), SENT), mem((32, 128), SENT), mem((16, 32, 128), SENT),
            mem((16, 32, 128), SENT), mem((32, 128), SENT), mem((16, 32, 128), SENT), mem((32, 128), SENT),
            mem((16, 32, 128), SENT),
            dma((8,)), dma((8,)), dma((2,)), dma((2,)), dma((5,)), dma((5,)),
        ],
        compiler_params=pltpu.CompilerParams(vmem_limit_bytes=LIMIT, has_side_effects=True, collective_id=1),
    )(*operands)
    return pl.pallas_call(
        finish,
        out_shape=[
            jax.ShapeDtypeStruct((2, 32, 256), BF16),
            jax.ShapeDtypeStruct((3, 3, 3, 4, 32), F32),
            jax.ShapeDtypeStruct((3, 3, 3, 32, 64), F32),
        ],
        in_specs=[VMEM] * 3,
        out_specs=[VMEM] * 3,
    )(*[pltpu.with_memory_space_constraint(x, pltpu.VMEM) for x in results])


def solution(mesh):
    placed = (P(None, "gz", "gy", None), P(), P(), P(), P(), P("gz", None, "gy"))
    return jax.shard_map(
        on_device,
        mesh=mesh,
        in_specs=placed,
        out_specs=(P("gz", None, "gy"), P(), P()),
        check_vma=False,
    )
```

```python
import jax
import jax.numpy as jnp
import numpy as np
from jax import lax
from jax.experimental import pallas as pl
from jax.experimental.pallas import tpu as pltpu
from jax.sharding import PartitionSpec as P

LEAK = 0.3
F32 = jnp.float32
BF16 = jnp.bfloat16
MESH = pl.DeviceIdType.MESH
VMEM = pl.BlockSpec(memory_space=pltpu.VMEM)
GZ, GY = 32, 8
LIMIT = 56 * 2**20


def lanes_of(shape):
    return lax.broadcasted_iota(jnp.int32, shape, len(shape) - 1)


def before(x):
    lane = lanes_of(x.shape)
    return jnp.where(lane >= 64, pltpu.roll(x, 64, 1), jnp.where(lane == 0, 0.0, pltpu.roll(x, 65, 1)))


def after(x):
    lane = lanes_of(x.shape)
    return jnp.where(lane < 64, pltpu.roll(x, 64, 1), jnp.where(lane == 127, 0.0, pltpu.roll(x, 63, 1)))


def mm(a, b):
    return jnp.dot(a, b, preferred_element_type=F32)


def mm_nt(a, b):
    return lax.dot_general(a, b, (((1,), (1,)), ((), ())), preferred_element_type=F32)


def eye(n):
    return lax.broadcasted_iota(jnp.int32, (n, n), 0) == lax.broadcasted_iota(jnp.int32, (n, n), 1)


def one_hot(n):
    return jnp.where(eye(n), 1.0, 0.0).astype(BF16)


def column(row, times):
    n = row.shape[0]
    wide = jnp.broadcast_to(row[None, :], (n, n))
    once = jnp.sum(jnp.where(eye(n), wide, 0.0), axis=1, keepdims=True)
    return jnp.concatenate([once] * times, axis=0)


def place():
    return lax.axis_index("gz"), lax.axis_index("gy")


def spread_matrix():
    out = np.zeros((256, 4, 128), np.float32)
    for lane in range(128):
        cell = 2 * (lane % 64) + lane // 64
        for dw in range(4):
            w = 2 * cell + dw - 1
            if 0 <= w < 256:
                out[w, dw, lane] = 1
    return out.reshape(256, 512).astype(jnp.bfloat16)


def channel_matrix():
    out = np.zeros((64, 64), np.float32)
    for q in range(64):
        out[q, (q % 2) * 32 + q // 2] = 1
    return out.astype(jnp.bfloat16)


def turn_matrix():
    out = np.zeros((64, 64), np.float32)
    for r in range(16):
        for c in range(4):
            out[r * 4 + c, c * 16 + r] = 1
    return out.astype(jnp.bfloat16)


def gather_matrix():
    out = np.zeros((2, 2, 2, 4, 4, 4, 4, 128), np.float32)
    for pd in range(2):
        for pr in range(2):
            for pw in range(2):
                for r in range(3):
                    for s in range(3):
                        for t in range(3):
                            for c in range(4):
                                out[pd, pr, pw, pd + r, pw + t, pr + s, c, ((r * 3 + s) * 3 + t) * 4 + c] = 1
    out = out.reshape(2048, 128)
    mirrored = np.zeros_like(out)
    for r in range(3):
        mirrored[:, r * 36 : r * 36 + 36] = out[:, (2 - r) * 36 : (2 - r) * 36 + 36]
    return np.stack([out, mirrored]).astype(jnp.bfloat16)


def around(dz, dy):
    gz, gy = place()
    return lax.rem(gz + dz + GZ, GZ), lax.rem(gy + dy + GY, GY)


def hops(offset):
    x, y, z, core = offset
    return min(x, 4 - x) + min(y, 4 - y) + min(z, 8 - z) + 0.5 * core


def spread_order(kind):
    xs, ys, zs, cores = (range(n) for n in ((4, 4, 1, 1), (1, 1, 8, 2), (4, 4, 1, 2))[kind])
    all_ = [(x, y, z, c) for x in xs for y in ys for z in zs for c in cores]
    return sorted([o for o in all_ if any(o)], key=lambda o: -hops(o))


def shifted(offset):
    gz, gy = place()
    x, y, core = gz // 8, lax.rem(gz // 2, 4), lax.rem(gz, 2)
    dx, dy, dz, dc = offset
    x = lax.rem(x + dx, 4) if dx else x
    y = lax.rem(y + dy, 4) if dy else y
    core = 1 - core if dc else core
    return x * 8 + y * 2 + core, lax.rem(gy + dz, GY) if dz else gy


def rank(kind, gz, gy):
    return (gz // 2, gy * 2 + lax.rem(gz, 2), gz)[kind]


COUNT = (16, 16, 32)


def share(kind, source, landing, send, recv, after=0, then=None):
    gz, gy = place()
    slot = rank(kind, gz, gy)
    for number, offset in enumerate(spread_order(kind)):
        if then is not None and number == after:
            then()
        to = shifted(offset)
        pltpu.make_async_remote_copy(
            src_ref=source(rank(kind, *to)),
            dst_ref=landing.at[slot],
            send_sem=send,
            recv_sem=recv,
            device_id=to,
            device_id_type=MESH,
        ).start()

    def wait():
        pltpu.make_async_remote_copy(
            src_ref=landing.at[pl.ds(0, COUNT[kind] - 1)],
            dst_ref=landing.at[pl.ds(0, COUNT[kind] - 1)],
            send_sem=send,
            recv_sem=recv,
            device_id=around(1, 0),
            device_id_type=MESH,
        ).wait()

    return wait


def greet():
    gz, gy = place()
    barrier = pltpu.get_barrier_semaphore()

    def tell(to):
        pl.semaphore_signal(barrier, inc=1, device_id=to, device_id_type=MESH)

    far = lax.rem(gz + 2 * lax.rem(gz, 2) - 1 + GZ, GZ)
    tell((far, lax.rem(gy + 1, GY)))
    tell((far, lax.rem(gy + GY - 1, GY)))
    offsets = [o for o in spread_order(1) if o[2]] + spread_order(2)
    for offset in sorted(offsets, key=lambda o: -hops(o)):
        tell(shifted(offset))

    def wait():
        pl.semaphore_wait(barrier, 47)

    return wait


def total16(landing):
    value = landing[0].astype(F32)
    for k in range(1, 16):
        value = value + landing[k].astype(F32)
    return value


def body(
    vol_in, w1_in, b1_in, w2_in, b2_in, up_in, spread_in, chan_in, turn_in, gather_in,
    pool_out, first_out, second_out,
    vol_ref, w1_ref, b1_ref, w2_ref, b2_ref, up_ref, spread_ref, chan_ref, turn_ref, gather_ref, load, seen,
    own, ext, up_stage, up_got, pool_stage, pool_got,
    w1_rows, w1, w2, w2_turned, rows, patch, pre, act, full, gact, ffull,
    sg, sg_one, sg_part, sg_two, sg_done, term, t_one, t_part, t_two,
    send, recv, a_send, a_recv, s_send, s_recv,
):
    gz, gy = place()
    core = lax.rem(gz, 2)
    near, far = gz + 1 - 2 * core, lax.rem(gz + 2 * core - 1 + GZ, GZ)
    edge = (gz == 0) | (gz == GZ - 1)

    def depth(d, count):
        return jnp.where(core == 0, count - 1 - d, d)

    loads = []
    for source, target in (
        (vol_in, vol_ref), (turn_in, turn_ref), (up_in, up_ref), (w1_in, w1_ref), (gather_in.at[1 - core], gather_ref),
        (b1_in, b1_ref), (b2_in, b2_ref), (w2_in, w2_ref), (spread_in, spread_ref), (chan_in, chan_ref),
    ):
        loads.append(pltpu.make_async_copy(source, target, load.at[len(loads)]))
    greeted = greet()
    for one in loads:
        one.start()
    for one in loads[:3]:
        one.wait()

    for d in range(4):
        flat = jnp.concatenate([vol_ref[c, depth(d, 4)] for c in range(4)], axis=0)
        own[d] = mm(turn_ref[...], flat).astype(BF16)
    for half in range(2):
        for chan in range(2):
            up_stage[:, chan * 2 + half, :] = up_ref[chan, :, half * 128 : half * 128 + 128].astype(F32)
    for one in loads[3:7]:
        one.wait()
    w1_rows[...] = jnp.zeros((128, 32), F32)
    for i in range(27):
        w1_rows[4 * i : 4 * i + 4, :] = w1_ref[i // 9, i // 3 % 3, i % 3].astype(F32)
    flat = mm_nt(one_hot(32), w1_rows[...].astype(BF16)).astype(BF16)
    for g in range(8):
        w1[g * 32 : g * 32 + 32, :] = mm_nt(flat, gather_ref[g * 256 : g * 256 + 256, :]).astype(BF16)
    b1 = column(b1_ref[...], 8)
    b2 = column(b2_ref[...], 4)
    greeted()

    copies = []

    def send_halo():
        sides = (
            (far, slice(1, 4), slice(7, 10), (0, 1, -1)),
            (near, slice(0, 3), slice(0, 3), (1, -1, 0)),
            (gz, slice(0, 4), slice(3, 7), (1, -1)),
        )
        for to, src_d, dst_d, steps in sides:
            for dy in steps:
                src_r, dst_r = {
                    -1: (slice(0, 16), slice(80, 96)),
                    0: (slice(0, 64), slice(16, 80)),
                    1: (slice(48, 64), slice(0, 16)),
                }[dy]
                copy = pltpu.make_async_remote_copy(
                    src_ref=own.at[src_d, src_r],
                    dst_ref=ext.at[dst_d, dst_r],
                    send_sem=send.at[len(copies)],
                    recv_sem=recv.at[len(copies)],
                    device_id=(to, lax.rem(gy + dy + GY, GY)),
                    device_id_type=MESH,
                )
                copy.start()
                copies.append(copy)

    up_wait = share(2, lambda j: up_stage.at[j], up_got, a_send.at[0], a_recv.at[0], 10, send_halo)
    for one in loads[7:]:
        one.wait()

    lane = lanes_of((32, 128))
    zero = jnp.zeros((32, 128), F32)
    for t in range(3):
        for r in range(4):
            for s in range(4):
                at = ((r * 3 + t) * 4 + s) * 32
                for pd in range(2):
                    here = w2_ref[depth(r - pd, 3), s, t].astype(F32) if 0 <= r - pd < 3 and s < 3 else None
                    next_ = w2_ref[depth(r - pd, 3), s - 1, t].astype(F32) if 0 <= r - pd < 3 and s > 0 else None
                    left = zero[:, :64] if here is None else here
                    right = zero[:, :64] if next_ is None else next_
                    w2[at : at + 32, pd * 128 : pd * 128 + 128] = jnp.concatenate([left, right], axis=1).astype(BF16)
    w2_turned[...] = mm_nt(one_hot(256), w2[...]).astype(BF16)

    def widen(value, targets, at):
        many, high, _ = value.shape
        flat = value.reshape(many * high, 256)
        for side in range(2):
            wide = mm(flat, spread_ref[:, side * 256 : side * 256 + 256])
            for k in range(2):
                for i, d in enumerate(targets):
                    rows[d, 2 * side + k, at : at + high] = wide[i * high : i * high + high, k * 128 : k * 128 + 128]

    def clear(deps, at):
        ext[deps, at : at + 16] = jnp.zeros((deps.stop - deps.start, 16, 256), BF16)

    def inside(d, r):
        ok = None
        if d == 3:
            ok = jnp.logical_not(edge)
        if r in (0, 9):
            side = gy > 0 if r == 0 else gy < GY - 1
            ok = side if ok is None else ok & side
        return ok

    def keep(ok, value):
        return value if ok is None else jnp.where(ok, value, 0.0)

    def layer_one(d):
        for dd in range(4):
            for dw in range(4):
                for r in range(10):
                    patch[d, dd * 64 + dw * 16 : dd * 64 + dw * 16 + 16, r * 128 : r * 128 + 128] = rows[
                        2 * d + dd, dw, 8 * r + 4 : 8 * r + 20, :
                    ].astype(BF16)
        for j in range(5):
            value = mm(w1[...], patch[d, :, j * 256 : j * 256 + 256]) + b1
            pre[d, :, j * 256 : j * 256 + 256] = value.astype(BF16)
            out = jnp.maximum(value, LEAK * value)
            cell = out[0:32]
            for g in range(1, 8):
                cell = cell + out[g * 32 : g * 32 + 32]
            cell = (cell * 0.125).astype(BF16).astype(F32)
            for k in range(2):
                r = 2 * j + k
                one = keep(inside(d, r), cell[:, k * 128 : k * 128 + 128])
                act[d, 0, r * 32 : r * 32 + 32, :] = before(one).astype(BF16)
                act[d, 1, r * 32 : r * 32 + 32, :] = one.astype(BF16)
                act[d, 2, r * 32 : r * 32 + 32, :] = after(one).astype(BF16)

    def windows(h, deps):
        sides = []
        for k in range(2):
            r = 4 * h + 2 * k
            sides.append(jnp.concatenate([act[dd, dw, r * 32 : r * 32 + 128, :] for dd in deps for dw in range(3)], axis=0))
        return jnp.concatenate(sides, axis=1)

    widen(own[...], (3, 4, 5, 6), 16)
    for copy in copies[3:]:
        copy.wait_recv()

    @pl.when(gy == 0)
    def _():
        clear(slice(0, 7), 0)

    @pl.when(gy == GY - 1)
    def _():
        clear(slice(0, 7), 80)

    widen(ext[0:3], (2, 1, 0), 0)
    for at in (0, 80):
        widen(ext[3:7, at : at + 16], (3, 4, 5, 6), at)
    for d in range(2):
        layer_one(d)
    for h in range(2):
        seen[h] = mm(w2_turned[:, :768], windows(h, (0, 1))) + b2

    for copy in copies[:3]:
        copy.wait_recv()

    @pl.when(gy == 0)
    def _():
        clear(slice(7, 10), 0)

    @pl.when(gy == GY - 1)
    def _():
        clear(slice(7, 10), 80)

    @pl.when(edge)
    def _():
        ext[7:10] = jnp.zeros((3, 96, 256), BF16)

    widen(ext[7:10], (9, 8, 7), 0)
    for d in range(2, 4):
        layer_one(d)

    up_wait()
    up_got[gz] = up_stage[gz]
    wide = []
    for half in range(2):
        wide.append(jnp.concatenate([up_got[:, chan * 2 + half, :] for chan in range(2)], axis=0))
    back = mm(chan_ref[...], jnp.concatenate(wide, axis=1).astype(BF16))
    lane = lanes_of((64, 128))
    grads = []
    for h in range(2):
        value = seen[h] + mm(w2_turned[:, 768:], windows(h, (2, 3)))
        seen[h] = value
        up = back[:, h * 128 : h * 128 + 128] * 0.125
        other = pltpu.roll(up, 64, 1)
        both = jnp.concatenate([jnp.where(lane < 64, up, other), jnp.where(lane < 64, other, up)], axis=1)
        weak = both * LEAK
        grad = jnp.concatenate(
            [jnp.where(value[g * 64 : g * 64 + 64] > 0, both, weak).astype(BF16) for g in range(4)], axis=0
        )
        grads.append(grad)
        full[h] = mm_nt(windows(h, range(4)), grad)

    lane = lanes_of((16, 128))
    for r in range(3):
        for t in range(3):
            near = []
            for s in range(4):
                a = ((r * 3 + t) * 4 + s) * 32
                b = (((r + 1) * 3 + t) * 4 + s) * 32
                near.append(
                    full[0, a : a + 32, 0:128]
                    + full[1, a : a + 32, 0:128]
                    + (full[0, b : b + 32, 128:256] + full[1, b : b + 32, 128:256])
                )
            for s in range(3):
                low = near[s][:16] + pltpu.roll(near[s + 1][:16], 64, 1)
                high = pltpu.roll(near[s][16:], 64, 1) + near[s + 1][16:]
                at = (depth(r, 3) * 3 + s) * 3 + t
                sg[pl.ds(pl.multiple_of(at * 16, 16), 16), :] = jnp.where(lane < 64, low, high).astype(SENT)
    sg[432:512] = jnp.zeros((80, 128), SENT)
    chip, line = rank(0, gz, gy), rank(1, gz, gy)
    one_wait = share(0, lambda j: sg.at[pl.ds(pl.multiple_of(j * 32, 32), 32)], sg_one, s_send.at[0], s_recv.at[0])
    sg_one[chip] = sg[pl.ds(pl.multiple_of(chip * 32, 32), 32), :]

    lane = lanes_of((64, 128))
    pooled = []
    for h in range(2):
        value = seen[h]
        out = jnp.maximum(value, LEAK * value)
        cell = out[0:64] + out[64:128] + out[128:192] + out[192:256]
        left, right = cell[:, :128], cell[:, 128:]
        left = left + pltpu.roll(left, 64, 1)
        right = right + pltpu.roll(right, 64, 1)
        pooled.append((jnp.where(lane < 64, left, right) * 0.125).astype(BF16))
    turned = lax.dot_general(
        chan_ref[...], jnp.concatenate(pooled, axis=1), (((0,), (0,)), ((), ())), preferred_element_type=F32
    )
    for half in range(2):
        for chan in range(2):
            pool_stage[:, chan * 2 + half, :] = turned[chan * 32 : chan * 32 + 32, half * 128 : half * 128 + 128]

    for h in range(2):
        pulled = mm(w2[...], grads[h])
        for dd in range(4):
            for t in range(3):
                at = (dd * 3 + t) * 128
                for k in range(2):
                    gact[dd, t, 2 * h + k] = pulled[at : at + 128, k * 128 : k * 128 + 128]

    def layer_back(d):
        for j in range(5):
            sides = []
            for k in range(2):
                parts = []
                for t in range(3):
                    value = None
                    for r, at in ((j, k * 32), (j - 1, 64 + k * 32)):
                        if 0 <= r < 4:
                            piece = gact[d, t, r, at : at + 32, :]
                            value = piece if value is None else value + piece
                    parts.append(value)
                value = (after(parts[0]) + parts[1] + before(parts[2])) * 0.125
                sides.append(keep(inside(d, 2 * j + k), value))
            strong = jnp.concatenate(sides, axis=1)
            weak = strong * LEAK
            seen = pre[d, :, j * 256 : j * 256 + 256].astype(F32)
            grad = jnp.concatenate(
                [jnp.where(seen[g * 32 : g * 32 + 32] > 0, strong, weak).astype(BF16) for g in range(8)], axis=0
            )
            ffull[...] += mm_nt(grad, patch[d, :, j * 256 : j * 256 + 256])

    ffull[...] = jnp.zeros((256, 256), F32)
    for d in range(4):
        layer_back(d)
    flat = jnp.concatenate([ffull[g * 32 : g * 32 + 32, :] for g in range(8)], axis=1)
    pieces = []
    for _ in range(3):
        pieces.append(flat.astype(BF16))
        flat = flat - pieces[-1].astype(F32)
    total = mm(jnp.concatenate(pieces, axis=0), gather_ref[...])
    total = total[0:32] + total[32:64] + total[64:96]
    term[...] = total.astype(SENT)

    t_wait = share(0, lambda j: term, t_one, s_send.at[3], s_recv.at[3])
    t_one[chip] = term[...]
    one_wait()
    sg_part[...] = total16(sg_one).astype(SENT)
    two_wait = share(1, lambda j: sg_part, sg_two, s_send.at[1], s_recv.at[1])
    pool_wait = share(2, lambda j: pool_stage.at[j], pool_got, a_send.at[1], a_recv.at[1])
    pool_got[gz] = pool_stage[gz]
    sg_two[line] = sg_part[...]
    t_wait()
    t_part[...] = total16(t_one).astype(SENT)
    t_wait = share(1, lambda j: t_part, t_two, s_send.at[4], s_recv.at[4])
    t_two[line] = t_part[...]
    two_wait()
    sg_done[chip] = total16(sg_two).astype(SENT)
    done_wait = share(0, lambda j: sg_done.at[chip], sg_done, s_send.at[2], s_recv.at[2])
    pool_wait()
    for copy in copies:
        copy.wait_send()
    for half in range(2):
        for chan in range(2):
            pool_out[chan, :, half * 128 : half * 128 + 128] = pool_got[:, chan * 2 + half, :].astype(BF16)
    t_wait()
    first_out[...] = jnp.transpose(total16(t_two))
    done_wait()
    second_out[...] = sg_done[...]


def finish(pool_in, first_in, second_in, pool_out, first_out, second_out):
    pool_out[...] = pool_in[...]
    for i in range(27):
        first_out[i // 9, i // 3 % 3, i % 3] = first_in[4 * i : 4 * i + 4, :]
        block = second_in[i // 2, (i % 2) * 16 : (i % 2) * 16 + 16, :].astype(F32)
        second_out[i // 9, i // 3 % 3, i % 3, 0:16, :] = block[:, :64]
        second_out[i // 9, i // 3 % 3, i % 3, 16:32, :] = block[:, 64:]


SENT = BF16


def on_device(volume, first_weight, first_bias, second_weight, second_bias, upstream):
    dma, mem = pltpu.SemaphoreType.DMA, pltpu.VMEM
    constants = [jnp.asarray(m()) for m in (spread_matrix, channel_matrix, turn_matrix, gather_matrix)]
    operands = [volume, first_weight, first_bias, second_weight, second_bias, upstream, *constants]
    results = pl.pallas_call(
        body,
        out_shape=[mem((2, 32, 256), BF16), mem((128, 32), F32), mem((16, 32, 128), SENT)],
        in_specs=[pl.BlockSpec(memory_space=pl.ANY)] * len(operands),
        out_specs=[VMEM] * 3,
        scratch_shapes=[
            *[mem(x.shape, x.dtype) for x in operands[:-1]], mem((2048, 128), BF16), dma((10,)), mem((2, 256, 256), F32),
            mem((4, 64, 256), BF16), mem((10, 96, 256), BF16), mem((32, 4, 128), F32), mem((32, 4, 128), F32),
            mem((32, 4, 128), F32), mem((32, 4, 128), F32),
            mem((128, 32), F32), mem((256, 256), BF16), mem((1536, 256), BF16), mem((256, 1536), BF16),
            mem((10, 4, 96, 128), F32), mem((4, 256, 1280), BF16), mem((4, 256, 1280), BF16), mem((4, 3, 320, 128), BF16),
            mem((2, 1536, 256), F32), mem((4, 3, 4, 128, 128), F32), mem((256, 256), F32),
            mem((512, 128), SENT), mem((16, 32, 128), SENT), mem((32, 128), SENT), mem((16, 32, 128), SENT),
            mem((16, 32, 128), SENT), mem((32, 128), SENT), mem((16, 32, 128), SENT), mem((32, 128), SENT),
            mem((16, 32, 128), SENT),
            dma((8,)), dma((8,)), dma((2,)), dma((2,)), dma((5,)), dma((5,)),
        ],
        compiler_params=pltpu.CompilerParams(vmem_limit_bytes=LIMIT, has_side_effects=True, collective_id=1),
    )(*operands)
    return pl.pallas_call(
        finish,
        out_shape=[
            jax.ShapeDtypeStruct((2, 32, 256), BF16),
            jax.ShapeDtypeStruct((3, 3, 3, 4, 32), F32),
            jax.ShapeDtypeStruct((3, 3, 3, 32, 64), F32),
        ],
        in_specs=[VMEM] * 3,
        out_specs=[VMEM] * 3,
    )(*[pltpu.with_memory_space_constraint(x, pltpu.VMEM) for x in results])


def solution(mesh):
    placed = (P(None, "gz", "gy", None), P(), P(), P(), P(), P("gz", None, "gy"))
    return jax.shard_map(
        on_device,
        mesh=mesh,
        in_specs=placed,
        out_specs=(P("gz", None, "gy"), P(), P()),
        check_vma=False,
    )
```

```python
import jax
import jax.numpy as jnp
import numpy as np
from jax import lax
from jax.experimental import pallas as pl
from jax.experimental.pallas import tpu as pltpu
from jax.sharding import PartitionSpec as P

LEAK = 0.3
F32 = jnp.float32
BF16 = jnp.bfloat16
MESH = pl.DeviceIdType.MESH
VMEM = pl.BlockSpec(memory_space=pltpu.VMEM)
GZ, GY = 32, 8
LIMIT = 56 * 2**20


def lanes_of(shape):
    return lax.broadcasted_iota(jnp.int32, shape, len(shape) - 1)


def before(x):
    lane = lanes_of(x.shape)
    return jnp.where(lane >= 64, pltpu.roll(x, 64, 1), jnp.where(lane == 0, 0.0, pltpu.roll(x, 65, 1)))


def after(x):
    lane = lanes_of(x.shape)
    return jnp.where(lane < 64, pltpu.roll(x, 64, 1), jnp.where(lane == 127, 0.0, pltpu.roll(x, 63, 1)))


def mm(a, b):
    return jnp.dot(a, b, preferred_element_type=F32)


def mm_nt(a, b):
    return lax.dot_general(a, b, (((1,), (1,)), ((), ())), preferred_element_type=F32)


def eye(n):
    return lax.broadcasted_iota(jnp.int32, (n, n), 0) == lax.broadcasted_iota(jnp.int32, (n, n), 1)


def one_hot(n):
    return jnp.where(eye(n), 1.0, 0.0).astype(BF16)


def column(row, times):
    n = row.shape[0]
    wide = jnp.broadcast_to(row[None, :], (n, n))
    once = jnp.sum(jnp.where(eye(n), wide, 0.0), axis=1, keepdims=True)
    return jnp.concatenate([once] * times, axis=0)


def place():
    return lax.axis_index("gz"), lax.axis_index("gy")


def spread_matrix():
    out = np.zeros((256, 4, 128), np.float32)
    for lane in range(128):
        cell = 2 * (lane % 64) + lane // 64
        for dw in range(4):
            w = 2 * cell + dw - 1
            if 0 <= w < 256:
                out[w, dw, lane] = 1
    return out.reshape(256, 512).astype(jnp.bfloat16)


def channel_matrix():
    out = np.zeros((64, 64), np.float32)
    for q in range(64):
        out[q, (q % 2) * 32 + q // 2] = 1
    return out.astype(jnp.bfloat16)


def turn_matrix():
    out = np.zeros((64, 64), np.float32)
    for r in range(16):
        for c in range(4):
            out[r * 4 + c, c * 16 + r] = 1
    return out.astype(jnp.bfloat16)


def gather_matrix():
    out = np.zeros((2, 2, 2, 4, 4, 4, 4, 128), np.float32)
    for pd in range(2):
        for pr in range(2):
            for pw in range(2):
                for r in range(3):
                    for s in range(3):
                        for t in range(3):
                            for c in range(4):
                                out[pd, pr, pw, pd + r, pw + t, pr + s, c, ((r * 3 + s) * 3 + t) * 4 + c] = 1
    out = out.reshape(2048, 128)
    mirrored = np.zeros_like(out)
    for r in range(3):
        mirrored[:, r * 36 : r * 36 + 36] = out[:, (2 - r) * 36 : (2 - r) * 36 + 36]
    return np.stack([out, mirrored]).astype(jnp.bfloat16)


def around(dz, dy):
    gz, gy = place()
    return lax.rem(gz + dz + GZ, GZ), lax.rem(gy + dy + GY, GY)


def hops(offset):
    x, y, z, core = offset
    return min(x, 4 - x) + min(y, 4 - y) + min(z, 8 - z) + 0.5 * core


def spread_order(kind):
    xs, ys, zs, cores = (range(n) for n in ((4, 4, 1, 1), (1, 1, 8, 2), (4, 4, 1, 2))[kind])
    all_ = [(x, y, z, c) for x in xs for y in ys for z in zs for c in cores]
    return sorted([o for o in all_ if any(o)], key=lambda o: -hops(o))


def shifted(offset):
    gz, gy = place()
    x, y, core = gz // 8, lax.rem(gz // 2, 4), lax.rem(gz, 2)
    dx, dy, dz, dc = offset
    x = lax.rem(x + dx, 4) if dx else x
    y = lax.rem(y + dy, 4) if dy else y
    core = 1 - core if dc else core
    return x * 8 + y * 2 + core, lax.rem(gy + dz, GY) if dz else gy


def rank(kind, gz, gy):
    return (gz // 2, gy * 2 + lax.rem(gz, 2), gz)[kind]


COUNT = (16, 16, 32)


def share(kind, source, landing, send, recv, after=0, then=None):
    gz, gy = place()
    slot = rank(kind, gz, gy)
    for number, offset in enumerate(spread_order(kind)):
        if then is not None and number == after:
            then()
        to = shifted(offset)
        pltpu.make_async_remote_copy(
            src_ref=source(rank(kind, *to)),
            dst_ref=landing.at[slot],
            send_sem=send,
            recv_sem=recv,
            device_id=to,
            device_id_type=MESH,
        ).start()

    def wait():
        pltpu.make_async_remote_copy(
            src_ref=landing.at[pl.ds(0, COUNT[kind] - 1)],
            dst_ref=landing.at[pl.ds(0, COUNT[kind] - 1)],
            send_sem=send,
            recv_sem=recv,
            device_id=around(1, 0),
            device_id_type=MESH,
        ).wait()

    return wait


def greet():
    gz, gy = place()
    barrier = pltpu.get_barrier_semaphore()

    def tell(to):
        pl.semaphore_signal(barrier, inc=1, device_id=to, device_id_type=MESH)

    far = lax.rem(gz + 2 * lax.rem(gz, 2) - 1 + GZ, GZ)
    tell((far, lax.rem(gy + 1, GY)))
    tell((far, lax.rem(gy + GY - 1, GY)))
    offsets = [o for o in spread_order(1) if o[2]] + spread_order(2)
    for offset in sorted(offsets, key=lambda o: -hops(o)):
        tell(shifted(offset))

    def wait():
        pl.semaphore_wait(barrier, 47)

    return wait


def total16(landing):
    value = landing[0].astype(F32)
    for k in range(1, 16):
        value = value + landing[k].astype(F32)
    return value


def body(
    vol_in, w1_in, b1_in, w2_in, b2_in, up_in, spread_in, chan_in, turn_in, gather_in,
    pool_out, first_out, second_out,
    vol_ref, w1_ref, b1_ref, w2_ref, b2_ref, up_ref, spread_ref, chan_ref, turn_ref, gather_ref, load, seen,
    own, ext, up_stage, up_got, pool_stage, pool_got,
    w1_rows, w1, w2, w2_turned, rows, patch, pre, act, full, gact, ffull,
    sg, sg_one, sg_part, sg_two, sg_done, term, t_one, t_part, t_two,
    send, recv, a_send, a_recv, s_send, s_recv,
):
    gz, gy = place()
    core = lax.rem(gz, 2)
    near, far = gz + 1 - 2 * core, lax.rem(gz + 2 * core - 1 + GZ, GZ)
    edge = (gz == 0) | (gz == GZ - 1)

    def depth(d, count):
        return jnp.where(core == 0, count - 1 - d, d)

    loads = []
    for source, target in (
        (vol_in, vol_ref), (turn_in, turn_ref), (up_in, up_ref), (w1_in, w1_ref), (gather_in.at[1 - core], gather_ref),
        (b1_in, b1_ref), (b2_in, b2_ref), (w2_in, w2_ref), (spread_in, spread_ref), (chan_in, chan_ref),
    ):
        loads.append(pltpu.make_async_copy(source, target, load.at[len(loads)]))
    greeted = greet()
    for one in loads:
        one.start()
    for one in loads[:3]:
        one.wait()

    for d in range(4):
        flat = jnp.concatenate([vol_ref[c, depth(d, 4)] for c in range(4)], axis=0)
        own[d] = mm(turn_ref[...], flat).astype(BF16)
    for half in range(2):
        for chan in range(2):
            up_stage[:, chan * 2 + half, :] = up_ref[chan, :, half * 128 : half * 128 + 128].astype(F32)
    for one in loads[3:7]:
        one.wait()
    w1_rows[...] = jnp.zeros((128, 32), F32)
    for i in range(27):
        w1_rows[4 * i : 4 * i + 4, :] = w1_ref[i // 9, i // 3 % 3, i % 3].astype(F32)
    flat = mm_nt(one_hot(32), w1_rows[...].astype(BF16)).astype(BF16)
    for g in range(8):
        w1[g * 32 : g * 32 + 32, :] = mm_nt(flat, gather_ref[g * 256 : g * 256 + 256, :]).astype(BF16)
    b1 = column(b1_ref[...], 8)
    b2 = column(b2_ref[...], 4)
    greeted()

    copies = []

    def send_halo():
        sides = (
            (far, slice(1, 4), slice(7, 10), (1, -1, 0)),
            (near, slice(0, 3), slice(0, 3), (1, -1, 0)),
            (gz, slice(0, 4), slice(3, 7), (1, -1)),
        )
        for to, src_d, dst_d, steps in sides:
            for dy in steps:
                src_r, dst_r = {
                    -1: (slice(0, 16), slice(80, 96)),
                    0: (slice(0, 64), slice(16, 80)),
                    1: (slice(48, 64), slice(0, 16)),
                }[dy]
                copy = pltpu.make_async_remote_copy(
                    src_ref=own.at[src_d, src_r],
                    dst_ref=ext.at[dst_d, dst_r],
                    send_sem=send.at[len(copies)],
                    recv_sem=recv.at[len(copies)],
                    device_id=(to, lax.rem(gy + dy + GY, GY)),
                    device_id_type=MESH,
                )
                copy.start()
                copies.append(copy)

    up_wait = share(2, lambda j: up_stage.at[j], up_got, a_send.at[0], a_recv.at[0], 10, send_halo)
    for one in loads[7:]:
        one.wait()

    lane = lanes_of((32, 128))
    zero = jnp.zeros((32, 128), F32)
    for t in range(3):
        for r in range(4):
            for s in range(4):
                at = ((r * 3 + t) * 4 + s) * 32
                for pd in range(2):
                    here = w2_ref[depth(r - pd, 3), s, t].astype(F32) if 0 <= r - pd < 3 and s < 3 else None
                    next_ = w2_ref[depth(r - pd, 3), s - 1, t].astype(F32) if 0 <= r - pd < 3 and s > 0 else None
                    left = zero[:, :64] if here is None else here
                    right = zero[:, :64] if next_ is None else next_
                    w2[at : at + 32, pd * 128 : pd * 128 + 128] = jnp.concatenate([left, right], axis=1).astype(BF16)
    w2_turned[...] = mm_nt(one_hot(256), w2[...]).astype(BF16)

    def widen(value, targets, at):
        many, high, _ = value.shape
        flat = value.reshape(many * high, 256)
        for side in range(2):
            wide = mm(flat, spread_ref[:, side * 256 : side * 256 + 256])
            for k in range(2):
                for i, d in enumerate(targets):
                    rows[d, 2 * side + k, at : at + high] = wide[i * high : i * high + high, k * 128 : k * 128 + 128]

    def clear(deps, at):
        ext[deps, at : at + 16] = jnp.zeros((deps.stop - deps.start, 16, 256), BF16)

    def inside(d, r):
        ok = None
        if d == 3:
            ok = jnp.logical_not(edge)
        if r in (0, 9):
            side = gy > 0 if r == 0 else gy < GY - 1
            ok = side if ok is None else ok & side
        return ok

    def keep(ok, value):
        return value if ok is None else jnp.where(ok, value, 0.0)

    def layer_one(d):
        for dd in range(4):
            for dw in range(4):
                for r in range(10):
                    patch[d, dd * 64 + dw * 16 : dd * 64 + dw * 16 + 16, r * 128 : r * 128 + 128] = rows[
                        2 * d + dd, dw, 8 * r + 4 : 8 * r + 20, :
                    ].astype(BF16)
        for j in range(5):
            value = mm(w1[...], patch[d, :, j * 256 : j * 256 + 256]) + b1
            pre[d, :, j * 256 : j * 256 + 256] = value.astype(BF16)
            out = jnp.maximum(value, LEAK * value)
            cell = out[0:32]
            for g in range(1, 8):
                cell = cell + out[g * 32 : g * 32 + 32]
            cell = (cell * 0.125).astype(BF16).astype(F32)
            for k in range(2):
                r = 2 * j + k
                one = keep(inside(d, r), cell[:, k * 128 : k * 128 + 128])
                act[d, 0, r * 32 : r * 32 + 32, :] = before(one).astype(BF16)
                act[d, 1, r * 32 : r * 32 + 32, :] = one.astype(BF16)
                act[d, 2, r * 32 : r * 32 + 32, :] = after(one).astype(BF16)

    def windows(h, deps):
        sides = []
        for k in range(2):
            r = 4 * h + 2 * k
            sides.append(jnp.concatenate([act[dd, dw, r * 32 : r * 32 + 128, :] for dd in deps for dw in range(3)], axis=0))
        return jnp.concatenate(sides, axis=1)

    widen(own[...], (3, 4, 5, 6), 16)
    for copy in copies[3:]:
        copy.wait()

    @pl.when(gy == 0)
    def _():
        clear(slice(0, 7), 0)

    @pl.when(gy == GY - 1)
    def _():
        clear(slice(0, 7), 80)

    widen(ext[0:3], (2, 1, 0), 0)
    for at in (0, 80):
        widen(ext[3:7, at : at + 16], (3, 4, 5, 6), at)
    for d in range(2):
        layer_one(d)
    for h in range(2):
        seen[h] = mm(w2_turned[:, :768], windows(h, (0, 1))) + b2

    for copy in copies[:3]:
        copy.wait()

    @pl.when(gy == 0)
    def _():
        clear(slice(7, 10), 0)

    @pl.when(gy == GY - 1)
    def _():
        clear(slice(7, 10), 80)

    @pl.when(edge)
    def _():
        ext[7:10] = jnp.zeros((3, 96, 256), BF16)

    widen(ext[7:10], (9, 8, 7), 0)
    for d in range(2, 4):
        layer_one(d)

    up_wait()
    up_got[gz] = up_stage[gz]
    wide = []
    for half in range(2):
        wide.append(jnp.concatenate([up_got[:, chan * 2 + half, :] for chan in range(2)], axis=0))
    back = mm(chan_ref[...], jnp.concatenate(wide, axis=1).astype(BF16))
    lane = lanes_of((64, 128))
    grads = []
    for h in range(2):
        value = seen[h] + mm(w2_turned[:, 768:], windows(h, (2, 3)))
        seen[h] = value
        up = back[:, h * 128 : h * 128 + 128] * 0.125
        other = pltpu.roll(up, 64, 1)
        both = jnp.concatenate([jnp.where(lane < 64, up, other), jnp.where(lane < 64, other, up)], axis=1)
        weak = both * LEAK
        grad = jnp.concatenate(
            [jnp.where(value[g * 64 : g * 64 + 64] > 0, both, weak).astype(BF16) for g in range(4)], axis=0
        )
        grads.append(grad)
        full[h] = mm_nt(windows(h, range(4)), grad)

    lane = lanes_of((16, 128))
    for r in range(3):
        for t in range(3):
            near = []
            for s in range(4):
                a = ((r * 3 + t) * 4 + s) * 32
                b = (((r + 1) * 3 + t) * 4 + s) * 32
                near.append(
                    full[0, a : a + 32, 0:128]
                    + full[1, a : a + 32, 0:128]
                    + (full[0, b : b + 32, 128:256] + full[1, b : b + 32, 128:256])
                )
            for s in range(3):
                low = near[s][:16] + pltpu.roll(near[s + 1][:16], 64, 1)
                high = pltpu.roll(near[s][16:], 64, 1) + near[s + 1][16:]
                at = (depth(r, 3) * 3 + s) * 3 + t
                sg[pl.ds(pl.multiple_of(at * 16, 16), 16), :] = jnp.where(lane < 64, low, high).astype(SENT)
    sg[432:512] = jnp.zeros((80, 128), SENT)
    chip, line = rank(0, gz, gy), rank(1, gz, gy)
    one_wait = share(0, lambda j: sg.at[pl.ds(pl.multiple_of(j * 32, 32), 32)], sg_one, s_send.at[0], s_recv.at[0])
    sg_one[chip] = sg[pl.ds(pl.multiple_of(chip * 32, 32), 32), :]

    lane = lanes_of((64, 128))
    pooled = []
    for h in range(2):
        value = seen[h]
        out = jnp.maximum(value, LEAK * value)
        cell = out[0:64] + out[64:128] + out[128:192] + out[192:256]
        left, right = cell[:, :128], cell[:, 128:]
        left = left + pltpu.roll(left, 64, 1)
        right = right + pltpu.roll(right, 64, 1)
        pooled.append((jnp.where(lane < 64, left, right) * 0.125).astype(BF16))
    turned = lax.dot_general(
        chan_ref[...], jnp.concatenate(pooled, axis=1), (((0,), (0,)), ((), ())), preferred_element_type=F32
    )
    for half in range(2):
        for chan in range(2):
            pool_stage[:, chan * 2 + half, :] = turned[chan * 32 : chan * 32 + 32, half * 128 : half * 128 + 128]

    for h in range(2):
        pulled = mm(w2[...], grads[h])
        for dd in range(4):
            for t in range(3):
                at = (dd * 3 + t) * 128
                for k in range(2):
                    gact[dd, t, 2 * h + k] = pulled[at : at + 128, k * 128 : k * 128 + 128]

    def layer_back(d):
        for j in range(5):
            sides = []
            for k in range(2):
                parts = []
                for t in range(3):
                    value = None
                    for r, at in ((j, k * 32), (j - 1, 64 + k * 32)):
                        if 0 <= r < 4:
                            piece = gact[d, t, r, at : at + 32, :]
                            value = piece if value is None else value + piece
                    parts.append(value)
                value = (after(parts[0]) + parts[1] + before(parts[2])) * 0.125
                sides.append(keep(inside(d, 2 * j + k), value))
            strong = jnp.concatenate(sides, axis=1)
            weak = strong * LEAK
            seen = pre[d, :, j * 256 : j * 256 + 256].astype(F32)
            grad = jnp.concatenate(
                [jnp.where(seen[g * 32 : g * 32 + 32] > 0, strong, weak).astype(BF16) for g in range(8)], axis=0
            )
            ffull[...] += mm_nt(grad, patch[d, :, j * 256 : j * 256 + 256])

    ffull[...] = jnp.zeros((256, 256), F32)
    for d in range(4):
        layer_back(d)
    flat = jnp.concatenate([ffull[g * 32 : g * 32 + 32, :] for g in range(8)], axis=1)
    pieces = []
    for _ in range(3):
        pieces.append(flat.astype(BF16))
        flat = flat - pieces[-1].astype(F32)
    total = mm(jnp.concatenate(pieces, axis=0), gather_ref[...])
    total = total[0:32] + total[32:64] + total[64:96]
    term[...] = total.astype(SENT)

    t_wait = share(0, lambda j: term, t_one, s_send.at[3], s_recv.at[3])
    t_one[chip] = term[...]
    one_wait()
    sg_part[...] = total16(sg_one).astype(SENT)
    two_wait = share(1, lambda j: sg_part, sg_two, s_send.at[1], s_recv.at[1])
    pool_wait = share(2, lambda j: pool_stage.at[j], pool_got, a_send.at[1], a_recv.at[1])
    pool_got[gz] = pool_stage[gz]
    sg_two[line] = sg_part[...]
    t_wait()
    t_part[...] = total16(t_one).astype(SENT)
    t_wait = share(1, lambda j: t_part, t_two, s_send.at[4], s_recv.at[4])
    t_two[line] = t_part[...]
    two_wait()
    second_out[chip] = total16(sg_two).astype(SENT)
    done_wait = share(0, lambda j: second_out.at[chip], second_out, s_send.at[2], s_recv.at[2])
    pool_wait()
    for half in range(2):
        for chan in range(2):
            pool_out[chan, :, half * 128 : half * 128 + 128] = pool_got[:, chan * 2 + half, :].astype(BF16)
    t_wait()
    first_out[...] = jnp.transpose(total16(t_two))
    done_wait()


def finish(pool_in, first_in, second_in, pool_out, first_out, second_out):
    pool_out[...] = pool_in[...]
    for i in range(27):
        first_out[i // 9, i // 3 % 3, i % 3] = first_in[4 * i : 4 * i + 4, :]
        block = second_in[i // 2, (i % 2) * 16 : (i % 2) * 16 + 16, :].astype(F32)
        second_out[i // 9, i // 3 % 3, i % 3, 0:16, :] = block[:, :64]
        second_out[i // 9, i // 3 % 3, i % 3, 16:32, :] = block[:, 64:]


SENT = BF16


def on_device(volume, first_weight, first_bias, second_weight, second_bias, upstream):
    dma, mem = pltpu.SemaphoreType.DMA, pltpu.VMEM
    constants = [jnp.asarray(m()) for m in (spread_matrix, channel_matrix, turn_matrix, gather_matrix)]
    operands = [volume, first_weight, first_bias, second_weight, second_bias, upstream, *constants]
    results = pl.pallas_call(
        body,
        out_shape=[mem((2, 32, 256), BF16), mem((128, 32), F32), mem((16, 32, 128), SENT)],
        in_specs=[pl.BlockSpec(memory_space=pl.ANY)] * len(operands),
        out_specs=[VMEM] * 3,
        scratch_shapes=[
            *[mem(x.shape, x.dtype) for x in operands[:-1]], mem((2048, 128), BF16), dma((10,)), mem((2, 256, 256), F32),
            mem((4, 64, 256), BF16), mem((10, 96, 256), BF16), mem((32, 4, 128), F32), mem((32, 4, 128), F32),
            mem((32, 4, 128), F32), mem((32, 4, 128), F32),
            mem((128, 32), F32), mem((256, 256), BF16), mem((1536, 256), BF16), mem((256, 1536), BF16),
            mem((10, 4, 96, 128), F32), mem((4, 256, 1280), BF16), mem((4, 256, 1280), BF16), mem((4, 3, 320, 128), BF16),
            mem((2, 1536, 256), F32), mem((4, 3, 4, 128, 128), F32), mem((256, 256), F32),
            mem((512, 128), SENT), mem((16, 32, 128), SENT), mem((32, 128), SENT), mem((16, 32, 128), SENT),
            mem((16, 32, 128), SENT), mem((32, 128), SENT), mem((16, 32, 128), SENT), mem((32, 128), SENT),
            mem((16, 32, 128), SENT),
            dma((8,)), dma((8,)), dma((2,)), dma((2,)), dma((5,)), dma((5,)),
        ],
        compiler_params=pltpu.CompilerParams(vmem_limit_bytes=LIMIT, has_side_effects=True, collective_id=1),
    )(*operands)
    return pl.pallas_call(
        finish,
        out_shape=[
            jax.ShapeDtypeStruct((2, 32, 256), BF16),
            jax.ShapeDtypeStruct((3, 3, 3, 4, 32), F32),
            jax.ShapeDtypeStruct((3, 3, 3, 32, 64), F32),
        ],
        in_specs=[VMEM] * 3,
        out_specs=[VMEM] * 3,
    )(*[pltpu.with_memory_space_constraint(x, pltpu.VMEM) for x in results])


def solution(mesh):
    placed = (P(None, "gz", "gy", None), P(), P(), P(), P(), P("gz", None, "gy"))
    return jax.shard_map(
        on_device,
        mesh=mesh,
        in_specs=placed,
        out_specs=(P("gz", None, "gy"), P(), P()),
        check_vma=False,
    )
```
